128 devices in a mesh: seq: 32 (over y, x, core), row: 4 (over z).
Axes of the slice: x: 4, y: 4, z: 4, core: 2. Of those that a mesh axis runs over, the one named last changes fastest.
Arguments:
- events: bfloat16 [8, 4096, 512], P('row', 'seq'), may hold values from -6 to 6
- grad_out: bfloat16 [8, 4096, 512], P('row', 'seq'), may hold values from -6 to 6
- w_inner: bfloat16 [512, 2048], replicated, may hold values from -0.25 to 0.25
- w_outer: bfloat16 [512, 512], replicated, may hold values from -0.25 to 0.25
- valid_lengths: int32 [8], P('row'), may hold values from 1024 to 4096, as said below
- item_ids: int32 [8, 4096], P('row', 'seq'), may hold values from 0 to 131071, as said below
Outputs:
- table_grad: float32 [131072, 512], P(('seq', 'row'))
The draws below stay inside these ranges and needn't reach their ends.
Inputs may be any that keep to these rules, and one draw needn't show every extreme that they name: `valid_lengths`: each sequence's valid events are its first ones; some sequence is full. `item_ids`: table row r lies in block r // 1024; block o belongs to device o of seq and row taken together, seq slowest. Of the events of one device, at most 4 have items in one block, and on every device some block gets exactly 4.
All inputs are finite; a program needn't handle non-finite values.
Results may differ from the reference program's by a relative error of at most 0.0047.
Values may be sent and summed in bfloat16 or wider, within the bound.
No kernel may reach another device: no remote copies, remote signals or barrier semaphores. Data moves between devices by JAX's collectives and lax.ppermute only.
A program may use at most 192 MiB of HBM per device.

```python
import jax
import jax.numpy as jnp
from jax import lax

D = 512
HEADS = 4
LEN = 4096
SEQ_GRP = 2
ROWS_DEV = 1024
SEQS = 8
ITEMS = 131072
CAP = 4
N_SEQ = 32
N_ROW = 4


def draw_valid_lengths(key, part):
    key = jax.random.fold_in(key, 5)
    key_len, key_full = jax.random.split(key)
    drawn = jax.random.randint(key_len, (SEQS,), LEN // 4, LEN + 1, dtype=jnp.int32)
    full_seq = jax.random.randint(key_full, (), 0, SEQS, dtype=jnp.int32)
    return jnp.where(jnp.arange(SEQS, dtype=jnp.int32) == full_seq, LEN, drawn).astype(jnp.int32)


def draw_item_ids(key, part):
    key = jax.random.fold_in(key, 11)
    owner_count = N_SEQ * N_ROW
    local_len = LEN // N_SEQ
    block_len = SEQ_GRP * local_len

    def one_block(block_key):
        key_heavy, key_pick, key_order, key_row = jax.random.split(block_key, 4)
        heavy_owner = jax.random.randint(key_heavy, (), 0, owner_count, dtype=jnp.int32)
        picks = jax.random.permutation(key_pick, (owner_count - 1) * CAP)[:block_len - CAP] // CAP
        others = (picks + (picks >= heavy_owner)).astype(jnp.int32)
        owners = jnp.concatenate([jnp.full((CAP,), heavy_owner, jnp.int32), others])
        owners = jax.random.permutation(key_order, owners)
        row_within = jax.random.randint(key_row, (block_len,), 0, ROWS_DEV, dtype=jnp.int32)
        return owners * ROWS_DEV + row_within
    blocks = jax.vmap(one_block)(jax.random.split(key, owner_count))
    blocks = blocks.reshape(N_ROW, N_SEQ, SEQ_GRP, local_len).transpose(0, 2, 1, 3)
    return blocks.reshape(SEQS, LEN).astype(jnp.int32)


def level_of(rng, shape, cuts, low, largest):
    def one(position, parts):
        steps = jax.random.uniform(jax.random.fold_in(jax.random.fold_in(rng, 6), position), (parts,), jnp.float32, low / len(cuts), largest / len(cuts))
        return jnp.repeat(jnp.exp(steps), shape[position] // parts).reshape((-1,) + (1,) * (len(shape) - position - 1))

    level = one(*cuts[0])
    for cut in cuts[1:]:
        level = level * one(*cut)
    return level


def gaussian(own_key, extent, width, limit, cuts=(), held_as=jnp.bfloat16):
    entries = jax.random.normal(own_key, extent, jnp.float32) * width
    if len(cuts) > 0:
        entries = level_of(own_key, extent, cuts, -0.22, 0.18) * entries
    return jnp.clip(entries, min=-limit, max=limit).astype(held_as)


def setup_inputs(seed: int = 0) -> dict:
    key_of = jax.random.split(jax.random.key(seed), 7)
    return {
        "events": gaussian(key_of[0], (SEQS, LEN, D), 1.0, 6.0, ((0, 4), (1, 32))),
        "grad_out": gaussian(key_of[1], (SEQS, LEN, D), 1.0, 6.0, ((0, 4), (1, 32))),
        "w_inner": gaussian(key_of[2], (D, 4 * D), D ** -0.5, 0.25),
        "w_outer": gaussian(key_of[3], (D, D), D ** -0.5, 0.25),
        "valid_lengths": draw_valid_lengths(jax.random.fold_in(key_of[6], 71), 0),
        "item_ids": draw_item_ids(jax.random.fold_in(key_of[6], 71), 0),
    }


def normalize(values):
    center = values - lax.optimization_barrier(jnp.mean(values, axis=-1, keepdims=True))
    inverse = lax.rsqrt(lax.optimization_barrier(jnp.mean(center * center, axis=-1, keepdims=True)) + 1e-05)
    return (center * inverse, inverse)

def norm_back(upstream, normed, inverse):
    return inverse * (upstream - lax.optimization_barrier(jnp.mean(upstream, axis=-1, keepdims=True)) - normed * lax.optimization_barrier(jnp.mean(upstream * normed, axis=-1, keepdims=True)))

def silu_slope(values):
    sigma = jax.nn.sigmoid(values)
    return sigma * (1.0 + values * (1.0 - sigma))

def reference(events, grad_out, w_inner, w_outer, valid_lengths, item_ids):
    head_dim = D // HEADS
    score_scale = head_dim ** (-0.5)

    def one_sequence(inputs):
        seq_events, seq_grad, length = inputs
        normed, norm_inv = normalize(seq_events.astype(jnp.float32))
        pre_act = jnp.dot(normed.astype(jnp.bfloat16), w_inner, preferred_element_type=jnp.float32)
        activated = jax.nn.silu(pre_act).astype(jnp.bfloat16)
        u_part = activated[:, :D]
        v_part = activated[:, D:2 * D]
        q_part = activated[:, 2 * D:3 * D]
        k_part = activated[:, 3 * D:]
        positions = jnp.arange(LEN, dtype=jnp.int32)
        causal_mask = (positions[None, :] <= positions[:, None]) & (positions[:, None] < length)
        pair_weight = jnp.where(causal_mask, 1.0 / length.astype(jnp.float32), 0.0)
        outputs = []
        for head_index in range(HEADS):
            head_cols = slice(head_index * head_dim, (head_index + 1) * head_dim)
            score_block = score_scale * jnp.dot(q_part[:, head_cols], k_part[:, head_cols].T, preferred_element_type=jnp.float32)
            attn_weights = (jax.nn.silu(score_block) * pair_weight).astype(jnp.bfloat16)
            outputs.append(jnp.dot(attn_weights, v_part[:, head_cols], preferred_element_type=jnp.float32))
        normed_out, out_inv = normalize(jnp.concatenate(outputs, axis=-1))
        grad_gated = jnp.dot(seq_grad, w_outer.T, preferred_element_type=jnp.float32)
        grad_upart = grad_gated * normed_out
        grad_attn = norm_back(grad_gated * u_part.astype(jnp.float32), normed_out, out_inv).astype(jnp.bfloat16)
        grad_query, grad_key, grad_value = ([], [], [])
        for head_index in range(HEADS):
            head_cols = slice(head_index * head_dim, (head_index + 1) * head_dim)
            score_block = score_scale * jnp.dot(q_part[:, head_cols], k_part[:, head_cols].T, preferred_element_type=jnp.float32)
            attn_weights = (jax.nn.silu(score_block) * pair_weight).astype(jnp.bfloat16)
            grad_weights = jnp.dot(grad_attn[:, head_cols], v_part[:, head_cols].T, preferred_element_type=jnp.float32)
            grad_score = (grad_weights * pair_weight * silu_slope(score_block)).astype(jnp.bfloat16)
            grad_query.append(score_scale * jnp.dot(grad_score, k_part[:, head_cols], preferred_element_type=jnp.float32))
            grad_key.append(score_scale * jnp.dot(grad_score.T, q_part[:, head_cols], preferred_element_type=jnp.float32))
            grad_value.append(jnp.dot(attn_weights.T, grad_attn[:, head_cols], preferred_element_type=jnp.float32))
        grad_joined = jnp.concatenate([grad_upart] + grad_value + grad_query + grad_key, axis=-1)
        grad_pre = (grad_joined * silu_slope(pre_act)).astype(jnp.bfloat16)
        grad_normed = jnp.dot(grad_pre, w_inner.T, preferred_element_type=jnp.float32)
        grad_events = seq_grad.astype(jnp.float32) + norm_back(grad_normed, normed, norm_inv)
        return jnp.where((positions < length)[:, None], grad_events, 0.0)
    grad_rows = lax.map(one_sequence, (events, grad_out, valid_lengths))
    table_grad = jnp.zeros((ITEMS, D), jnp.float32)
    return table_grad.at[item_ids.reshape(-1)].add(grad_rows.reshape(-1, D))
```

```python
import functools

import jax
import jax.numpy as jnp
from jax import lax
from jax.experimental import pallas as pl
from jax.experimental.pallas import tpu as pltpu
from jax.sharding import Mesh
from jax.sharding import PartitionSpec as P

HEADS = 4
ROWS_DEV = 1024
D = 512
HD = 128
BLK = 128
CAP = 4
EXT = 128
F32 = jnp.float32
BF16 = jnp.bfloat16
SCALE = HD**-0.5


def dot(a, b):
    return lax.dot_general(a, b, (((1,), (0,)), ((), ())), preferred_element_type=F32)


def dot_t(a, b):
    return lax.dot_general(a, b, (((1,), (1,)), ((), ())), preferred_element_type=F32)


def normalize(values):
    center = values - jnp.mean(values, axis=-1, keepdims=True)
    inverse = lax.rsqrt(jnp.mean(center * center, axis=-1, keepdims=True) + 1e-05)
    return center * inverse, inverse


def silu(values):
    half = 0.5 * values
    return half * jnp.tanh(half) + half


def silu_slope(values):
    half = 0.5 * values
    two_sigma = 1.0 + jnp.tanh(half)
    return 0.5 * two_sigma * (1.0 + values - half * two_sigma)


def project_kernel(events, w_inner, pre, send):
    normed = normalize(events[...].astype(F32))[0].astype(BF16)
    for part, slot in ((0, 2), (1, 0), (2, 1)):
        values = dot(normed, w_inner[:, (part + 1) * D : (part + 2) * D])
        pre[:, part * D : (part + 1) * D] = values
        act = silu(values).astype(BF16)
        for g in range(2):
            for h in range(HEADS):
                piece = act[g * BLK : (g + 1) * BLK, h * HD : (h + 1) * HD]
                for p in range(2):
                    at = ((g * HEADS + h) * 2 + p) * BLK
                    send[at : at + BLK, slot * HD : (slot + 1) * HD] = piece


def gate_kernel(events, grad_out, w_u, w_outer, ids, pre_u, gated, send_g, hot, ext):
    normed = normalize(events[...].astype(F32))[0].astype(BF16)
    values = dot(normed, w_u[...])
    pre_u[...] = values
    grad_gated = dot_t(grad_out[...], w_outer[...])
    gated[...] = grad_gated
    prod = (grad_gated * silu(values).astype(BF16).astype(F32)).astype(BF16)
    for g in range(2):
        for h in range(HEADS):
            at = (g * HEADS + h) * BLK
            send_g[at : at + BLK, :] = prod[g * BLK : (g + 1) * BLK, h * HD : (h + 1) * HD]
    count = 2 * BLK
    id_row = ids[...]
    id_cols = jnp.transpose(jnp.broadcast_to(id_row.astype(F32), (BLK, count))).astype(jnp.int32)
    owner_row = id_row // ROWS_DEV
    owner_col = id_cols[:, :1] // ROWS_DEV
    earlier = lax.broadcasted_iota(jnp.int32, (count, count), 0) < lax.broadcasted_iota(
        jnp.int32, (count, count), 1
    )
    same = jnp.where((owner_col == owner_row) & earlier, 1, 0)
    rank = jnp.sum(same, axis=0, keepdims=True)
    slot = owner_row * CAP + rank
    slots = hot.shape[0]
    hot[...] = jnp.where(
        lax.broadcasted_iota(jnp.int32, (slots, count), 0) == slot, 1.0, 0.0
    ).astype(BF16)
    within = id_cols - (id_cols // ROWS_DEV) * ROWS_DEV
    high = within // 32
    lane = lax.broadcasted_iota(jnp.int32, (count, EXT), 1)
    ext[...] = jnp.where(
        lane == 0, high + 1, jnp.where(lane == 1, within - high * 32, 0)
    ).astype(F32).astype(BF16)


def diagonal(place, core, rows_are_keys):
    row = lax.broadcasted_iota(jnp.int32, (BLK, 2 * BLK), 0) + place[2] * BLK
    lane = lax.broadcasted_iota(jnp.int32, (BLK, 2 * BLK), 1)
    col = lane + jnp.where(lane >= BLK, BLK, 0) + core * BLK
    return row <= col if rows_are_keys else col <= row


def forward_kernel(last, place, inv_len, mine, theirs, *refs):
    if last:
        before, grad, out, stats, queries = refs
    else:
        out, queries = refs
    p = place[0]
    core = place[1]
    if last:
        core = 1 - core
    for m in range(8):
        at = pl.multiple_of((2 * m + p) * BLK, BLK)
        queries[m * BLK : (m + 1) * BLK, :] = mine[pl.ds(at, BLK), :HD]
    mask = diagonal(place, core, False)
    for m in range(8):
        rows = slice(m * BLK, (m + 1) * BLK)
        q = queries[rows, :]
        total = before[rows, :] if last else jnp.zeros((BLK, HD), F32)
        for j in range(m + 1):
            keys = slice(j * 2 * BLK, (j + 1) * 2 * BLK)
            half = dot_t(q, theirs[keys, HD : 2 * HD]) * (0.5 * SCALE)
            attn = half * jnp.tanh(half) + half
            if j == m:
                attn = jnp.where(mask, attn, 0.0)
            total = total + dot(attn.astype(BF16), theirs[keys, 2 * HD :])
        if last:
            total = total * inv_len[0]
            g = grad[rows, :].astype(F32)
            mean = jnp.mean(total, axis=-1, keepdims=True)
            center = total - mean
            square = jnp.sum(center * center, axis=-1, keepdims=True)
            sum_g = jnp.sum(g, axis=-1, keepdims=True)
            sum_ga = jnp.sum(g * center, axis=-1, keepdims=True)
            lane = lax.broadcasted_iota(jnp.int32, (BLK, BLK), 1)
            packed = jnp.where(
                lane == 0, mean, jnp.where(lane == 1, square, jnp.where(lane == 2, sum_g, sum_ga))
            )
            stats[:, rows] = jnp.transpose(packed)[:8, :]
        out[rows, :] = total


def grad_attn_kernel(place, length, attn_out, grad, s0, s1, s2, s3, grad_attn, normed_out):
    parts = [s0[...], s1[...], s2[...], s3[...]]
    means = [part[0:1, :] for part in parts]
    mean = 0.25 * (means[0] + means[1] + means[2] + means[3])
    square = 0.0
    sum_g = 0.0
    sum_ga = 0.0
    for part, own in zip(parts, means):
        shift = own - mean
        square = square + part[1:2, :] + HD * (shift * shift)
        sum_g = sum_g + part[2:3, :]
        sum_ga = sum_ga + part[3:4, :] + part[2:3, :] * shift
    inverse = lax.rsqrt(square * (1.0 / D) + 1e-05)
    mean_g = sum_g * (1.0 / D)
    mean_gn = inverse * sum_ga * (1.0 / D)
    row = lax.broadcasted_iota(jnp.int32, (BLK, 1024), 0)
    packed = jnp.where(
        row == 0, mean, jnp.where(row == 1, inverse, jnp.where(row == 2, mean_g, mean_gn))
    )
    for m in range(8):
        rows = slice(m * BLK, (m + 1) * BLK)
        cols = jnp.transpose(packed[:, rows])
        inv = cols[:, 1:2]
        n = (attn_out[rows, :] - cols[:, 0:1]) * inv
        back = (grad[rows, :].astype(F32) - cols[:, 2:3] - n * cols[:, 3:4]) * inv
        pos = lax.broadcasted_iota(jnp.int32, (BLK, 1), 0) + (m * 4 + place[2]) * BLK
        grad_attn[rows, :] = jnp.where(pos < length[0], back, 0.0).astype(BF16)
        normed_out[rows, :] = n.astype(BF16)


def slopes(raw):
    half = raw * (0.5 * SCALE)
    two_sigma = 1.0 + jnp.tanh(half)
    attn = half * two_sigma
    return two_sigma * (1.0 + (half + half) - attn), attn


def grad_query_kernel(place, inv_len, mine, theirs, grad_attn, normed_out, ret):
    p = place[0]
    masks = [diagonal(place, place[1], False), diagonal(place, 1 - place[1], False)]
    for m in range(8):
        rows = slice(m * BLK, (m + 1) * BLK)
        at = pl.multiple_of((2 * m + p) * BLK, BLK)
        q = mine[pl.ds(at, BLK), :HD]
        ga = grad_attn[rows, :]
        total = jnp.zeros((BLK, HD), F32)
        for j in range(m + 1):
            keys = slice(j * 2 * BLK, (j + 1) * 2 * BLK)
            for src, mask in zip((mine, theirs), masks):
                k = src[keys, HD : 2 * HD]
                slope, _ = slopes(dot_t(q, k))
                score = slope * dot_t(ga, src[keys, 2 * HD :])
                if j == m:
                    score = jnp.where(mask, score, 0.0)
                total = total + dot(score.astype(BF16), k)
        ret[rows, :HD] = normed_out[rows, :]
        ret[rows, HD:] = (total * (0.5 * SCALE * inv_len[0])).astype(BF16)


def grad_key_kernel(place, inv_len, mine, theirs, g_own, g_p, g_c, g_pc, ret, mine_g, theirs_g):
    p = place[0]
    masks = [diagonal(place, place[1], True), diagonal(place, 1 - place[1], True)]
    for m in range(8):
        rows = slice(m * BLK, (m + 1) * BLK)
        here = pl.multiple_of((2 * m + p) * BLK, BLK)
        there = pl.multiple_of((2 * m + 1 - p) * BLK, BLK)
        mine_g[pl.ds(here, BLK), :] = g_own[rows, :]
        mine_g[pl.ds(there, BLK), :] = g_p[rows, :]
        theirs_g[pl.ds(here, BLK), :] = g_c[rows, :]
        theirs_g[pl.ds(there, BLK), :] = g_pc[rows, :]
    for m in range(8):
        rows = slice(m * BLK, (m + 1) * BLK)
        at = pl.multiple_of((2 * m + p) * BLK, BLK)
        k = mine[pl.ds(at, BLK), HD : 2 * HD]
        v = mine[pl.ds(at, BLK), 2 * HD :]
        grad_k = jnp.zeros((BLK, HD), F32)
        grad_v = jnp.zeros((BLK, HD), F32)
        for j in range(m, 8):
            events = slice(j * 2 * BLK, (j + 1) * 2 * BLK)
            for src, src_g, mask in zip((mine, theirs), (mine_g, theirs_g), masks):
                q = src[events, :HD]
                ga = src_g[events, :]
                slope, attn = slopes(dot_t(k, q))
                score = slope * dot_t(v, ga)
                if j == m:
                    score = jnp.where(mask, score, 0.0)
                    attn = jnp.where(mask, attn, 0.0)
                grad_k = grad_k + dot(score.astype(BF16), q)
                grad_v = grad_v + dot(attn.astype(BF16), ga)
        ret[rows, :HD] = (grad_k * (0.5 * SCALE * inv_len[0])).astype(BF16)
        ret[rows, HD:] = (grad_v * inv_len[0]).astype(BF16)


def finish_kernel(
    first, lengths, ret1, ret2, pre_u, pre, gated, events, grad_out, w_inner, hot, ext, send, grads
):
    for g in range(2):
        rows = slice(g * BLK, (g + 1) * BLK)
        for h in range(HEADS):
            cols = slice(h * HD, (h + 1) * HD)
            at = slice((g * HEADS + h) * BLK, (g * HEADS + h + 1) * BLK)
            pieces = (
                (gated[rows, cols] * ret1[at, :HD].astype(F32), pre_u[rows, cols]),
                (ret2[at, HD:].astype(F32), pre[rows, h * HD : (h + 1) * HD]),
                (ret1[at, HD:].astype(F32), pre[rows, D + h * HD : D + (h + 1) * HD]),
                (ret2[at, :HD].astype(F32), pre[rows, 2 * D + h * HD : 2 * D + (h + 1) * HD]),
            )
            for part, (grad, value) in enumerate(pieces):
                grads[rows, part * D + h * HD : part * D + (h + 1) * HD] = (
                    grad * silu_slope(value)
                ).astype(BF16)
    grad_normed = dot_t(grads[...], w_inner[...])
    normed, inverse = normalize(events[...].astype(F32))
    back = inverse * (
        grad_normed
        - jnp.mean(grad_normed, axis=-1, keepdims=True)
        - normed * jnp.mean(grad_normed * normed, axis=-1, keepdims=True)
    )
    total = grad_out[...].astype(F32) + back
    row = lax.broadcasted_iota(jnp.int32, (2 * BLK, 1), 0)
    second = row >= BLK
    pos = first[0] + jnp.where(second, row - BLK, row)
    total = jnp.where(pos < jnp.where(second, lengths[1], lengths[0]), total, 0.0)
    send[:, :D] = dot(hot[...], total.astype(BF16)).astype(BF16)
    send[:, D:] = dot(hot[...], ext[...]).astype(BF16)


def table_kernel(got, table):
    rows = table.shape[0]
    packed = jnp.transpose(got[:, D:].astype(F32))
    dest = ((packed[0:1, :] - 1.0) * 32.0 + packed[1:2, :]).astype(jnp.int32)
    dest = dest - pl.program_id(0) * rows
    hot = jnp.where(
        lax.broadcasted_iota(jnp.int32, (rows, got.shape[0]), 0) == dest, 1.0, 0.0
    ).astype(BF16)
    table[...] = dot(hot, got[:, :D])


def call(kernel, outs, args, scalars=0, scratch=(), flops=0):
    vmem = pl.BlockSpec(memory_space=pltpu.VMEM)
    smem = pl.BlockSpec(memory_space=pltpu.SMEM)
    return pl.pallas_call(
        kernel,
        out_shape=[jax.ShapeDtypeStruct(shape, dtype) for shape, dtype in outs],
        in_specs=[smem] * scalars + [vmem] * (len(args) - scalars),
        out_specs=[vmem] * len(outs),
        scratch_shapes=[pltpu.VMEM(shape, dtype) for shape, dtype in scratch],
        compiler_params=pltpu.CompilerParams(vmem_limit_bytes=48 * 2**20),
        cost_estimate=pl.CostEstimate(flops=flops, bytes_accessed=2**20, transcendentals=0),
    )(*args)


def local(events, grad_out, w_inner, w_outer, valid_lengths, item_ids):
    place_y = lax.axis_index("y")
    place_p = lax.axis_index("p")
    place_c = lax.axis_index("c")
    chip = (place_y * 2 + lax.axis_index("w")) * 2 + place_p
    place = jnp.stack([place_p, place_c, 2 * place_p + place_c]).astype(jnp.int32)
    first = ((chip * 2 + place_c) * BLK).astype(jnp.int32).reshape(1)
    length = lax.dynamic_slice_in_dim(valid_lengths, place_y // 2, 1)
    inv_len = 1.0 / length.astype(F32)
    events = events.reshape(2 * BLK, D)
    grad_out = grad_out.reshape(2 * BLK, D)

    pre, send = call(
        project_kernel,
        [((2 * BLK, 3 * D), F32), ((16 * BLK, 3 * HD), BF16)],
        (events, w_inner),
        flops=10**9,
    )
    mine = lax.all_to_all(send, ("y", "w", "p"), 0, 0, tiled=True)
    swap_c = [(0, 1), (1, 0)]
    theirs = lax.ppermute(mine, "c", swap_c)
    pre_u, gated, send_g, hot, ext = call(
        gate_kernel,
        [
            ((2 * BLK, D), F32),
            ((2 * BLK, D), F32),
            ((8 * BLK, HD), BF16),
            ((CAP * 128, 2 * BLK), BF16),
            ((2 * BLK, EXT), BF16),
        ],
        (events, grad_out, w_inner[:, :D], w_outer, item_ids.reshape(1, 2 * BLK)),
        flops=10**9,
    )
    grad = lax.all_to_all(send_g, ("y", "w"), 0, 0, tiled=True)
    queries = ((1024, HD), BF16)
    (attn_one,) = call(
        functools.partial(forward_kernel, False),
        [((1024, HD), F32)],
        (place, inv_len, mine, mine),
        scalars=2,
        scratch=[queries],
        flops=10**9,
    )
    attn_out, stats = call(
        functools.partial(forward_kernel, True),
        [((1024, HD), F32), ((8, 1024), F32)],
        (place, inv_len, mine, theirs, attn_one, grad),
        scalars=2,
        scratch=[queries],
        flops=10**9,
    )
    others = [
        lax.ppermute(stats, ("y", "w"), [(i, i ^ m) for i in range(8)]) for m in (1, 2, 3)
    ]
    grad_attn, normed_out = call(
        grad_attn_kernel,
        [((1024, HD), BF16), ((1024, HD), BF16)],
        (place, length, attn_out, grad, stats, *others),
        scalars=2,
        flops=10**7,
    )
    grad_p = lax.ppermute(grad_attn, "p", swap_c)
    grad_c = lax.ppermute(grad_attn, "c", swap_c)
    grad_pc = lax.ppermute(grad_p, "c", swap_c)
    (ret1,) = call(
        grad_query_kernel,
        [((1024, 2 * HD), BF16)],
        (place, inv_len, mine, theirs, grad_attn, normed_out),
        scalars=2,
        flops=4 * 10**9,
    )
    got1 = lax.all_to_all(ret1, ("y", "w"), 0, 0, tiled=True)
    (ret2,) = call(
        grad_key_kernel,
        [((1024, 2 * HD), BF16)],
        (place, inv_len, mine, theirs, grad_attn, grad_p, grad_c, grad_pc),
        scalars=2,
        scratch=[((2048, HD), BF16), ((2048, HD), BF16)],
        flops=6 * 10**9,
    )
    got2 = lax.all_to_all(ret2, ("y", "w"), 0, 0, tiled=True)
    (rows,) = call(
        finish_kernel,
        [((CAP * 128, D + EXT), BF16)],
        (
            first,
            valid_lengths,
            got1,
            got2,
            pre_u,
            pre,
            gated,
            events,
            grad_out,
            w_inner,
            hot,
            ext,
        ),
        scalars=2,
        scratch=[((2 * BLK, 4 * D), BF16)],
        flops=10**9,
    )
    got = lax.all_to_all(
        rows.reshape(128, CAP, D + EXT), ("y", "w", "p", "c", "row"), 0, 0, tiled=True
    ).reshape(128 * CAP, D + EXT)
    return pl.pallas_call(
        table_kernel,
        out_shape=jax.ShapeDtypeStruct((ROWS_DEV, D), F32),
        grid=(4,),
        in_specs=[pl.BlockSpec((128 * CAP, D + EXT), lambda i: (0, 0))],
        out_specs=pl.BlockSpec((ROWS_DEV // 4, D), lambda i: (i, 0)),
    )(got)


def solution(mesh):
    fine = Mesh(mesh.devices.reshape(4, 2, 2, 2, 4), ("y", "w", "p", "c", "row"))
    seq = ("y", "w", "p", "c")
    return jax.shard_map(
        local,
        mesh=fine,
        in_specs=(
            P("row", seq, None),
            P("row", seq, None),
            P(),
            P(),
            P("row"),
            P("row", seq),
        ),
        out_specs=P(seq + ("row",), None),
        check_vma=False,
    )
```

```python
import functools

import jax
import jax.numpy as jnp
from jax import lax
from jax.experimental import pallas as pl
from jax.experimental.pallas import tpu as pltpu
from jax.sharding import Mesh
from jax.sharding import PartitionSpec as P

HEADS = 4
ROWS_DEV = 1024
D = 512
HD = 128
BLK = 128
CAP = 4
EXT = 128
F32 = jnp.float32
BF16 = jnp.bfloat16
SCALE = HD**-0.5
VMEM_LIMIT = 24 * 2**20


def dot(a, b):
    return lax.dot_general(a, b, (((1,), (0,)), ((), ())), preferred_element_type=F32)


def dot_t(a, b):
    return lax.dot_general(a, b, (((1,), (1,)), ((), ())), preferred_element_type=F32)


def normalize(values):
    center = values - jnp.mean(values, axis=-1, keepdims=True)
    inverse = lax.rsqrt(jnp.mean(center * center, axis=-1, keepdims=True) + 1e-05)
    return center * inverse, inverse


def silu(values):
    half = 0.5 * values
    return half * jnp.tanh(half) + half


def silu_slope(values):
    half = 0.5 * values
    two_sigma = 1.0 + jnp.tanh(half)
    return 0.5 * two_sigma * (1.0 + values - half * two_sigma)


def project_kernel(events, w_part, pre, send, normed):
    @pl.when(pl.program_id(0) == 0)
    def _():
        normed[...] = normalize(events[...].astype(F32))[0].astype(BF16)

    values = dot(normed[...], w_part[...])
    pre[...] = values
    act = silu(values).astype(BF16)
    for g in range(2):
        for h in range(HEADS):
            piece = act[g * BLK : (g + 1) * BLK, h * HD : (h + 1) * HD]
            for p in range(2):
                at = ((g * HEADS + h) * 2 + p) * BLK
                send[at : at + BLK, :] = piece


def gate_kernel(
    events, grad_out, w_u, w_outer, ids, pre, slope, normed_out, inv_out, send_g, hot, ext
):
    normed, inverse = normalize(events[...].astype(F32))
    normed_out[...] = normed
    inv_out[...] = jnp.broadcast_to(inverse, inv_out.shape)
    values = dot(normed.astype(BF16), w_u[...])
    grad_gated = dot_t(grad_out[...], w_outer[...])
    prod = (grad_gated * silu(values).astype(BF16).astype(F32)).astype(BF16)
    for g in range(2):
        for h in range(HEADS):
            at = (g * HEADS + h) * BLK
            send_g[at : at + BLK, :] = prod[g * BLK : (g + 1) * BLK, h * HD : (h + 1) * HD]
    slope[:, :D] = grad_gated * silu_slope(values)
    slope[:, D:] = silu_slope(pre[...])
    count = 2 * BLK
    id_row = ids[...]
    id_cols = jnp.transpose(jnp.broadcast_to(id_row.astype(F32), (BLK, count))).astype(jnp.int32)
    owner_row = id_row // ROWS_DEV
    owner_col = id_cols[:, :1] // ROWS_DEV
    earlier = lax.broadcasted_iota(jnp.int32, (count, count), 0) < lax.broadcasted_iota(
        jnp.int32, (count, count), 1
    )
    same = jnp.where((owner_col == owner_row) & earlier, 1, 0)
    rank = jnp.sum(same, axis=0, keepdims=True)
    slot = owner_row * CAP + rank
    slots = hot.shape[0]
    hot[...] = jnp.where(
        lax.broadcasted_iota(jnp.int32, (slots, count), 0) == slot, 1.0, 0.0
    ).astype(BF16)
    within = id_cols - (id_cols // ROWS_DEV) * ROWS_DEV
    high = within // 32
    lane = lax.broadcasted_iota(jnp.int32, (count, EXT), 1)
    ext[...] = (
        jnp.where(lane == 0, high + 1, jnp.where(lane == 1, within - high * 32, 0))
        .astype(F32)
        .astype(BF16)
    )


V_COLS, Q_COLS, K_COLS = (slice(i * HD, (i + 1) * HD) for i in range(3))


def my_place():
    p, c = lax.axis_index("p"), lax.axis_index("c")
    return p, c, 2 * p + c


def my_length(lengths):
    return lengths[lax.axis_index("y") // 2]


def inverse_of(length):
    return 1.0 / jnp.full((1, HD), length, jnp.int32).astype(F32)


def query_mask(place, core, count):
    row = lax.broadcasted_iota(jnp.int32, (count, 2 * BLK), 0)
    lane = lax.broadcasted_iota(jnp.int32, (count, 2 * BLK), 1)
    col = lane + jnp.where(lane >= BLK, BLK, 0) + core * BLK
    return (row >= BLK) | (col <= row + place[2] * BLK)


def key_mask(place, core, count):
    row = lax.broadcasted_iota(jnp.int32, (count, 2 * BLK), 0) - (count - BLK)
    lane = lax.broadcasted_iota(jnp.int32, (count, 2 * BLK), 1)
    col = lane + jnp.where(lane >= BLK, BLK, 0) + core * BLK
    return (row < 0) | (row + place[2] * BLK <= col)


def own_blocks(place, src, cols, dst):
    for m in range(8):
        at = pl.multiple_of((2 * m + place[0]) * BLK, BLK)
        dst[m * BLK : (m + 1) * BLK, :] = src[pl.ds(at, BLK), cols]


def forward_kernel(last, lengths, mine, *refs):
    place = my_place()
    inv_len = inverse_of(my_length(lengths))
    if last:
        theirs, before, grad, out, stats, queries = refs
        keys_of, core = theirs, 1 - place[1]
    else:
        out, queries = refs
        keys_of, core = mine, place[1]
    own_blocks(place, mine, Q_COLS, queries)
    out[...] = before[...] if last else jnp.zeros_like(out)
    for j in range(8):
        keys = slice(j * 2 * BLK, (j + 1) * 2 * BLK)
        rows = slice(j * BLK, 8 * BLK)
        half = dot_t(queries[rows, :], keys_of[keys, K_COLS]) * (0.5 * SCALE)
        attn = half * jnp.tanh(half) + half
        attn = jnp.where(query_mask(place, core, (8 - j) * BLK), attn, 0.0)
        out[rows, :] += dot(attn.astype(BF16), keys_of[keys, V_COLS])
    if not last:
        return
    for m in range(8):
        rows = slice(m * BLK, (m + 1) * BLK)
        total = out[rows, :] * inv_len
        out[rows, :] = total
        g = grad[rows, :].astype(F32)
        mean = jnp.mean(total, axis=-1, keepdims=True)
        center = total - mean
        square = jnp.sum(center * center, axis=-1, keepdims=True)
        sum_g = jnp.sum(g, axis=-1, keepdims=True)
        sum_ga = jnp.sum(g * center, axis=-1, keepdims=True)
        lane = lax.broadcasted_iota(jnp.int32, (BLK, BLK), 1)
        packed = jnp.where(
            lane == 0, mean, jnp.where(lane == 1, square, jnp.where(lane == 2, sum_g, sum_ga))
        )
        stats[:, rows] = jnp.transpose(packed)[:8, :]


def grad_attn_kernel(lengths, attn_out, grad, s0, s1, s2, s3, grad_attn, normed_out):
    place = my_place()
    length = my_length(lengths)
    parts = [s0[...], s1[...], s2[...], s3[...]]
    means = [part[0:1, :] for part in parts]
    mean = 0.25 * (means[0] + means[1] + means[2] + means[3])
    square = 0.0
    sum_g = 0.0
    sum_ga = 0.0
    for part, own in zip(parts, means):
        shift = own - mean
        square = square + part[1:2, :] + HD * (shift * shift)
        sum_g = sum_g + part[2:3, :]
        sum_ga = sum_ga + part[3:4, :] + part[2:3, :] * shift
    inverse = lax.rsqrt(square * (1.0 / D) + 1e-05)
    mean_g = sum_g * (1.0 / D)
    mean_gn = inverse * sum_ga * (1.0 / D)
    row = lax.broadcasted_iota(jnp.int32, (BLK, 1024), 0)
    packed = jnp.where(
        row == 0, mean, jnp.where(row == 1, inverse, jnp.where(row == 2, mean_g, mean_gn))
    )
    for m in range(8):
        rows = slice(m * BLK, (m + 1) * BLK)
        cols = jnp.transpose(packed[:, rows])
        inv = cols[:, 1:2]
        n = (attn_out[rows, :] - cols[:, 0:1]) * inv
        back = (grad[rows, :].astype(F32) - cols[:, 2:3] - n * cols[:, 3:4]) * inv
        pos = lax.broadcasted_iota(jnp.int32, (BLK, 1), 0) + (m * 4 + place[2]) * BLK
        grad_attn[rows, :] = jnp.where(pos < length, back, 0.0).astype(BF16)
        normed_out[rows, :] = n.astype(BF16)


def slopes(raw):
    half = raw * (0.5 * SCALE)
    t = jnp.tanh(half)
    two_sigma = 1.0 + t
    return two_sigma + half * (1.0 - t * t), half * two_sigma


def grad_query_kernel(lengths, mine, theirs, grad_attn, ret, queries, total):
    place = my_place()
    inv_len = inverse_of(my_length(lengths))
    own_blocks(place, mine, Q_COLS, queries)
    total[...] = jnp.zeros_like(total)
    for j in range(8):
        keys = slice(j * 2 * BLK, (j + 1) * 2 * BLK)
        rows = slice(j * BLK, 8 * BLK)
        for src, core in ((mine, place[1]), (theirs, 1 - place[1])):
            k = src[keys, K_COLS]
            slope, _ = slopes(dot_t(queries[rows, :], k))
            score = slope * dot_t(grad_attn[rows, :], src[keys, V_COLS])
            score = jnp.where(query_mask(place, core, (8 - j) * BLK), score, 0.0)
            total[rows, :] += dot(score.astype(BF16), k)
    ret[...] = (total[...] * (0.5 * SCALE * inv_len)).astype(BF16)


def grad_key_kernel(
    lengths,
    mine,
    theirs,
    g_own,
    g_p,
    g_c,
    g_pc,
    normed_out,
    grad_q,
    ret,
    mine_g,
    theirs_g,
    keys,
    values,
    grad_k,
    grad_v,
):
    place = my_place()
    inv_len = inverse_of(my_length(lengths))
    p = place[0]
    own_blocks(place, mine, K_COLS, keys)
    own_blocks(place, mine, V_COLS, values)
    for m in range(8):
        rows = slice(m * BLK, (m + 1) * BLK)
        here = pl.multiple_of((2 * m + p) * BLK, BLK)
        there = pl.multiple_of((2 * m + 1 - p) * BLK, BLK)
        mine_g[pl.ds(here, BLK), :] = g_own[rows, :]
        mine_g[pl.ds(there, BLK), :] = g_p[rows, :]
        theirs_g[pl.ds(here, BLK), :] = g_c[rows, :]
        theirs_g[pl.ds(there, BLK), :] = g_pc[rows, :]
    grad_k[...] = jnp.zeros_like(grad_k)
    grad_v[...] = jnp.zeros_like(grad_v)
    for j in range(8):
        events = slice(j * 2 * BLK, (j + 1) * 2 * BLK)
        rows = slice(0, (j + 1) * BLK)
        for src, src_g, core in ((mine, mine_g, place[1]), (theirs, theirs_g, 1 - place[1])):
            q = src[events, Q_COLS]
            ga = src_g[events, :]
            slope, attn = slopes(dot_t(keys[rows, :], q))
            mask = key_mask(place, core, (j + 1) * BLK)
            score = jnp.where(mask, slope * dot_t(values[rows, :], ga), 0.0)
            attn = jnp.where(mask, attn, 0.0)
            grad_k[rows, :] += dot(score.astype(BF16), q)
            grad_v[rows, :] += dot(attn.astype(BF16), ga)
    ret[:, :HD] = normed_out[...]
    ret[:, HD : 2 * HD] = (grad_v[...] * inv_len).astype(BF16)
    ret[:, 2 * HD : 3 * HD] = grad_q[...]
    ret[:, 3 * HD :] = (grad_k[...] * (0.5 * SCALE * inv_len)).astype(BF16)


def finish_kernel(
    lengths, ret, slope, normed, inverse, grad_out, w_inner, hot, ext, send, grads
):
    for g in range(2):
        rows = slice(g * BLK, (g + 1) * BLK)
        for h in range(HEADS):
            at = slice((g * HEADS + h) * BLK, (g * HEADS + h + 1) * BLK)
            for part in range(4):
                cols = slice(part * D + h * HD, part * D + (h + 1) * HD)
                grad = ret[at, part * HD : (part + 1) * HD].astype(F32)
                grads[rows, cols] = (grad * slope[rows, cols]).astype(BF16)
    grad_normed = dot_t(grads[...], w_inner[...])
    back = inverse[:, :1] * (
        grad_normed
        - jnp.mean(grad_normed, axis=-1, keepdims=True)
        - normed[...] * jnp.mean(grad_normed * normed[...], axis=-1, keepdims=True)
    )
    total = grad_out[...].astype(F32) + back
    chip = (lax.axis_index("y") * 2 + lax.axis_index("w")) * 2 + lax.axis_index("p")
    first = (chip * 2 + lax.axis_index("c")) * BLK
    row = lax.broadcasted_iota(jnp.int32, (2 * BLK, 1), 0)
    second = row >= BLK
    pos = first + jnp.where(second, row - BLK, row)
    total = jnp.where(pos < jnp.where(second, lengths[1], lengths[0]), total, 0.0)
    send[:, :D] = dot(hot[...], total.astype(BF16)).astype(BF16)
    send[:, D:] = dot(hot[...], ext[...]).astype(BF16)


def table_kernel(got, table):
    packed = jnp.transpose(got[:, D:].astype(F32))
    dest = ((packed[0:1, :] - 1.0) * 32.0 + packed[1:2, :]).astype(jnp.int32)
    rows = 256
    for i in range(ROWS_DEV // rows):
        hot = jnp.where(
            lax.broadcasted_iota(jnp.int32, (rows, got.shape[0]), 0) == dest - i * rows, 1.0, 0.0
        ).astype(BF16)
        table[i * rows : (i + 1) * rows, :] = dot(hot, got[:, :D])


def call(kernel, outs, args, scalars=1, scratch=(), flops=0):
    vmem = pl.BlockSpec(memory_space=pltpu.VMEM)
    smem = pl.BlockSpec(memory_space=pltpu.SMEM)
    return pl.pallas_call(
        kernel,
        out_shape=[jax.ShapeDtypeStruct(shape, dtype) for shape, dtype in outs],
        in_specs=[smem] * scalars + [vmem] * (len(args) - scalars),
        out_specs=[vmem] * len(outs),
        scratch_shapes=[pltpu.VMEM(shape, dtype) for shape, dtype in scratch],
        compiler_params=pltpu.CompilerParams(vmem_limit_bytes=VMEM_LIMIT),
        cost_estimate=pl.CostEstimate(flops=flops, bytes_accessed=2**20, transcendentals=0),
    )(*args)


def project(events, w_inner):
    return pl.pallas_call(
        project_kernel,
        grid=(3,),
        out_shape=[
            jax.ShapeDtypeStruct((2 * BLK, 3 * D), F32),
            jax.ShapeDtypeStruct((16 * BLK, 3 * HD), BF16),
        ],
        in_specs=[
            pl.BlockSpec((2 * BLK, D), lambda i: (0, 0)),
            pl.BlockSpec((D, D), lambda i: (0, i + 1)),
        ],
        out_specs=[
            pl.BlockSpec((2 * BLK, D), lambda i: (0, i)),
            pl.BlockSpec((16 * BLK, HD), lambda i: (0, i)),
        ],
        scratch_shapes=[pltpu.VMEM((2 * BLK, D), BF16)],
        compiler_params=pltpu.CompilerParams(vmem_limit_bytes=VMEM_LIMIT),
    )(events, w_inner)


def local(events, grad_out, w_inner, w_outer, valid_lengths, item_ids):
    events = events.reshape(2 * BLK, D)
    grad_out = grad_out.reshape(2 * BLK, D)
    pre, send = project(events, w_inner)
    mine = lax.all_to_all(send, ("y", "w", "p"), 0, 0, tiled=True)
    slope, normed, inverse, send_g, hot, ext = call(
        gate_kernel,
        [
            ((2 * BLK, 4 * D), F32),
            ((2 * BLK, D), F32),
            ((2 * BLK, HD), F32),
            ((8 * BLK, HD), BF16),
            ((CAP * 128, 2 * BLK), BF16),
            ((2 * BLK, EXT), BF16),
        ],
        (events, grad_out, w_inner[:, :D], w_outer, item_ids.reshape(1, 2 * BLK), pre),
        scalars=0,
        flops=10**9,
    )
    grad = lax.all_to_all(send_g, ("y", "w"), 0, 0, tiled=True)
    mine, grad = lax.optimization_barrier((mine, grad))
    theirs = lax.ppermute(mine, "c", [(0, 1), (1, 0)])
    queries = ((1024, HD), BF16)
    (attn_one,) = call(
        functools.partial(forward_kernel, False),
        [((1024, HD), F32)],
        (valid_lengths, mine),
        scratch=[queries],
        flops=10**9,
    )
    attn_out, stats = call(
        functools.partial(forward_kernel, True),
        [((1024, HD), F32), ((8, 1024), F32)],
        (valid_lengths, mine, theirs, attn_one, grad),
        scratch=[queries],
        flops=10**9,
    )
    others = [
        lax.ppermute(stats, ("y", "w"), [(i, i ^ m) for i in range(8)]) for m in (1, 2, 3)
    ]
    grad_attn, normed_out = call(
        grad_attn_kernel,
        [((1024, HD), BF16), ((1024, HD), BF16)],
        (valid_lengths, attn_out, grad, stats, *others),
        flops=10**7,
    )
    grad_p, grad_c, grad_pc = [
        lax.ppermute(grad_attn, ("p", "c"), [(i, i ^ m) for i in range(4)]) for m in (2, 1, 3)
    ]
    (grad_q,) = call(
        grad_query_kernel,
        [((1024, HD), BF16)],
        (valid_lengths, mine, theirs, grad_attn),
        scratch=[queries, ((1024, HD), F32)],
        flops=4 * 10**9,
    )
    (ret,) = call(
        grad_key_kernel,
        [((1024, 4 * HD), BF16)],
        (
            valid_lengths,
            mine,
            theirs,
            grad_attn,
            grad_p,
            grad_c,
            grad_pc,
            normed_out,
            grad_q,
        ),
        scratch=[((2048, HD), BF16)] * 2 + [queries] * 2 + [((1024, HD), F32)] * 2,
        flops=6 * 10**9,
    )
    got = lax.all_to_all(ret, ("y", "w"), 0, 0, tiled=True)
    (rows,) = call(
        finish_kernel,
        [((CAP * 128, D + EXT), BF16)],
        (valid_lengths, got, slope, normed, inverse, grad_out, w_inner, hot, ext),
        scratch=[((2 * BLK, 4 * D), BF16)],
        flops=10**9,
    )
    got = lax.all_to_all(
        rows.reshape(128, CAP, D + EXT), ("y", "w", "p", "c", "row"), 0, 0, tiled=True
    ).reshape(128 * CAP, D + EXT)
    (table,) = call(table_kernel, [((ROWS_DEV, D), F32)], (got,), scalars=0)
    return table


def solution(mesh):
    fine = Mesh(mesh.devices.reshape(4, 2, 2, 2, 4), ("y", "w", "p", "c", "row"))
    seq = ("y", "w", "p", "c")
    return jax.shard_map(
        local,
        mesh=fine,
        in_specs=(
            P("row", seq, None),
            P("row", seq, None),
            P(),
            P(),
            P("row"),
            P("row", seq),
        ),
        out_specs=P(seq + ("row",), None),
        check_vma=False,
    )
```

```python
import functools

import jax
import jax.numpy as jnp
from jax import lax
from jax.experimental import pallas as pl
from jax.experimental.pallas import tpu as pltpu
from jax.sharding import Mesh
from jax.sharding import PartitionSpec as P

HEADS = 4
ROWS_DEV = 1024
D = 512
HD = 128
BLK = 128
CAP = 4
EXT = 128
F32 = jnp.float32
BF16 = jnp.bfloat16
SCALE = HD**-0.5
VMEM_LIMIT = 12 * 2**20
PROJECT_LIMIT = 60 * 2**20


def dot(a, b):
    return lax.dot_general(a, b, (((1,), (0,)), ((), ())), preferred_element_type=F32)


def dot_t(a, b):
    return lax.dot_general(a, b, (((1,), (1,)), ((), ())), preferred_element_type=F32)


def normalize(values):
    center = values - jnp.mean(values, axis=-1, keepdims=True)
    inverse = lax.rsqrt(jnp.mean(center * center, axis=-1, keepdims=True) + 1e-05)
    return center * inverse, inverse


def silu(values):
    half = 0.5 * values
    return half * jnp.tanh(half) + half


def silu_slope(values):
    half = 0.5 * values
    two_sigma = 1.0 + jnp.tanh(half)
    return 0.5 * two_sigma * (1.0 + values - half * two_sigma)


def project_kernel(
    events_hbm, grad_hbm, w_hbm, w_outer_hbm, send, events, grad_out, weights, w_outer, sems
):
    copies = [pltpu.make_async_copy(events_hbm, events, sems.at[4])]
    for part in (1, 2, 3, 0):
        cols = slice(part * D, (part + 1) * D)
        copies.append(pltpu.make_async_copy(w_hbm.at[:, cols], weights.at[part], sems.at[part]))
    copies.append(pltpu.make_async_copy(w_outer_hbm, w_outer, sems.at[5]))
    copies.append(pltpu.make_async_copy(grad_hbm, grad_out, sems.at[6]))
    for copy in copies:
        copy.start()
    copies[0].wait()
    normed = normalize(events[...].astype(F32))[0].astype(BF16)
    for slot, part in enumerate((1, 2, 3, 0)):
        copies[slot + 1].wait()
        act = silu(dot(normed, weights[part])).astype(BF16)
        if part == 0:
            copies[5].wait()
            copies[6].wait()
            act = (dot_t(grad_out[...], w_outer[...]) * act.astype(F32)).astype(BF16)
        for g in range(2):
            for h in range(HEADS):
                piece = act[g * BLK : (g + 1) * BLK, h * HD : (h + 1) * HD]
                for p in range(2):
                    at = ((g * HEADS + h) * 2 + p) * BLK
                    send[at : at + BLK, slot * HD : (slot + 1) * HD] = piece


def gate_kernel(events, grad_out, w_inner, w_outer, ids, slope, normed_out, inv_out, hot, ext):
    normed, inverse = normalize(events[...].astype(F32))
    normed_out[...] = normed
    inv_out[...] = jnp.broadcast_to(inverse, inv_out.shape)
    normed = normed.astype(BF16)
    for part in range(4):
        cols = slice(part * D, (part + 1) * D)
        values = silu_slope(dot(normed, w_inner[:, cols]))
        if part == 0:
            values = values * dot_t(grad_out[...], w_outer[...])
        slope[:, cols] = values
    count = 2 * BLK
    id_row = ids[...]
    id_cols = jnp.transpose(jnp.broadcast_to(id_row.astype(F32), (BLK, count))).astype(jnp.int32)
    owner_row = id_row // ROWS_DEV
    owner_col = id_cols[:, :1] // ROWS_DEV
    earlier = lax.broadcasted_iota(jnp.int32, (count, count), 0) < lax.broadcasted_iota(
        jnp.int32, (count, count), 1
    )
    same = jnp.where((owner_col == owner_row) & earlier, 1, 0)
    rank = jnp.sum(same, axis=0, keepdims=True)
    slot = owner_row * CAP + rank
    slots = hot.shape[0]
    hot[...] = jnp.where(
        lax.broadcasted_iota(jnp.int32, (slots, count), 0) == slot, 1.0, 0.0
    ).astype(BF16)
    within = id_cols - (id_cols // ROWS_DEV) * ROWS_DEV
    high = within // 32
    lane = lax.broadcasted_iota(jnp.int32, (count, EXT), 1)
    ext[...] = (
        jnp.where(lane == 0, high + 1, jnp.where(lane == 1, within - high * 32, 0))
        .astype(F32)
        .astype(BF16)
    )


V_COLS, Q_COLS, K_COLS, G_COLS = (slice(i * HD, (i + 1) * HD) for i in range(4))


def my_place():
    p, c = lax.axis_index("p"), lax.axis_index("c")
    return p, c, 2 * p + c


def my_length(lengths):
    return lengths[lax.axis_index("y") // 2]


def inverse_of(length):
    return 1.0 / jnp.full((1, HD), length, jnp.int32).astype(F32)


def diagonal(place, core, rows_are_keys):
    row = lax.broadcasted_iota(jnp.int32, (BLK, 2 * BLK), 0) + place[2] * BLK
    lane = lax.broadcasted_iota(jnp.int32, (BLK, 2 * BLK), 1)
    col = lane + jnp.where(lane >= BLK, BLK, 0) + core * BLK
    return row <= col if rows_are_keys else col <= row


def mask_first(mask, values):
    first = jnp.where(mask, values[:BLK, :], 0.0)
    return jnp.concatenate([first, values[BLK:, :]], axis=0) if values.shape[0] > BLK else first


def mask_last(mask, values):
    last = jnp.where(mask, values[-BLK:, :], 0.0)
    return jnp.concatenate([values[:-BLK, :], last], axis=0) if values.shape[0] > BLK else last


def own_blocks(place, src, cols, dst):
    for m in range(8):
        at = pl.multiple_of((2 * m + place[0]) * BLK, BLK)
        dst[m * BLK : (m + 1) * BLK, :] = src[pl.ds(at, BLK), cols]


def forward_kernel(last, lengths, mine, *refs):
    place = my_place()
    if last:
        theirs, before, out, stats, grad, queries = refs
        keys_of, core = theirs, 1 - place[1]
        own_blocks(place, mine, G_COLS, grad)
        out[...] = before[...]
    else:
        out, queries = refs
        keys_of, core = mine, place[1]
        out[...] = jnp.zeros_like(out)
    own_blocks(place, mine, Q_COLS, queries)
    mask = diagonal(place, core, False)
    for j in range(8):
        keys = slice(j * 2 * BLK, (j + 1) * 2 * BLK)
        rows = slice(j * BLK, 8 * BLK)
        half = dot_t(queries[rows, :], keys_of[keys, K_COLS]) * (0.5 * SCALE)
        attn = half * jnp.tanh(half) + half
        attn = mask_first(mask, attn)
        out[rows, :] += dot(attn.astype(BF16), keys_of[keys, V_COLS])
    if not last:
        return
    inv_len = inverse_of(my_length(lengths))
    for m in range(8):
        rows = slice(m * BLK, (m + 1) * BLK)
        total = out[rows, :] * inv_len
        out[rows, :] = total
        g = grad[rows, :].astype(F32)
        mean = jnp.mean(total, axis=-1, keepdims=True)
        center = total - mean
        square = jnp.sum(center * center, axis=-1, keepdims=True)
        sum_g = jnp.sum(g, axis=-1, keepdims=True)
        sum_ga = jnp.sum(g * center, axis=-1, keepdims=True)
        lane = lax.broadcasted_iota(jnp.int32, (BLK, BLK), 1)
        packed = jnp.where(
            lane == 0, mean, jnp.where(lane == 1, square, jnp.where(lane == 2, sum_g, sum_ga))
        )
        stats[:, rows] = jnp.transpose(packed)[:8, :]


def grad_attn_kernel(lengths, attn_out, grad, s0, s1, s2, s3, grad_attn, normed_out):
    place = my_place()
    length = my_length(lengths)
    parts = [s0[...], s1[...], s2[...], s3[...]]
    means = [part[0:1, :] for part in parts]
    mean = 0.25 * (means[0] + means[1] + means[2] + means[3])
    square = 0.0
    sum_g = 0.0
    sum_ga = 0.0
    for part, own in zip(parts, means):
        shift = own - mean
        square = square + part[1:2, :] + HD * (shift * shift)
        sum_g = sum_g + part[2:3, :]
        sum_ga = sum_ga + part[3:4, :] + part[2:3, :] * shift
    inverse = lax.rsqrt(square * (1.0 / D) + 1e-05)
    mean_g = sum_g * (1.0 / D)
    mean_gn = inverse * sum_ga * (1.0 / D)
    row = lax.broadcasted_iota(jnp.int32, (BLK, 1024), 0)
    packed = jnp.where(
        row == 0, mean, jnp.where(row == 1, inverse, jnp.where(row == 2, mean_g, mean_gn))
    )
    for m in range(8):
        rows = slice(m * BLK, (m + 1) * BLK)
        cols = jnp.transpose(packed[:, rows])
        inv = cols[:, 1:2]
        n = (attn_out[rows, :] - cols[:, 0:1]) * inv
        back = (grad[rows, :].astype(F32) - cols[:, 2:3] - n * cols[:, 3:4]) * inv
        pos = lax.broadcasted_iota(jnp.int32, (BLK, 1), 0) + (m * 4 + place[2]) * BLK
        grad_attn[rows, :] = jnp.where(pos < length, back, 0.0).astype(BF16)
        normed_out[rows, :] = n.astype(BF16)


def slopes(raw):
    half = raw * (0.5 * SCALE)
    t = jnp.tanh(half)
    two_sigma = 1.0 + t
    return two_sigma + half * (1.0 - t * t), half * two_sigma


def grad_query_kernel(last, lengths, mine, *refs):
    place = my_place()
    if last:
        theirs, grad_attn, before, ret, queries, total = refs
        src, core = theirs, 1 - place[1]
        total[...] = before[...]
    else:
        grad_attn, total, queries = refs
        src, core = mine, place[1]
        total[...] = jnp.zeros_like(total)
    own_blocks(place, mine, Q_COLS, queries)
    mask = diagonal(place, core, False)
    for j in range(8):
        keys = slice(j * 2 * BLK, (j + 1) * 2 * BLK)
        rows = slice(j * BLK, 8 * BLK)
        k = src[keys, K_COLS]
        slope, _ = slopes(dot_t(queries[rows, :], k))
        score = slope * dot_t(grad_attn[rows, :], src[keys, V_COLS])
        score = mask_first(mask, score)
        total[rows, :] += dot(score.astype(BF16), k)
    if last:
        inv_len = inverse_of(my_length(lengths))
        ret[...] = (total[...] * (0.5 * SCALE * inv_len)).astype(BF16)


def packed_rows(j):
    return slice(j * (j + 1) // 2 * BLK, (j + 1) * (j + 2) // 2 * BLK)


def key_scores_kernel(other, mine, *refs):
    place = my_place()
    if other:
        src, slope_out, attn_out, keys = refs
        core = 1 - place[1]
    else:
        slope_out, attn_out, keys = refs
        src, core = mine, place[1]
    own_blocks(place, mine, K_COLS, keys)
    mask = diagonal(place, core, True)
    for j in range(8):
        events = slice(j * 2 * BLK, (j + 1) * 2 * BLK)
        rows = slice(0, (j + 1) * BLK)
        slope, attn = slopes(dot_t(keys[rows, :], src[events, Q_COLS]))
        slope_out[packed_rows(j), :] = mask_last(mask, slope)
        attn_out[packed_rows(j), :] = mask_last(mask, attn).astype(BF16)


def grad_key_kernel(
    lengths,
    mine,
    theirs,
    slope_m,
    attn_m,
    slope_t,
    attn_t,
    g_own,
    g_p,
    g_c,
    g_pc,
    normed_out,
    grad_q,
    ret,
    mine_g,
    theirs_g,
    values,
    grad_k,
    grad_v,
):
    place = my_place()
    inv_len = inverse_of(my_length(lengths))
    p = place[0]
    own_blocks(place, mine, V_COLS, values)
    for m in range(8):
        rows = slice(m * BLK, (m + 1) * BLK)
        here = pl.multiple_of((2 * m + p) * BLK, BLK)
        there = pl.multiple_of((2 * m + 1 - p) * BLK, BLK)
        mine_g[pl.ds(here, BLK), :] = g_own[rows, :]
        mine_g[pl.ds(there, BLK), :] = g_p[rows, :]
        theirs_g[pl.ds(here, BLK), :] = g_c[rows, :]
        theirs_g[pl.ds(there, BLK), :] = g_pc[rows, :]
    grad_k[...] = jnp.zeros_like(grad_k)
    grad_v[...] = jnp.zeros_like(grad_v)
    for j in range(8):
        events = slice(j * 2 * BLK, (j + 1) * 2 * BLK)
        rows = slice(0, (j + 1) * BLK)
        for src, src_g, slope, attn in (
            (mine, mine_g, slope_m, attn_m),
            (theirs, theirs_g, slope_t, attn_t),
        ):
            ga = src_g[events, :]
            score = slope[packed_rows(j), :] * dot_t(values[rows, :], ga)
            grad_k[rows, :] += dot(score.astype(BF16), src[events, Q_COLS])
            grad_v[rows, :] += dot(attn[packed_rows(j), :], ga)
    ret[:, :HD] = normed_out[...]
    ret[:, HD : 2 * HD] = (grad_v[...] * inv_len).astype(BF16)
    ret[:, 2 * HD : 3 * HD] = grad_q[...]
    ret[:, 3 * HD :] = (grad_k[...] * (0.5 * SCALE * inv_len)).astype(BF16)


def finish_kernel(
    lengths, ret, slope, normed, inverse, grad_out, w_inner, hot, ext, send, grads
):
    for g in range(2):
        rows = slice(g * BLK, (g + 1) * BLK)
        for h in range(HEADS):
            at = slice((g * HEADS + h) * BLK, (g * HEADS + h + 1) * BLK)
            for part in range(4):
                cols = slice(part * D + h * HD, part * D + (h + 1) * HD)
                grad = ret[at, part * HD : (part + 1) * HD].astype(F32)
                grads[rows, cols] = (grad * slope[rows, cols]).astype(BF16)
    grad_normed = dot_t(grads[...], w_inner[...])
    back = inverse[:, :1] * (
        grad_normed
        - jnp.mean(grad_normed, axis=-1, keepdims=True)
        - normed[...] * jnp.mean(grad_normed * normed[...], axis=-1, keepdims=True)
    )
    total = grad_out[...].astype(F32) + back
    chip = (lax.axis_index("y") * 2 + lax.axis_index("w")) * 2 + lax.axis_index("p")
    first = (chip * 2 + lax.axis_index("c")) * BLK
    row = lax.broadcasted_iota(jnp.int32, (2 * BLK, 1), 0)
    second = row >= BLK
    pos = first + jnp.where(second, row - BLK, row)
    total = jnp.where(pos < jnp.where(second, lengths[1], lengths[0]), total, 0.0)
    send[:, :D] = dot(hot[...], total.astype(BF16)).astype(BF16)
    send[:, D:] = dot(hot[...], ext[...]).astype(BF16)


def table_kernel(got, table):
    packed = jnp.transpose(got[:, D:].astype(F32))
    dest = ((packed[0:1, :] - 1.0) * 32.0 + packed[1:2, :]).astype(jnp.int32)
    rows = 256
    for i in range(ROWS_DEV // rows):
        hot = jnp.where(
            lax.broadcasted_iota(jnp.int32, (rows, got.shape[0]), 0) == dest - i * rows, 1.0, 0.0
        ).astype(BF16)
        table[i * rows : (i + 1) * rows, :] = dot(hot, got[:, :D])


def call(kernel, outs, args, scalars=1, scratch=(), flops=0):
    vmem = pl.BlockSpec(memory_space=pltpu.VMEM)
    smem = pl.BlockSpec(memory_space=pltpu.SMEM)
    return pl.pallas_call(
        kernel,
        out_shape=[jax.ShapeDtypeStruct(shape, dtype) for shape, dtype in outs],
        in_specs=[smem] * scalars + [vmem] * (len(args) - scalars),
        out_specs=[vmem] * len(outs),
        scratch_shapes=[pltpu.VMEM(shape, dtype) for shape, dtype in scratch],
        compiler_params=pltpu.CompilerParams(vmem_limit_bytes=VMEM_LIMIT),
        cost_estimate=pl.CostEstimate(flops=flops, bytes_accessed=2**20, transcendentals=0),
    )(*args)


def project(*args):
    hbm = pl.BlockSpec(memory_space=pltpu.HBM)
    vmem = pl.BlockSpec(memory_space=pltpu.VMEM)
    return pl.pallas_call(
        project_kernel,
        out_shape=jax.ShapeDtypeStruct((16 * BLK, 4 * HD), BF16),
        in_specs=[hbm] * len(args),
        out_specs=vmem,
        scratch_shapes=[
            pltpu.VMEM((2 * BLK, D), BF16),
            pltpu.VMEM((2 * BLK, D), BF16),
            pltpu.VMEM((4, D, D), BF16),
            pltpu.VMEM((D, D), BF16),
            pltpu.SemaphoreType.DMA((7,)),
        ],
        compiler_params=pltpu.CompilerParams(vmem_limit_bytes=PROJECT_LIMIT),
    )(*args)


def local(events, grad_out, w_inner, w_outer, valid_lengths, item_ids):
    events = events.reshape(2 * BLK, D)
    grad_out = grad_out.reshape(2 * BLK, D)
    rows_bf16, rows_f32 = ((1024, HD), BF16), ((1024, HD), F32)
    swap_c = [(0, 1), (1, 0)]
    send = project(events, grad_out, w_inner, w_outer)
    mine = lax.all_to_all(send, ("y", "w", "p"), 0, 0, tiled=True)
    slope, normed, inverse, hot, ext = call(
        gate_kernel,
        [
            ((2 * BLK, 4 * D), F32),
            ((2 * BLK, D), F32),
            ((2 * BLK, HD), F32),
            ((CAP * 128, 2 * BLK), BF16),
            ((2 * BLK, EXT), BF16),
        ],
        (events, grad_out, w_inner, w_outer, item_ids.reshape(1, 2 * BLK)),
        scalars=0,
        flops=2 * 10**9,
    )
    mine, slope = lax.optimization_barrier((mine, slope))
    theirs = lax.ppermute(mine, "c", swap_c)
    (attn_one,) = call(
        functools.partial(forward_kernel, False),
        [rows_f32],
        (valid_lengths, mine),
        scratch=[rows_bf16],
        flops=10**9,
    )
    score_shapes = [((36 * BLK, 2 * BLK), F32), ((36 * BLK, 2 * BLK), BF16)]
    scores_m = call(
        functools.partial(key_scores_kernel, False),
        score_shapes,
        (mine,),
        scalars=0,
        scratch=[rows_bf16],
        flops=10**9,
    )
    theirs, scores_m, attn_one = lax.optimization_barrier((theirs, scores_m, attn_one))
    attn_out, stats, grad = call(
        functools.partial(forward_kernel, True),
        [rows_f32, ((8, 1024), F32), rows_bf16],
        (valid_lengths, mine, theirs, attn_one),
        scratch=[rows_bf16],
        flops=10**9,
    )
    others = [
        lax.ppermute(stats, ("y", "w"), [(i, i ^ m) for i in range(8)]) for m in (1, 2, 3)
    ]
    scores_t = call(
        functools.partial(key_scores_kernel, True),
        score_shapes,
        (mine, theirs),
        scalars=0,
        scratch=[rows_bf16],
        flops=10**9,
    )
    others, scores_t = lax.optimization_barrier((others, scores_t))
    grad_attn, normed_out = call(
        grad_attn_kernel,
        [rows_bf16, rows_bf16],
        (valid_lengths, attn_out, grad, stats, *others),
        flops=10**7,
    )
    grad_p, grad_c = [
        lax.ppermute(grad_attn, ("p", "c"), [(i, i ^ m) for i in range(4)]) for m in (2, 1)
    ]
    (grad_q,) = call(
        functools.partial(grad_query_kernel, False),
        [rows_f32],
        (valid_lengths, mine, grad_attn),
        scratch=[rows_bf16],
        flops=2 * 10**9,
    )
    grad_p, grad_q = lax.optimization_barrier((grad_p, grad_q))
    grad_pc = lax.ppermute(grad_p, "c", swap_c)
    (grad_q,) = call(
        functools.partial(grad_query_kernel, True),
        [rows_bf16],
        (valid_lengths, mine, theirs, grad_attn, grad_q),
        scratch=[rows_bf16, rows_f32],
        flops=2 * 10**9,
    )
    (ret,) = call(
        grad_key_kernel,
        [((1024, 4 * HD), BF16)],
        (
            valid_lengths,
            mine,
            theirs,
            *scores_m,
            *scores_t,
            grad_attn,
            grad_p,
            grad_c,
            grad_pc,
            normed_out,
            grad_q,
        ),
        scratch=[((2048, HD), BF16)] * 2 + [rows_bf16] + [rows_f32] * 2,
        flops=6 * 10**9,
    )
    got = lax.all_to_all(ret, ("y", "w"), 0, 0, tiled=True)
    (rows,) = call(
        finish_kernel,
        [((CAP * 128, D + EXT), BF16)],
        (valid_lengths, got, slope, normed, inverse, grad_out, w_inner, hot, ext),
        scratch=[((2 * BLK, 4 * D), BF16)],
        flops=10**9,
    )
    got = lax.all_to_all(
        rows.reshape(128, CAP, D + EXT), ("y", "w", "p", "c", "row"), 0, 0, tiled=True
    ).reshape(128 * CAP, D + EXT)
    (table,) = call(table_kernel, [((ROWS_DEV, D), F32)], (got,), scalars=0)
    return table


def solution(mesh):
    fine = Mesh(mesh.devices.reshape(4, 2, 2, 2, 4), ("y", "w", "p", "c", "row"))
    seq = ("y", "w", "p", "c")
    return jax.shard_map(
        local,
        mesh=fine,
        in_specs=(
            P("row", seq, None),
            P("row", seq, None),
            P(),
            P(),
            P("row"),
            P("row", seq),
        ),
        out_specs=P(seq + ("row",), None),
        check_vma=False,
    )
```

```python
import functools

import jax
import jax.numpy as jnp
from jax import lax
from jax.experimental import pallas as pl
from jax.experimental.pallas import tpu as pltpu
from jax.sharding import Mesh
from jax.sharding import PartitionSpec as P

HEADS = 4
ROWS_DEV = 1024
D = 512
HD = 128
BLK = 128
CAP = 4
EXT = 128
F32 = jnp.float32
BF16 = jnp.bfloat16
SCALE = HD**-0.5
VMEM_LIMIT = 12 * 2**20
PROJECT_LIMIT = 60 * 2**20


def dot(a, b):
    return lax.dot_general(a, b, (((1,), (0,)), ((), ())), preferred_element_type=F32)


def dot_t(a, b):
    return lax.dot_general(a, b, (((1,), (1,)), ((), ())), preferred_element_type=F32)


def normalize(values):
    center = values - jnp.mean(values, axis=-1, keepdims=True)
    inverse = lax.rsqrt(jnp.mean(center * center, axis=-1, keepdims=True) + 1e-05)
    return center * inverse, inverse


def silu(values):
    half = 0.5 * values
    return half * jnp.tanh(half) + half


def silu_slope(values):
    half = 0.5 * values
    two_sigma = 1.0 + jnp.tanh(half)
    return 0.5 * two_sigma * (1.0 + values - half * two_sigma)


def project_kernel(
    events_hbm, grad_hbm, w_hbm, w_outer_hbm, send, events, grad_out, weights, w_outer, parts, sems
):
    copies = [pltpu.make_async_copy(events_hbm, events, sems.at[4])]
    for part in (1, 2, 3, 0):
        cols = slice(part * D, (part + 1) * D)
        copies.append(pltpu.make_async_copy(w_hbm.at[:, cols], weights.at[part], sems.at[part]))
    copies.append(pltpu.make_async_copy(w_outer_hbm, w_outer, sems.at[5]))
    copies.append(pltpu.make_async_copy(grad_hbm, grad_out, sems.at[6]))
    for copy in copies:
        copy.start()
    leaving = []
    copies[0].wait()
    normed = normalize(events[...].astype(F32))[0].astype(BF16)
    for slot, part in enumerate((1, 2, 3, 0)):
        copies[slot + 1].wait()
        act = silu(dot(normed, weights[part])).astype(BF16)
        if part == 0:
            copies[5].wait()
            copies[6].wait()
            act = (dot_t(grad_out[...], w_outer[...]) * act.astype(F32)).astype(BF16)
        for g in range(2):
            for h in range(HEADS):
                piece = act[g * BLK : (g + 1) * BLK, h * HD : (h + 1) * HD]
                for p in range(2):
                    at = ((g * HEADS + h) * 2 + p) * BLK
                    parts[slot, at : at + BLK, :] = piece
        cols = slice(slot * HD, (slot + 1) * HD)
        leaving.append(pltpu.make_async_copy(parts.at[slot], send.at[:, cols], sems.at[7 + slot]))
        leaving[-1].start()
    for copy in leaving:
        copy.wait()


def gate_kernel(events, grad_out, w_inner, w_outer, ids, slope, normed_out, inv_out, hot, ext):
    normed, inverse = normalize(events[...].astype(F32))
    normed_out[...] = normed
    inv_out[...] = jnp.broadcast_to(inverse, inv_out.shape)
    normed = normed.astype(BF16)
    for part in range(4):
        cols = slice(part * D, (part + 1) * D)
        values = silu_slope(dot(normed, w_inner[:, cols]))
        if part == 0:
            values = values * dot_t(grad_out[...], w_outer[...])
        slope[:, cols] = values
    count = 2 * BLK
    id_row = ids[...]
    id_cols = jnp.transpose(jnp.broadcast_to(id_row.astype(F32), (BLK, count))).astype(jnp.int32)
    owner_row = id_row // ROWS_DEV
    owner_col = id_cols[:, :1] // ROWS_DEV
    earlier = lax.broadcasted_iota(jnp.int32, (count, count), 0) < lax.broadcasted_iota(
        jnp.int32, (count, count), 1
    )
    same = jnp.where((owner_col == owner_row) & earlier, 1, 0)
    rank = jnp.sum(same, axis=0, keepdims=True)
    slot = owner_row * CAP + rank
    slots = hot.shape[0]
    hot[...] = jnp.where(
        lax.broadcasted_iota(jnp.int32, (slots, count), 0) == slot, 1.0, 0.0
    ).astype(BF16)
    within = id_cols - (id_cols // ROWS_DEV) * ROWS_DEV
    high = within // 32
    lane = lax.broadcasted_iota(jnp.int32, (count, EXT), 1)
    ext[...] = (
        jnp.where(lane == 0, high + 1, jnp.where(lane == 1, within - high * 32, 0))
        .astype(F32)
        .astype(BF16)
    )


V_COLS, Q_COLS, K_COLS, G_COLS = (slice(i * HD, (i + 1) * HD) for i in range(4))


def my_place():
    p, c = lax.axis_index("p"), lax.axis_index("c")
    return p, c, 2 * p + c


def my_length(lengths):
    return lengths[lax.axis_index("y") // 2]


def inverse_of(length):
    return 1.0 / jnp.full((1, HD), length, jnp.int32).astype(F32)


def diagonal(place, core, rows_are_keys):
    row = lax.broadcasted_iota(jnp.int32, (BLK, 2 * BLK), 0) + place[2] * BLK
    lane = lax.broadcasted_iota(jnp.int32, (BLK, 2 * BLK), 1)
    col = lane + jnp.where(lane >= BLK, BLK, 0) + core * BLK
    return row <= col if rows_are_keys else col <= row


def mask_first(mask, values):
    first = jnp.where(mask, values[:BLK, :], 0.0)
    return jnp.concatenate([first, values[BLK:, :]], axis=0) if values.shape[0] > BLK else first


def mask_last(mask, values):
    last = jnp.where(mask, values[-BLK:, :], 0.0)
    return jnp.concatenate([values[:-BLK, :], last], axis=0) if values.shape[0] > BLK else last


def own_blocks(place, src, cols, dst):
    for m in range(8):
        at = pl.multiple_of((2 * m + place[0]) * BLK, BLK)
        dst[m * BLK : (m + 1) * BLK, :] = src[pl.ds(at, BLK), cols]


def forward_kernel(last, lengths, mine, *refs):
    place = my_place()
    if last:
        theirs, before, out, stats, grad, queries = refs
        keys_of, core = theirs, 1 - place[1]
        own_blocks(place, mine, G_COLS, grad)
        out[...] = before[...]
    else:
        out, queries = refs
        keys_of, core = mine, place[1]
        out[...] = jnp.zeros_like(out)
    own_blocks(place, mine, Q_COLS, queries)
    mask = diagonal(place, core, False)
    for j in range(8):
        keys = slice(j * 2 * BLK, (j + 1) * 2 * BLK)
        rows = slice(j * BLK, 8 * BLK)
        half = dot_t(queries[rows, :], keys_of[keys, K_COLS]) * (0.5 * SCALE)
        attn = half * jnp.tanh(half) + half
        attn = mask_first(mask, attn)
        out[rows, :] += dot(attn.astype(BF16), keys_of[keys, V_COLS])
    if not last:
        return
    inv_len = inverse_of(my_length(lengths))
    for m in range(8):
        rows = slice(m * BLK, (m + 1) * BLK)
        total = out[rows, :] * inv_len
        out[rows, :] = total
        g = grad[rows, :].astype(F32)
        mean = jnp.mean(total, axis=-1, keepdims=True)
        center = total - mean
        square = jnp.sum(center * center, axis=-1, keepdims=True)
        sum_g = jnp.sum(g, axis=-1, keepdims=True)
        sum_ga = jnp.sum(g * center, axis=-1, keepdims=True)
        lane = lax.broadcasted_iota(jnp.int32, (BLK, BLK), 1)
        packed = jnp.where(
            lane == 0, mean, jnp.where(lane == 1, square, jnp.where(lane == 2, sum_g, sum_ga))
        )
        stats[:, rows] = jnp.transpose(packed)[:8, :]


def grad_attn_kernel(lengths, attn_out, grad, s0, s1, s2, s3, grad_attn, normed_out):
    place = my_place()
    length = my_length(lengths)
    parts = [s0[...], s1[...], s2[...], s3[...]]
    means = [part[0:1, :] for part in parts]
    mean = 0.25 * (means[0] + means[1] + means[2] + means[3])
    square = 0.0
    sum_g = 0.0
    sum_ga = 0.0
    for part, own in zip(parts, means):
        shift = own - mean
        square = square + part[1:2, :] + HD * (shift * shift)
        sum_g = sum_g + part[2:3, :]
        sum_ga = sum_ga + part[3:4, :] + part[2:3, :] * shift
    inverse = lax.rsqrt(square * (1.0 / D) + 1e-05)
    mean_g = sum_g * (1.0 / D)
    mean_gn = inverse * sum_ga * (1.0 / D)
    row = lax.broadcasted_iota(jnp.int32, (BLK, 1024), 0)
    packed = jnp.where(
        row == 0, mean, jnp.where(row == 1, inverse, jnp.where(row == 2, mean_g, mean_gn))
    )
    for m in range(8):
        rows = slice(m * BLK, (m + 1) * BLK)
        cols = jnp.transpose(packed[:, rows])
        inv = cols[:, 1:2]
        n = (attn_out[rows, :] - cols[:, 0:1]) * inv
        back = (grad[rows, :].astype(F32) - cols[:, 2:3] - n * cols[:, 3:4]) * inv
        pos = lax.broadcasted_iota(jnp.int32, (BLK, 1), 0) + (m * 4 + place[2]) * BLK
        grad_attn[rows, :] = jnp.where(pos < length, back, 0.0).astype(BF16)
        normed_out[rows, :] = n.astype(BF16)


def slopes(raw):
    half = raw * (0.5 * SCALE)
    t = jnp.tanh(half)
    two_sigma = 1.0 + t
    return two_sigma + half * (1.0 - t * t), half * two_sigma


def grad_query_kernel(lengths, mine, theirs, grad_attn, ret, queries, total):
    place = my_place()
    total[...] = jnp.zeros_like(total)
    own_blocks(place, mine, Q_COLS, queries)
    masks = [diagonal(place, place[1], False), diagonal(place, 1 - place[1], False)]
    for j in range(8):
        keys = slice(j * 2 * BLK, (j + 1) * 2 * BLK)
        rows = slice(j * BLK, 8 * BLK)
        for src, mask in zip((mine, theirs), masks):
            k = src[keys, K_COLS]
            slope, _ = slopes(dot_t(queries[rows, :], k))
            score = slope * dot_t(grad_attn[rows, :], src[keys, V_COLS])
            total[rows, :] += dot(mask_first(mask, score).astype(BF16), k)
    inv_len = inverse_of(my_length(lengths))
    ret[...] = (total[...] * (0.5 * SCALE * inv_len)).astype(BF16)


def packed_rows(j):
    return slice(j * (j + 1) // 2 * BLK, (j + 1) * (j + 2) // 2 * BLK)


def key_scores_kernel(other, mine, *refs):
    place = my_place()
    if other:
        src, slope_out, attn_out, keys = refs
        core = 1 - place[1]
    else:
        slope_out, attn_out, keys = refs
        src, core = mine, place[1]
    own_blocks(place, mine, K_COLS, keys)
    mask = diagonal(place, core, True)
    for j in range(8):
        events = slice(j * 2 * BLK, (j + 1) * 2 * BLK)
        rows = slice(0, (j + 1) * BLK)
        slope, attn = slopes(dot_t(keys[rows, :], src[events, Q_COLS]))
        slope_out[packed_rows(j), :] = mask_last(mask, slope)
        attn_out[packed_rows(j), :] = mask_last(mask, attn).astype(BF16)


def grad_key_kernel(last, lengths, mine, *refs):
    place = my_place()
    p = place[0]
    if last:
        theirs, slope, attn, g_here, g_there, k_before, v_before, normed_out, grad_q, *refs = refs
        ret, src_g, values, grad_k, grad_v = refs
        src = theirs
        grad_k[...] = k_before[...]
        grad_v[...] = v_before[...]
    else:
        slope, attn, g_here, g_there, grad_k, grad_v, src_g, values = refs
        src = mine
        grad_k[...] = jnp.zeros_like(grad_k)
        grad_v[...] = jnp.zeros_like(grad_v)
    own_blocks(place, mine, V_COLS, values)
    for m in range(8):
        rows = slice(m * BLK, (m + 1) * BLK)
        src_g[pl.ds(pl.multiple_of((2 * m + p) * BLK, BLK), BLK), :] = g_here[rows, :]
        src_g[pl.ds(pl.multiple_of((2 * m + 1 - p) * BLK, BLK), BLK), :] = g_there[rows, :]
    for j in range(8):
        events = slice(j * 2 * BLK, (j + 1) * 2 * BLK)
        rows = slice(0, (j + 1) * BLK)
        ga = src_g[events, :]
        score = slope[packed_rows(j), :] * dot_t(values[rows, :], ga)
        grad_k[rows, :] += dot(score.astype(BF16), src[events, Q_COLS])
        grad_v[rows, :] += dot(attn[packed_rows(j), :], ga)
    if last:
        inv_len = inverse_of(my_length(lengths))
        ret[:, :HD] = normed_out[...]
        ret[:, HD : 2 * HD] = (grad_v[...] * inv_len).astype(BF16)
        ret[:, 2 * HD : 3 * HD] = grad_q[...]
        ret[:, 3 * HD :] = (grad_k[...] * (0.5 * SCALE * inv_len)).astype(BF16)


def finish_kernel(
    lengths, ret, slope, normed, inverse, grad_out, w_inner, hot, ext, send, grads
):
    for g in range(2):
        rows = slice(g * BLK, (g + 1) * BLK)
        for h in range(HEADS):
            at = slice((g * HEADS + h) * BLK, (g * HEADS + h + 1) * BLK)
            for part in range(4):
                cols = slice(part * D + h * HD, part * D + (h + 1) * HD)
                grad = ret[at, part * HD : (part + 1) * HD].astype(F32)
                grads[rows, cols] = (grad * slope[rows, cols]).astype(BF16)
    grad_normed = dot_t(grads[...], w_inner[...])
    back = inverse[:, :1] * (
        grad_normed
        - jnp.mean(grad_normed, axis=-1, keepdims=True)
        - normed[...] * jnp.mean(grad_normed * normed[...], axis=-1, keepdims=True)
    )
    total = grad_out[...].astype(F32) + back
    chip = (lax.axis_index("y") * 2 + lax.axis_index("w")) * 2 + lax.axis_index("p")
    first = (chip * 2 + lax.axis_index("c")) * BLK
    row = lax.broadcasted_iota(jnp.int32, (2 * BLK, 1), 0)
    second = row >= BLK
    pos = first + jnp.where(second, row - BLK, row)
    total = jnp.where(pos < jnp.where(second, lengths[1], lengths[0]), total, 0.0)
    send[:, :D] = dot(hot[...], total.astype(BF16)).astype(BF16)
    send[:, D:] = dot(hot[...], ext[...]).astype(BF16)


def table_kernel(got, table, stage, sems):
    packed = jnp.transpose(got[:, D:].astype(F32))
    dest = ((packed[0:1, :] - 1.0) * 32.0 + packed[1:2, :]).astype(jnp.int32)
    leaving = []
    for i in range(ROWS_DEV // BLK):
        rows = slice(i * BLK, (i + 1) * BLK)
        row = lax.broadcasted_iota(jnp.int32, (BLK, got.shape[0]), 0) + i * BLK
        hot = jnp.where(row == dest, 1.0, 0.0).astype(BF16)
        stage[rows, :] = dot(hot, got[:, :D])
        leaving.append(pltpu.make_async_copy(stage.at[rows], table.at[rows], sems.at[i]))
        leaving[-1].start()
    for copy in leaving:
        copy.wait()


def call(kernel, outs, args, scalars=1, scratch=(), flops=0):
    vmem = pl.BlockSpec(memory_space=pltpu.VMEM)
    smem = pl.BlockSpec(memory_space=pltpu.SMEM)
    return pl.pallas_call(
        kernel,
        out_shape=[jax.ShapeDtypeStruct(shape, dtype) for shape, dtype in outs],
        in_specs=[smem] * scalars + [vmem] * (len(args) - scalars),
        out_specs=[vmem] * len(outs),
        scratch_shapes=[pltpu.VMEM(shape, dtype) for shape, dtype in scratch],
        compiler_params=pltpu.CompilerParams(vmem_limit_bytes=VMEM_LIMIT),
        cost_estimate=pl.CostEstimate(flops=flops, bytes_accessed=2**20, transcendentals=0),
    )(*args)


def project(*args):
    hbm = pl.BlockSpec(memory_space=pltpu.HBM)
    return pl.pallas_call(
        project_kernel,
        out_shape=jax.ShapeDtypeStruct((16 * BLK, 4 * HD), BF16),
        in_specs=[hbm] * len(args),
        out_specs=hbm,
        scratch_shapes=[
            pltpu.VMEM((2 * BLK, D), BF16),
            pltpu.VMEM((2 * BLK, D), BF16),
            pltpu.VMEM((4, D, D), BF16),
            pltpu.VMEM((D, D), BF16),
            pltpu.VMEM((4, 16 * BLK, HD), BF16),
            pltpu.SemaphoreType.DMA((11,)),
        ],
        compiler_params=pltpu.CompilerParams(vmem_limit_bytes=PROJECT_LIMIT),
    )(*args)


def local(events, grad_out, w_inner, w_outer, valid_lengths, item_ids):
    events = events.reshape(2 * BLK, D)
    grad_out = grad_out.reshape(2 * BLK, D)
    rows_bf16, rows_f32 = ((1024, HD), BF16), ((1024, HD), F32)
    swap_c = [(0, 1), (1, 0)]
    send = project(events, grad_out, w_inner, w_outer)
    mine = lax.all_to_all(send, ("y", "w", "p"), 0, 0, tiled=True)
    slope, normed, inverse, hot, ext = call(
        gate_kernel,
        [
            ((2 * BLK, 4 * D), F32),
            ((2 * BLK, D), F32),
            ((2 * BLK, HD), F32),
            ((CAP * 128, 2 * BLK), BF16),
            ((2 * BLK, EXT), BF16),
        ],
        (events, grad_out, w_inner, w_outer, item_ids.reshape(1, 2 * BLK)),
        scalars=0,
        flops=2 * 10**9,
    )
    mine, slope = lax.optimization_barrier((mine, slope))
    theirs = lax.ppermute(mine, "c", swap_c)
    (attn_one,) = call(
        functools.partial(forward_kernel, False),
        [rows_f32],
        (valid_lengths, mine),
        scratch=[rows_bf16],
        flops=10**9,
    )
    score_shapes = [((36 * BLK, 2 * BLK), F32), ((36 * BLK, 2 * BLK), BF16)]
    scores_m = call(
        functools.partial(key_scores_kernel, False),
        score_shapes,
        (mine,),
        scalars=0,
        scratch=[rows_bf16],
        flops=10**9,
    )
    theirs, scores_m, attn_one = lax.optimization_barrier((theirs, scores_m, attn_one))
    attn_out, stats, grad = call(
        functools.partial(forward_kernel, True),
        [rows_f32, ((8, 1024), F32), rows_bf16],
        (valid_lengths, mine, theirs, attn_one),
        scratch=[rows_bf16],
        flops=10**9,
    )
    others = [
        lax.ppermute(stats, ("y", "w"), [(i, i ^ m) for i in range(8)]) for m in (1, 2, 3)
    ]
    scores_t = call(
        functools.partial(key_scores_kernel, True),
        score_shapes,
        (mine, theirs),
        scalars=0,
        scratch=[rows_bf16],
        flops=10**9,
    )
    others, scores_t = lax.optimization_barrier((others, scores_t))
    grad_attn, normed_out = call(
        grad_attn_kernel,
        [rows_bf16, rows_bf16],
        (valid_lengths, attn_out, grad, stats, *others),
        flops=10**7,
    )
    grad_p, grad_c = [
        lax.ppermute(grad_attn, ("p", "c"), [(i, i ^ m) for i in range(4)]) for m in (2, 1)
    ]
    (grad_q,) = call(
        grad_query_kernel,
        [rows_bf16],
        (valid_lengths, mine, theirs, grad_attn),
        scratch=[rows_bf16, rows_f32],
        flops=4 * 10**9,
    )
    grad_p, grad_q = lax.optimization_barrier((grad_p, grad_q))
    grad_pc = lax.ppermute(grad_p, "c", swap_c)
    grad_k, grad_v = call(
        functools.partial(grad_key_kernel, False),
        [rows_f32, rows_f32],
        (valid_lengths, mine, *scores_m, grad_attn, grad_p),
        scratch=[((2048, HD), BF16), rows_bf16],
        flops=3 * 10**9,
    )
    (ret,) = call(
        functools.partial(grad_key_kernel, True),
        [((1024, 4 * HD), BF16)],
        (
            valid_lengths,
            mine,
            theirs,
            *scores_t,
            grad_c,
            grad_pc,
            grad_k,
            grad_v,
            normed_out,
            grad_q,
        ),
        scratch=[((2048, HD), BF16), rows_bf16, rows_f32, rows_f32],
        flops=3 * 10**9,
    )
    got = lax.all_to_all(ret, ("y", "w"), 0, 0, tiled=True)
    (rows,) = call(
        finish_kernel,
        [((CAP * 128, D + EXT), BF16)],
        (valid_lengths, got, slope, normed, inverse, grad_out, w_inner, hot, ext),
        scratch=[((2 * BLK, 4 * D), BF16)],
        flops=10**9,
    )
    got = lax.all_to_all(
        rows.reshape(128, CAP, D + EXT), ("y", "w", "p", "c", "row"), 0, 0, tiled=True
    ).reshape(128 * CAP, D + EXT)
    return pl.pallas_call(
        table_kernel,
        out_shape=jax.ShapeDtypeStruct((ROWS_DEV, D), F32),
        in_specs=[pl.BlockSpec(memory_space=pltpu.VMEM)],
        out_specs=pl.BlockSpec(memory_space=pltpu.HBM),
        scratch_shapes=[pltpu.VMEM((ROWS_DEV, D), F32), pltpu.SemaphoreType.DMA((8,))],
        compiler_params=pltpu.CompilerParams(vmem_limit_bytes=VMEM_LIMIT),
    )(got)


def solution(mesh):
    fine = Mesh(mesh.devices.reshape(4, 2, 2, 2, 4), ("y", "w", "p", "c", "row"))
    seq = ("y", "w", "p", "c")
    return jax.shard_map(
        local,
        mesh=fine,
        in_specs=(
            P("row", seq, None),
            P("row", seq, None),
            P(),
            P(),
            P("row"),
            P("row", seq),
        ),
        out_specs=P(seq + ("row",), None),
        check_vma=False,
    )
```

```python
import functools

import jax
import jax.numpy as jnp
from jax import lax
from jax.experimental import pallas as pl
from jax.experimental.pallas import tpu as pltpu
from jax.sharding import Mesh
from jax.sharding import PartitionSpec as P

HEADS = 4
ROWS_DEV = 1024
D = 512
HD = 128
BLK = 128
CAP = 4
EXT = 128
F32 = jnp.float32
BF16 = jnp.bfloat16
SCALE = HD**-0.5
VMEM_LIMIT = 12 * 2**20
PROJECT_LIMIT = 60 * 2**20


def dot(a, b):
    return lax.dot_general(a, b, (((1,), (0,)), ((), ())), preferred_element_type=F32)


def dot_t(a, b):
    return lax.dot_general(a, b, (((1,), (1,)), ((), ())), preferred_element_type=F32)


def normalize(values):
    center = values - jnp.mean(values, axis=-1, keepdims=True)
    inverse = lax.rsqrt(jnp.mean(center * center, axis=-1, keepdims=True) + 1e-05)
    return center * inverse, inverse


def silu(values):
    half = 0.5 * values
    return half * jnp.tanh(half) + half


def silu_slope(values):
    half = 0.5 * values
    two_sigma = 1.0 + jnp.tanh(half)
    return 0.5 * two_sigma * (1.0 + values - half * two_sigma)


def project_kernel(
    events_hbm, grad_hbm, w_hbm, w_outer_hbm, send, events, grad_out, weights, w_outer, parts, sems
):
    copies = [pltpu.make_async_copy(events_hbm, events, sems.at[4])]
    for part in (1, 2, 3, 0):
        cols = slice(part * D, (part + 1) * D)
        copies.append(pltpu.make_async_copy(w_hbm.at[:, cols], weights.at[part], sems.at[part]))
    copies.append(pltpu.make_async_copy(w_outer_hbm, w_outer, sems.at[5]))
    copies.append(pltpu.make_async_copy(grad_hbm, grad_out, sems.at[6]))
    for copy in copies:
        copy.start()
    leaving = []
    copies[0].wait()
    normed = normalize(events[...].astype(F32))[0].astype(BF16)
    for slot, part in enumerate((1, 2, 3, 0)):
        copies[slot + 1].wait()
        act = silu(dot(normed, weights[part])).astype(BF16)
        if part == 0:
            copies[5].wait()
            copies[6].wait()
            act = (dot_t(grad_out[...], w_outer[...]) * act.astype(F32)).astype(BF16)
        for g in range(2):
            for h in range(HEADS):
                piece = act[g * BLK : (g + 1) * BLK, h * HD : (h + 1) * HD]
                for p in range(2):
                    at = (p * 8 + g * HEADS + h) * BLK
                    parts[slot, at : at + BLK, :] = piece
        cols = slice(slot * HD, (slot + 1) * HD)
        leaving.append(pltpu.make_async_copy(parts.at[slot], send.at[:, cols], sems.at[7 + slot]))
        leaving[-1].start()
    for copy in leaving:
        copy.wait()


def gate_kernel(events, grad_out, w_inner, w_outer, ids, slope, normed_out, inv_out, hot, ext):
    normed, inverse = normalize(events[...].astype(F32))
    normed_out[...] = normed
    inv_out[...] = jnp.broadcast_to(inverse, inv_out.shape)
    normed = normed.astype(BF16)
    for part in range(4):
        cols = slice(part * D, (part + 1) * D)
        values = silu_slope(dot(normed, w_inner[:, cols]))
        if part == 0:
            values = values * dot_t(grad_out[...], w_outer[...])
        slope[:, cols] = values
    count = 2 * BLK
    id_row = ids[...]
    id_cols = jnp.transpose(jnp.broadcast_to(id_row.astype(F32), (BLK, count))).astype(jnp.int32)
    owner_row = id_row // ROWS_DEV
    owner_col = id_cols[:, :1] // ROWS_DEV
    earlier = lax.broadcasted_iota(jnp.int32, (count, count), 0) < lax.broadcasted_iota(
        jnp.int32, (count, count), 1
    )
    same = jnp.where((owner_col == owner_row) & earlier, 1, 0)
    rank = jnp.sum(same, axis=0, keepdims=True)
    dest = (owner_row // 4 % 2) * 64 + owner_row // 8 * 4 + owner_row % 4
    slot = dest * CAP + rank
    slots = hot.shape[0]
    hot[...] = jnp.where(
        lax.broadcasted_iota(jnp.int32, (slots, count), 0) == slot, 1.0, 0.0
    ).astype(BF16)
    within = id_cols - (id_cols // ROWS_DEV) * ROWS_DEV
    high = within // 32
    lane = lax.broadcasted_iota(jnp.int32, (count, EXT), 1)
    ext[...] = (
        jnp.where(lane == 0, high + 1, jnp.where(lane == 1, within - high * 32, 0))
        .astype(F32)
        .astype(BF16)
    )


V_COLS, Q_COLS, K_COLS, G_COLS = (slice(i * HD, (i + 1) * HD) for i in range(4))
GRP = 2 * BLK


def my_place():
    return lax.axis_index("p"), lax.axis_index("c")


def my_length(lengths):
    return lengths[lax.axis_index("y") // 2]


def inverse_of(length):
    return 1.0 / jnp.full((1, HD), length, jnp.int32).astype(F32)


def at_rows(p, start, count):
    return pl.ds(pl.multiple_of(p * 1024 + start, GRP), count)


def diagonal(row_place, col_place, rows_are_keys):
    def start(place):
        return (4 * place[0] + place[1]) * BLK

    row = lax.broadcasted_iota(jnp.int32, (GRP, GRP), 0)
    col = lax.broadcasted_iota(jnp.int32, (GRP, GRP), 1)
    row = jnp.where(row >= BLK, row + BLK, row) + start(row_place)
    col = jnp.where(col >= BLK, col + BLK, col) + start(col_place)
    return row <= col if rows_are_keys else col <= row


def mask_first(mask, values):
    first = jnp.where(mask, values[:GRP, :], 0.0)
    return jnp.concatenate([first, values[GRP:, :]], axis=0) if values.shape[0] > GRP else first


def mask_last(mask, values):
    last = jnp.where(mask, values[-GRP:, :], 0.0)
    return jnp.concatenate([values[:-GRP, :], last], axis=0) if values.shape[0] > GRP else last


def query_rows(y, part):
    start = (y * (9 - y) + part * (4 - y)) * GRP
    return slice(start, start + (4 - y) * GRP)


def forward_kernel(last, lengths, mine, *refs):
    place = my_place()
    p = place[0]
    if last:
        theirs, before, out, slope_out, stats, grad = refs
        keys_of, core = theirs, 1 - place[1]
        grad[...] = mine[at_rows(p, 0, 1024), G_COLS]
        out[...] = before[...]
    else:
        out, slope_out = refs
        keys_of, core = mine, place[1]
        out[...] = jnp.zeros_like(out)
    for y in range(4):
        rows = slice(y * GRP, 1024)
        queries = mine[at_rows(p, y * GRP, 1024 - y * GRP), Q_COLS]
        for part in range(2):
            keys = slice(part * 1024 + y * GRP, part * 1024 + (y + 1) * GRP)
            slope, attn = slopes(dot_t(queries, keys_of[keys, K_COLS]))
            mask = diagonal(place, (part, core), False)
            slope_out[query_rows(y, part), :] = mask_first(mask, slope)
            attn = mask_first(mask, attn)
            out[rows, :] += dot(attn.astype(BF16), keys_of[keys, V_COLS])
    if not last:
        return
    inv_len = inverse_of(my_length(lengths))
    for m in range(8):
        rows = slice(m * BLK, (m + 1) * BLK)
        total = out[rows, :] * inv_len
        out[rows, :] = total
        g = grad[rows, :].astype(F32)
        mean = jnp.mean(total, axis=-1, keepdims=True)
        center = total - mean
        square = jnp.sum(center * center, axis=-1, keepdims=True)
        sum_g = jnp.sum(g, axis=-1, keepdims=True)
        sum_ga = jnp.sum(g * center, axis=-1, keepdims=True)
        lane = lax.broadcasted_iota(jnp.int32, (BLK, BLK), 1)
        packed = jnp.where(
            lane == 0, mean, jnp.where(lane == 1, square, jnp.where(lane == 2, sum_g, sum_ga))
        )
        stats[:, rows] = jnp.transpose(packed)[:8, :]


def grad_attn_kernel(lengths, attn_out, grad, s0, s1, s2, s3, grad_attn, normed_out):
    p, c = my_place()
    length = my_length(lengths)
    parts = [s0[...], s1[...], s2[...], s3[...]]
    means = [part[0:1, :] for part in parts]
    mean = 0.25 * (means[0] + means[1] + means[2] + means[3])
    square = 0.0
    sum_g = 0.0
    sum_ga = 0.0
    for part, own in zip(parts, means):
        shift = own - mean
        square = square + part[1:2, :] + HD * (shift * shift)
        sum_g = sum_g + part[2:3, :]
        sum_ga = sum_ga + part[3:4, :] + part[2:3, :] * shift
    inverse = lax.rsqrt(square * (1.0 / D) + 1e-05)
    mean_g = sum_g * (1.0 / D)
    mean_gn = inverse * sum_ga * (1.0 / D)
    row = lax.broadcasted_iota(jnp.int32, (BLK, 1024), 0)
    packed = jnp.where(
        row == 0, mean, jnp.where(row == 1, inverse, jnp.where(row == 2, mean_g, mean_gn))
    )
    for m in range(8):
        rows = slice(m * BLK, (m + 1) * BLK)
        cols = jnp.transpose(packed[:, rows])
        inv = cols[:, 1:2]
        n = (attn_out[rows, :] - cols[:, 0:1]) * inv
        back = (grad[rows, :].astype(F32) - cols[:, 2:3] - n * cols[:, 3:4]) * inv
        pos = lax.broadcasted_iota(jnp.int32, (BLK, 1), 0)
        pos = pos + (m // 2 * 8 + 4 * p + m % 2 * 2 + c) * BLK
        grad_attn[rows, :] = jnp.where(pos < length, back, 0.0).astype(BF16)
        normed_out[rows, :] = n.astype(BF16)


def slopes(raw):
    half = raw * (0.5 * SCALE)
    t = jnp.tanh(half)
    two_sigma = 1.0 + t
    return two_sigma + half * (1.0 - t * t), half * two_sigma


def grad_query_kernel(lengths, mine, theirs, slope_m, slope_t, grad_attn, ret, total):
    total[...] = jnp.zeros_like(total)
    for y in range(4):
        rows = slice(y * GRP, 1024)
        for part in range(2):
            keys = slice(part * 1024 + y * GRP, part * 1024 + (y + 1) * GRP)
            for src, slope in ((mine, slope_m), (theirs, slope_t)):
                score = slope[query_rows(y, part), :] * dot_t(grad_attn[rows, :], src[keys, V_COLS])
                total[rows, :] += dot(score.astype(BF16), src[keys, K_COLS])
    inv_len = inverse_of(my_length(lengths))
    ret[...] = (total[...] * (0.5 * SCALE * inv_len)).astype(BF16)


PACKED = 20 * GRP


def packed_rows(y, other):
    start = (y + 1) * (y + other) * GRP
    return slice(start, start + (y + 1) * GRP)


def key_scores_kernel(theirs_too, mine, *refs):
    place = my_place()
    p = place[0]
    if theirs_too:
        src, slope_out, attn_out = refs
        core = 1 - place[1]
    else:
        slope_out, attn_out = refs
        src, core = mine, place[1]
    for y in range(4):
        count = (y + 1) * GRP
        keys = mine[at_rows(p, 0, count), K_COLS]
        for other in range(2):
            part = 1 - p if other else p
            slope, attn = slopes(dot_t(keys, src[at_rows(part, y * GRP, GRP), Q_COLS]))
            mask = diagonal(place, (part, core), True)
            rows = packed_rows(y, other)
            slope_out[rows, :] = mask_last(mask, slope)
            attn_out[rows, :] = mask_last(mask, attn).astype(BF16)


def grad_key_kernel(last, lengths, mine, *refs):
    p = lax.axis_index("p")
    if last:
        theirs, slope, attn, g_here, g_there, k_before, v_before, normed_out, grad_q, *refs = refs
        ret, grad_k, grad_v = refs
        src = theirs
        grad_k[...] = k_before[...]
        grad_v[...] = v_before[...]
    else:
        slope, attn, g_here, g_there, grad_k, grad_v = refs
        src = mine
        grad_k[...] = jnp.zeros_like(grad_k)
        grad_v[...] = jnp.zeros_like(grad_v)
    for y in range(4):
        count = (y + 1) * GRP
        rows = slice(0, count)
        values = mine[at_rows(p, 0, count), V_COLS]
        for other, grad_attn in enumerate((g_here, g_there)):
            ga = grad_attn[y * GRP : (y + 1) * GRP, :]
            q = src[at_rows(1 - p if other else p, y * GRP, GRP), Q_COLS]
            packed = packed_rows(y, other)
            score = slope[packed, :] * dot_t(values, ga)
            grad_k[rows, :] += dot(score.astype(BF16), q)
            grad_v[rows, :] += dot(attn[packed, :], ga)
    if last:
        inv_len = inverse_of(my_length(lengths))
        ret[:, :HD] = normed_out[...]
        ret[:, HD : 2 * HD] = (grad_v[...] * inv_len).astype(BF16)
        ret[:, 2 * HD : 3 * HD] = grad_q[...]
        ret[:, 3 * HD :] = (grad_k[...] * (0.5 * SCALE * inv_len)).astype(BF16)


def finish_kernel(
    lengths, ret, slope, normed, inverse, grad_out, w_inner, hot, ext, send, grads
):
    for g in range(2):
        rows = slice(g * BLK, (g + 1) * BLK)
        for h in range(HEADS):
            at = slice((g * HEADS + h) * BLK, (g * HEADS + h + 1) * BLK)
            for part in range(4):
                cols = slice(part * D + h * HD, part * D + (h + 1) * HD)
                grad = ret[at, part * HD : (part + 1) * HD].astype(F32)
                grads[rows, cols] = (grad * slope[rows, cols]).astype(BF16)
    grad_normed = dot_t(grads[...], w_inner[...])
    back = inverse[:, :1] * (
        grad_normed
        - jnp.mean(grad_normed, axis=-1, keepdims=True)
        - normed[...] * jnp.mean(grad_normed * normed[...], axis=-1, keepdims=True)
    )
    total = grad_out[...].astype(F32) + back
    chip = (lax.axis_index("y") * 2 + lax.axis_index("p")) * 2 + lax.axis_index("w")
    first = (chip * 2 + lax.axis_index("c")) * BLK
    row = lax.broadcasted_iota(jnp.int32, (2 * BLK, 1), 0)
    second = row >= BLK
    pos = first + jnp.where(second, row - BLK, row)
    total = jnp.where(pos < jnp.where(second, lengths[1], lengths[0]), total, 0.0)
    send[:, :D] = dot(hot[...], total.astype(BF16)).astype(BF16)
    send[:, D:] = dot(hot[...], ext[...]).astype(BF16)


def table_kernel(got, table, stage, sems):
    packed = jnp.transpose(got[:, D:].astype(F32))
    dest = ((packed[0:1, :] - 1.0) * 32.0 + packed[1:2, :]).astype(jnp.int32)
    leaving = []
    for i in range(ROWS_DEV // BLK):
        rows = slice(i * BLK, (i + 1) * BLK)
        row = lax.broadcasted_iota(jnp.int32, (BLK, got.shape[0]), 0) + i * BLK
        hot = jnp.where(row == dest, 1.0, 0.0).astype(BF16)
        stage[rows, :] = dot(hot, got[:, :D])
        leaving.append(pltpu.make_async_copy(stage.at[rows], table.at[rows], sems.at[i]))
        leaving[-1].start()
    for copy in leaving:
        copy.wait()


def call(kernel, outs, args, scalars=1, scratch=(), flops=0):
    vmem = pl.BlockSpec(memory_space=pltpu.VMEM)
    smem = pl.BlockSpec(memory_space=pltpu.SMEM)
    return pl.pallas_call(
        kernel,
        out_shape=[jax.ShapeDtypeStruct(shape, dtype) for shape, dtype in outs],
        in_specs=[smem] * scalars + [vmem] * (len(args) - scalars),
        out_specs=[vmem] * len(outs),
        scratch_shapes=[pltpu.VMEM(shape, dtype) for shape, dtype in scratch],
        compiler_params=pltpu.CompilerParams(vmem_limit_bytes=VMEM_LIMIT),
        cost_estimate=pl.CostEstimate(flops=flops, bytes_accessed=2**20, transcendentals=0),
    )(*args)


def project(*args):
    hbm = pl.BlockSpec(memory_space=pltpu.HBM)
    return pl.pallas_call(
        project_kernel,
        out_shape=jax.ShapeDtypeStruct((16 * BLK, 4 * HD), BF16),
        in_specs=[hbm] * len(args),
        out_specs=hbm,
        scratch_shapes=[
            pltpu.VMEM((2 * BLK, D), BF16),
            pltpu.VMEM((2 * BLK, D), BF16),
            pltpu.VMEM((4, D, D), BF16),
            pltpu.VMEM((D, D), BF16),
            pltpu.VMEM((4, 16 * BLK, HD), BF16),
            pltpu.SemaphoreType.DMA((11,)),
        ],
        compiler_params=pltpu.CompilerParams(vmem_limit_bytes=PROJECT_LIMIT),
    )(*args)


def local(events, grad_out, w_inner, w_outer, valid_lengths, item_ids):
    events = events.reshape(2 * BLK, D)
    grad_out = grad_out.reshape(2 * BLK, D)
    rows_bf16, rows_f32 = ((1024, HD), BF16), ((1024, HD), F32)
    swap_c = [(0, 1), (1, 0)]
    send = project(events, grad_out, w_inner, w_outer)
    mine = lax.all_to_all(send, ("p", "y", "w"), 0, 0, tiled=True)
    slope, normed, inverse, hot, ext = call(
        gate_kernel,
        [
            ((2 * BLK, 4 * D), F32),
            ((2 * BLK, D), F32),
            ((2 * BLK, HD), F32),
            ((CAP * 128, 2 * BLK), BF16),
            ((2 * BLK, EXT), BF16),
        ],
        (events, grad_out, w_inner, w_outer, item_ids.reshape(1, 2 * BLK)),
        scalars=0,
        flops=2 * 10**9,
    )
    mine, slope = lax.optimization_barrier((mine, slope))
    theirs = lax.ppermute(mine, "c", swap_c)
    score_shapes = [((PACKED, GRP), F32), ((PACKED, GRP), BF16)]
    attn_one, slope_m = call(
        functools.partial(forward_kernel, False),
        [rows_f32, score_shapes[0]],
        (valid_lengths, mine),
        flops=10**9,
    )
    attn_out, slope_t, stats, grad = call(
        functools.partial(forward_kernel, True),
        [rows_f32, score_shapes[0], ((8, 1024), F32), rows_bf16],
        (valid_lengths, mine, theirs, attn_one),
        flops=10**9,
    )
    others = [
        lax.ppermute(stats, ("y", "w"), [(i, i ^ m) for i in range(8)]) for m in (1, 2, 3)
    ]
    scores_t = call(
        functools.partial(key_scores_kernel, True),
        score_shapes,
        (mine, theirs),
        scalars=0,
        flops=10**9,
    )
    others, scores_t = lax.optimization_barrier((others, scores_t))
    grad_attn, normed_out = call(
        grad_attn_kernel,
        [rows_bf16, rows_bf16],
        (valid_lengths, attn_out, grad, stats, *others),
        flops=10**7,
    )
    grad_p, grad_c = [
        lax.ppermute(grad_attn, ("p", "c"), [(i, i ^ m) for i in range(4)]) for m in (2, 1)
    ]
    mine_late, grad_attn = lax.optimization_barrier((mine, grad_attn))
    scores_m = call(
        functools.partial(key_scores_kernel, False),
        score_shapes,
        (mine_late,),
        scalars=0,
        flops=10**9,
    )
    (grad_q,) = call(
        grad_query_kernel,
        [rows_bf16],
        (valid_lengths, mine, theirs, slope_m, slope_t, grad_attn),
        scratch=[rows_f32],
        flops=4 * 10**9,
    )
    grad_p, grad_q, scores_m = lax.optimization_barrier((grad_p, grad_q, scores_m))
    grad_pc = lax.ppermute(grad_p, "c", swap_c)
    grad_k, grad_v = call(
        functools.partial(grad_key_kernel, False),
        [rows_f32, rows_f32],
        (valid_lengths, mine, *scores_m, grad_attn, grad_p),
        flops=3 * 10**9,
    )
    (ret,) = call(
        functools.partial(grad_key_kernel, True),
        [((1024, 4 * HD), BF16)],
        (
            valid_lengths,
            mine,
            theirs,
            *scores_t,
            grad_c,
            grad_pc,
            grad_k,
            grad_v,
            normed_out,
            grad_q,
        ),
        scratch=[rows_f32, rows_f32],
        flops=3 * 10**9,
    )
    got = lax.all_to_all(ret, ("y", "w"), 0, 0, tiled=True)
    (rows,) = call(
        finish_kernel,
        [((CAP * 128, D + EXT), BF16)],
        (valid_lengths, got, slope, normed, inverse, grad_out, w_inner, hot, ext),
        scratch=[((2 * BLK, 4 * D), BF16)],
        flops=10**9,
    )
    got = lax.all_to_all(
        rows.reshape(128, CAP, D + EXT), ("c", "y", "p", "w", "row"), 0, 0, tiled=True
    ).reshape(128 * CAP, D + EXT)
    return pl.pallas_call(
        table_kernel,
        out_shape=jax.ShapeDtypeStruct((ROWS_DEV, D), F32),
        in_specs=[pl.BlockSpec(memory_space=pltpu.VMEM)],
        out_specs=pl.BlockSpec(memory_space=pltpu.HBM),
        scratch_shapes=[pltpu.VMEM((ROWS_DEV, D), F32), pltpu.SemaphoreType.DMA((8,))],
        compiler_params=pltpu.CompilerParams(vmem_limit_bytes=VMEM_LIMIT),
    )(got)


def solution(mesh):
    fine = Mesh(mesh.devices.reshape(4, 2, 2, 2, 4), ("y", "p", "w", "c", "row"))
    seq = ("y", "p", "w", "c")
    return jax.shard_map(
        local,
        mesh=fine,
        in_specs=(
            P("row", seq, None),
            P("row", seq, None),
            P(),
            P(),
            P("row"),
            P("row", seq),
        ),
        out_specs=P(seq + ("row",), None),
        check_vma=False,
    )
```

```python
import functools

import jax
import jax.numpy as jnp
from jax import lax
from jax.experimental import pallas as pl
from jax.experimental.pallas import tpu as pltpu
from jax.sharding import Mesh
from jax.sharding import PartitionSpec as P

HEADS = 4
ROWS_DEV = 1024
D = 512
HD = 128
BLK = 128
CAP = 4
EXT = 128
F32 = jnp.float32
BF16 = jnp.bfloat16
SCALE = HD**-0.5
VMEM_LIMIT = 12 * 2**20
PROJECT_LIMIT = 60 * 2**20


def dot(a, b):
    return lax.dot_general(a, b, (((1,), (0,)), ((), ())), preferred_element_type=F32)


def dot_t(a, b):
    return lax.dot_general(a, b, (((1,), (1,)), ((), ())), preferred_element_type=F32)


def normalize(values):
    center = values - jnp.mean(values, axis=-1, keepdims=True)
    inverse = lax.rsqrt(jnp.mean(center * center, axis=-1, keepdims=True) + 1e-05)
    return center * inverse, inverse


def silu(values):
    half = 0.5 * values
    return half * jnp.tanh(half) + half


def silu_slope(values):
    half = 0.5 * values
    two_sigma = 1.0 + jnp.tanh(half)
    return 0.5 * two_sigma * (1.0 + values - half * two_sigma)


def project_kernel(
    events_hbm, grad_hbm, w_hbm, w_outer_hbm, send, events, grad_out, weights, w_outer, parts, sems
):
    copies = [pltpu.make_async_copy(events_hbm, events, sems.at[4])]
    for part in (1, 3, 2, 0):
        cols = slice(part * D, (part + 1) * D)
        copies.append(pltpu.make_async_copy(w_hbm.at[:, cols], weights.at[part], sems.at[part]))
    copies.append(pltpu.make_async_copy(w_outer_hbm, w_outer, sems.at[5]))
    copies.append(pltpu.make_async_copy(grad_hbm, grad_out, sems.at[6]))
    for copy in copies:
        copy.start()
    leaving = []
    copies[0].wait()
    normed = normalize(events[...].astype(F32))[0].astype(BF16)
    for slot, part in enumerate((1, 3, 2, 0)):
        copies[slot + 1].wait()
        act = silu(dot(normed, weights[part])).astype(BF16)
        if part == 0:
            copies[5].wait()
            copies[6].wait()
            act = (dot_t(grad_out[...], w_outer[...]) * act.astype(F32)).astype(BF16)
        for g in range(2):
            for h in range(HEADS):
                piece = act[g * BLK : (g + 1) * BLK, h * HD : (h + 1) * HD]
                at = (g * HEADS + h) * BLK
                parts[slot, at : at + BLK, :] = piece
        cols = slice(slot * HD, (slot + 1) * HD)
        leaving.append(pltpu.make_async_copy(parts.at[slot], send.at[:, cols], sems.at[7 + slot]))
        leaving[-1].start()
    for copy in leaving:
        copy.wait()


def gate_kernel(events, grad_out, w_inner, w_outer, ids, slope, normed_out, inv_out, hot, ext):
    normed, inverse = normalize(events[...].astype(F32))
    normed_out[...] = normed
    inv_out[...] = jnp.broadcast_to(inverse, inv_out.shape)
    normed = normed.astype(BF16)
    for part in range(4):
        cols = slice(part * D, (part + 1) * D)
        values = silu_slope(dot(normed, w_inner[:, cols]))
        if part == 0:
            values = values * dot_t(grad_out[...], w_outer[...])
        slope[:, cols] = values
    count = 2 * BLK
    id_row = ids[...]
    id_cols = jnp.transpose(jnp.broadcast_to(id_row.astype(F32), (BLK, count))).astype(jnp.int32)
    owner_row = id_row // ROWS_DEV
    owner_col = id_cols[:, :1] // ROWS_DEV
    earlier = lax.broadcasted_iota(jnp.int32, (count, count), 0) < lax.broadcasted_iota(
        jnp.int32, (count, count), 1
    )
    same = jnp.where((owner_col == owner_row) & earlier, 1, 0)
    rank = jnp.sum(same, axis=0, keepdims=True)
    dest = (owner_row // 4 % 2) * 64 + owner_row // 8 * 4 + owner_row % 4
    slot = dest * CAP + rank
    slots = hot.shape[0]
    hot[...] = jnp.where(
        lax.broadcasted_iota(jnp.int32, (slots, count), 0) == slot, 1.0, 0.0
    ).astype(BF16)
    within = id_cols - (id_cols // ROWS_DEV) * ROWS_DEV
    high = within // 32
    lane = lax.broadcasted_iota(jnp.int32, (count, EXT), 1)
    ext[...] = (
        jnp.where(lane == 0, high + 1, jnp.where(lane == 1, within - high * 32, 0))
        .astype(F32)
        .astype(BF16)
    )


V_COLS, K_COLS, Q_COLS, G_COLS = (slice(i * HD, (i + 1) * HD) for i in range(4))
GRP = 2 * BLK


def my_place():
    return lax.axis_index("p"), lax.axis_index("c")


def my_length(lengths):
    return lengths[lax.axis_index("y") // 2]


def inverse_of(length):
    return 1.0 / jnp.full((1, HD), length, jnp.int32).astype(F32)


def diagonal(row_place, col_place, rows_are_keys):
    def start(place):
        return (4 * place[0] + place[1]) * BLK

    row = lax.broadcasted_iota(jnp.int32, (GRP, GRP), 0)
    col = lax.broadcasted_iota(jnp.int32, (GRP, GRP), 1)
    row = jnp.where(row >= BLK, row + BLK, row) + start(row_place)
    col = jnp.where(col >= BLK, col + BLK, col) + start(col_place)
    return row <= col if rows_are_keys else col <= row


def mask_first(mask, values):
    first = jnp.where(mask, values[:GRP, :], 0.0)
    return jnp.concatenate([first, values[GRP:, :]], axis=0) if values.shape[0] > GRP else first


def mask_last(mask, values):
    last = jnp.where(mask, values[-GRP:, :], 0.0)
    return jnp.concatenate([values[:-GRP, :], last], axis=0) if values.shape[0] > GRP else last


def part_place(part):
    p, c = my_place()
    return (1 - p if part & 2 else p), (1 - c if part & 1 else c)


def query_rows(y):
    start = y * (9 - y) // 2 * GRP
    return slice(start, start + (4 - y) * GRP)


def forward_kernel(part_ids, lengths, own, *refs):
    count = len(part_ids)
    first, last = part_ids[0] == 0, part_ids[-1] == 3
    keys_of, refs = refs[:count], refs[count:]
    if not first:
        before, *refs = refs
    out, *refs = refs
    slopes_out, refs = refs[:count], refs[count:]
    out[...] = jnp.zeros_like(out) if first else before[...]
    for y in range(4):
        rows = slice(y * GRP, 1024)
        queries = own[rows, Q_COLS]
        keys = slice(y * GRP, (y + 1) * GRP)
        for part, src, slope_out in zip(part_ids, keys_of, slopes_out):
            slope, attn = slopes(dot_t(queries, src[keys, K_COLS]))
            mask = diagonal(my_place(), part_place(part), False)
            slope_out[query_rows(y), :] = mask_first(mask, slope)
            attn = mask_first(mask, attn)
            out[rows, :] += dot(attn.astype(BF16), src[keys, V_COLS])
    if not last:
        return
    (stats,) = refs
    inv_len = inverse_of(my_length(lengths))
    for m in range(8):
        rows = slice(m * BLK, (m + 1) * BLK)
        total = out[rows, :] * inv_len
        out[rows, :] = total
        g = own[rows, G_COLS].astype(F32)
        mean = jnp.mean(total, axis=-1, keepdims=True)
        center = total - mean
        square = jnp.sum(center * center, axis=-1, keepdims=True)
        sum_g = jnp.sum(g, axis=-1, keepdims=True)
        sum_ga = jnp.sum(g * center, axis=-1, keepdims=True)
        lane = lax.broadcasted_iota(jnp.int32, (BLK, BLK), 1)
        packed = jnp.where(
            lane == 0, mean, jnp.where(lane == 1, square, jnp.where(lane == 2, sum_g, sum_ga))
        )
        stats[:, rows] = jnp.transpose(packed)[:8, :]


def grad_attn_kernel(lengths, attn_out, own, s0, s1, s2, s3, grad_attn, normed_out):
    p, c = my_place()
    length = my_length(lengths)
    parts = [s0[...], s1[...], s2[...], s3[...]]
    means = [part[0:1, :] for part in parts]
    mean = 0.25 * (means[0] + means[1] + means[2] + means[3])
    square = 0.0
    sum_g = 0.0
    sum_ga = 0.0
    for part, local_mean in zip(parts, means):
        shift = local_mean - mean
        square = square + part[1:2, :] + HD * (shift * shift)
        sum_g = sum_g + part[2:3, :]
        sum_ga = sum_ga + part[3:4, :] + part[2:3, :] * shift
    inverse = lax.rsqrt(square * (1.0 / D) + 1e-05)
    mean_g = sum_g * (1.0 / D)
    mean_gn = inverse * sum_ga * (1.0 / D)
    row = lax.broadcasted_iota(jnp.int32, (BLK, 1024), 0)
    packed = jnp.where(
        row == 0, mean, jnp.where(row == 1, inverse, jnp.where(row == 2, mean_g, mean_gn))
    )
    for m in range(8):
        rows = slice(m * BLK, (m + 1) * BLK)
        cols = jnp.transpose(packed[:, rows])
        inv = cols[:, 1:2]
        n = (attn_out[rows, :] - cols[:, 0:1]) * inv
        back = (own[rows, G_COLS].astype(F32) - cols[:, 2:3] - n * cols[:, 3:4]) * inv
        pos = lax.broadcasted_iota(jnp.int32, (BLK, 1), 0)
        pos = pos + (m // 2 * 8 + 4 * p + m % 2 * 2 + c) * BLK
        grad_attn[rows, :] = jnp.where(pos < length, back, 0.0).astype(BF16)
        normed_out[rows, :] = n.astype(BF16)


def slopes(raw):
    half = raw * (0.5 * SCALE)
    t = jnp.tanh(half)
    two_sigma = 1.0 + t
    return two_sigma + half * (1.0 - t * t), half * two_sigma


def grad_query_kernel(lengths, grad_attn, *refs):
    keys_of, slopes_of, (ret, total) = refs[:4], refs[4:8], refs[8:]
    total[...] = jnp.zeros_like(total)
    for y in range(4):
        rows = slice(y * GRP, 1024)
        keys = slice(y * GRP, (y + 1) * GRP)
        for src, slope in zip(keys_of, slopes_of):
            score = slope[query_rows(y), :] * dot_t(grad_attn[rows, :], src[keys, V_COLS])
            total[rows, :] += dot(score.astype(BF16), src[keys, K_COLS])
    inv_len = inverse_of(my_length(lengths))
    ret[...] = (total[...] * (0.5 * SCALE * inv_len)).astype(BF16)


PACKED = 10 * GRP


def packed_rows(y):
    start = y * (y + 1) // 2 * GRP
    return slice(start, start + (y + 1) * GRP)


def key_scores_kernel(part_ids, own, *refs):
    queries_of, outs = refs[:2], (refs[2:4], refs[4:6])
    for y in range(4):
        keys = own[: (y + 1) * GRP, K_COLS]
        events = slice(y * GRP, (y + 1) * GRP)
        for part, src, (slope_out, attn_out) in zip(part_ids, queries_of, outs):
            slope, attn = slopes(dot_t(keys, src[events, :]))
            mask = diagonal(my_place(), part_place(part), True)
            slope_out[packed_rows(y), :] = mask_last(mask, slope)
            attn_out[packed_rows(y), :] = mask_last(mask, attn).astype(BF16)


def grad_key_kernel(last, lengths, own, *refs):
    queries_of, scores, grads_of, refs = refs[:2], (refs[2:4], refs[4:6]), refs[6:8], refs[8:]
    if last:
        k_before, v_before, normed_out, grad_q, ret, grad_k, grad_v = refs
        grad_k[...] = k_before[...]
        grad_v[...] = v_before[...]
    else:
        grad_k, grad_v = refs
        grad_k[...] = jnp.zeros_like(grad_k)
        grad_v[...] = jnp.zeros_like(grad_v)
    for y in range(4):
        rows = slice(0, (y + 1) * GRP)
        events = slice(y * GRP, (y + 1) * GRP)
        values = own[rows, V_COLS]
        for q, (slope, attn), grad_attn in zip(queries_of, scores, grads_of):
            ga = grad_attn[events, :]
            score = slope[packed_rows(y), :] * dot_t(values, ga)
            grad_k[rows, :] += dot(score.astype(BF16), q[events, :])
            grad_v[rows, :] += dot(attn[packed_rows(y), :], ga)
    if last:
        inv_len = inverse_of(my_length(lengths))
        ret[:, :HD] = normed_out[...]
        ret[:, HD : 2 * HD] = (grad_v[...] * inv_len).astype(BF16)
        ret[:, 2 * HD : 3 * HD] = grad_q[...]
        ret[:, 3 * HD :] = (grad_k[...] * (0.5 * SCALE * inv_len)).astype(BF16)


def finish_kernel(
    lengths, ret, slope, normed, inverse, grad_out, w_inner, hot, ext, send, grads
):
    for g in range(2):
        rows = slice(g * BLK, (g + 1) * BLK)
        for h in range(HEADS):
            at = slice((g * HEADS + h) * BLK, (g * HEADS + h + 1) * BLK)
            for part in range(4):
                cols = slice(part * D + h * HD, part * D + (h + 1) * HD)
                grad = ret[at, part * HD : (part + 1) * HD].astype(F32)
                grads[rows, cols] = (grad * slope[rows, cols]).astype(BF16)
    grad_normed = dot_t(grads[...], w_inner[...])
    back = inverse[:, :1] * (
        grad_normed
        - jnp.mean(grad_normed, axis=-1, keepdims=True)
        - normed[...] * jnp.mean(grad_normed * normed[...], axis=-1, keepdims=True)
    )
    total = grad_out[...].astype(F32) + back
    chip = (lax.axis_index("y") * 2 + lax.axis_index("p")) * 2 + lax.axis_index("w")
    first = (chip * 2 + lax.axis_index("c")) * BLK
    row = lax.broadcasted_iota(jnp.int32, (2 * BLK, 1), 0)
    second = row >= BLK
    pos = first + jnp.where(second, row - BLK, row)
    total = jnp.where(pos < jnp.where(second, lengths[1], lengths[0]), total, 0.0)
    send[:, :D] = dot(hot[...], total.astype(BF16)).astype(BF16)
    send[:, D:] = dot(hot[...], ext[...]).astype(BF16)


def table_kernel(got, table, stage, sems):
    packed = jnp.transpose(got[:, D:].astype(F32))
    dest = ((packed[0:1, :] - 1.0) * 32.0 + packed[1:2, :]).astype(jnp.int32)
    leaving = []
    for i in range(ROWS_DEV // BLK):
        rows = slice(i * BLK, (i + 1) * BLK)
        row = lax.broadcasted_iota(jnp.int32, (BLK, got.shape[0]), 0) + i * BLK
        hot = jnp.where(row == dest, 1.0, 0.0).astype(BF16)
        stage[rows, :] = dot(hot, got[:, :D])
        leaving.append(pltpu.make_async_copy(stage.at[rows], table.at[rows], sems.at[i]))
        leaving[-1].start()
    for copy in leaving:
        copy.wait()


def call(kernel, outs, args, scalars=1, scratch=(), flops=0):
    vmem = pl.BlockSpec(memory_space=pltpu.VMEM)
    smem = pl.BlockSpec(memory_space=pltpu.SMEM)
    return pl.pallas_call(
        kernel,
        out_shape=[jax.ShapeDtypeStruct(shape, dtype) for shape, dtype in outs],
        in_specs=[smem] * scalars + [vmem] * (len(args) - scalars),
        out_specs=[vmem] * len(outs),
        scratch_shapes=[pltpu.VMEM(shape, dtype) for shape, dtype in scratch],
        compiler_params=pltpu.CompilerParams(vmem_limit_bytes=VMEM_LIMIT),
        cost_estimate=pl.CostEstimate(flops=flops, bytes_accessed=2**20, transcendentals=0),
    )(*args)


def project(*args):
    hbm = pl.BlockSpec(memory_space=pltpu.HBM)
    return pl.pallas_call(
        project_kernel,
        out_shape=jax.ShapeDtypeStruct((8 * BLK, 4 * HD), BF16),
        in_specs=[hbm] * len(args),
        out_specs=hbm,
        scratch_shapes=[
            pltpu.VMEM((2 * BLK, D), BF16),
            pltpu.VMEM((2 * BLK, D), BF16),
            pltpu.VMEM((4, D, D), BF16),
            pltpu.VMEM((D, D), BF16),
            pltpu.VMEM((4, 8 * BLK, HD), BF16),
            pltpu.SemaphoreType.DMA((11,)),
        ],
        compiler_params=pltpu.CompilerParams(vmem_limit_bytes=PROJECT_LIMIT),
    )(*args)


def local(events, grad_out, w_inner, w_outer, valid_lengths, item_ids):
    events = events.reshape(2 * BLK, D)
    grad_out = grad_out.reshape(2 * BLK, D)
    rows_bf16, rows_f32 = ((1024, HD), BF16), ((1024, HD), F32)
    swap = [(0, 1), (1, 0)]
    send = project(events, grad_out, w_inner, w_outer)
    own = lax.all_to_all(send, ("y", "w"), 0, 0, tiled=True)
    slope, normed, inverse, hot, ext = call(
        gate_kernel,
        [
            ((2 * BLK, 4 * D), F32),
            ((2 * BLK, D), F32),
            ((2 * BLK, HD), F32),
            ((CAP * 128, 2 * BLK), BF16),
            ((2 * BLK, EXT), BF16),
        ],
        (events, grad_out, w_inner, w_outer, item_ids.reshape(1, 2 * BLK)),
        scalars=0,
        flops=2 * 10**9,
    )
    own, slope = lax.optimization_barrier((own, slope))
    slope_shape, score_shapes = ((PACKED, GRP), F32), [((PACKED, GRP), F32), ((PACKED, GRP), BF16)]
    vk, q = own[:, : 2 * HD], own[:, Q_COLS]
    vk_p = lax.ppermute(vk, "p", swap)
    vk_c = lax.ppermute(vk, "c", swap)
    q_c = lax.ppermute(q, "c", swap)

    def forward(part_ids, keys, before, extra=()):
        return call(
            functools.partial(forward_kernel, part_ids),
            [rows_f32] + [slope_shape] * len(keys) + list(extra),
            (valid_lengths, own, *keys, *before),
            flops=10**9 * len(keys) // 2,
        )

    def key_scores(part_ids, src, queries):
        return call(
            functools.partial(key_scores_kernel, part_ids),
            score_shapes * 2,
            (src, *queries),
            scalars=0,
            flops=10**9,
        )

    attn_out, slope_o, slope_c = forward((0, 1), (own, vk_c), ())
    scores_one = key_scores((0, 1), own, (q, q_c))
    vk_p, attn_out, scores_one, q_late = lax.optimization_barrier((vk_p, attn_out, scores_one, q))
    vk_pc = lax.ppermute(vk_p, "c", swap)
    q_p = lax.ppermute(q_late, "p", swap)
    attn_out, slope_p = forward((2,), (vk_p,), (attn_out,))
    attn_out, slope_pc, stats = forward((3,), (vk_pc,), (attn_out,), [((8, 1024), F32)])
    others = [
        lax.ppermute(stats, ("y", "w"), [(i, i ^ m) for i in range(8)]) for m in (1, 2, 3)
    ]
    q_p, others = lax.optimization_barrier((q_p, others))
    q_pc = lax.ppermute(q_p, "c", swap)
    grad_attn, normed_out = call(
        grad_attn_kernel,
        [rows_bf16, rows_bf16],
        (valid_lengths, attn_out, own, stats, *others),
        flops=10**7,
    )
    grad_p, grad_c = [
        lax.ppermute(grad_attn, ("p", "c"), [(i, i ^ m) for i in range(4)]) for m in (2, 1)
    ]
    own_late, grad_attn = lax.optimization_barrier((own, grad_attn))
    scores_two = key_scores((2, 3), own_late, (q_p, q_pc))
    (grad_q,) = call(
        grad_query_kernel,
        [rows_bf16],
        (valid_lengths, grad_attn, own, vk_c, vk_p, vk_pc, slope_o, slope_c, slope_p, slope_pc),
        scratch=[rows_f32],
        flops=4 * 10**9,
    )
    grad_p, grad_q, scores_two = lax.optimization_barrier((grad_p, grad_q, scores_two))
    grad_pc = lax.ppermute(grad_p, "c", swap)
    grad_k, grad_v = call(
        functools.partial(grad_key_kernel, False),
        [rows_f32, rows_f32],
        (valid_lengths, own, q, q_c, *scores_one, grad_attn, grad_c),
        flops=3 * 10**9,
    )
    (ret,) = call(
        functools.partial(grad_key_kernel, True),
        [((1024, 4 * HD), BF16)],
        (
            valid_lengths,
            own,
            q_p,
            q_pc,
            *scores_two,
            grad_p,
            grad_pc,
            grad_k,
            grad_v,
            normed_out,
            grad_q,
        ),
        scratch=[rows_f32, rows_f32],
        flops=3 * 10**9,
    )
    got = lax.all_to_all(ret, ("y", "w"), 0, 0, tiled=True)
    (rows,) = call(
        finish_kernel,
        [((CAP * 128, D + EXT), BF16)],
        (valid_lengths, got, slope, normed, inverse, grad_out, w_inner, hot, ext),
        scratch=[((2 * BLK, 4 * D), BF16)],
        flops=10**9,
    )
    got = lax.all_to_all(
        rows.reshape(128, CAP, D + EXT), ("c", "y", "p", "w", "row"), 0, 0, tiled=True
    ).reshape(128 * CAP, D + EXT)
    return pl.pallas_call(
        table_kernel,
        out_shape=jax.ShapeDtypeStruct((ROWS_DEV, D), F32),
        in_specs=[pl.BlockSpec(memory_space=pltpu.VMEM)],
        out_specs=pl.BlockSpec(memory_space=pltpu.HBM),
        scratch_shapes=[pltpu.VMEM((ROWS_DEV, D), F32), pltpu.SemaphoreType.DMA((8,))],
        compiler_params=pltpu.CompilerParams(vmem_limit_bytes=VMEM_LIMIT),
    )(got)


def solution(mesh):
    fine = Mesh(mesh.devices.reshape(4, 2, 2, 2, 4), ("y", "p", "w", "c", "row"))
    seq = ("y", "p", "w", "c")
    return jax.shard_map(
        local,
        mesh=fine,
        in_specs=(
            P("row", seq, None),
            P("row", seq, None),
            P(),
            P(),
            P("row"),
            P("row", seq),
        ),
        out_specs=P(seq + ("row",), None),
        check_vma=False,
    )
```

```python
import functools

import jax
import jax.numpy as jnp
from jax import lax
from jax.experimental import pallas as pl
from jax.experimental.pallas import tpu as pltpu
from jax.sharding import Mesh
from jax.sharding import PartitionSpec as P

HEADS = 4
ROWS_DEV = 1024
D = 512
HD = 128
BLK = 128
CAP = 4
EXT = 128
F32 = jnp.float32
BF16 = jnp.bfloat16
SCALE = HD**-0.5
VMEM_LIMIT = 12 * 2**20
PROJECT_LIMIT = 60 * 2**20


def dot(a, b):
    return lax.dot_general(a, b, (((1,), (0,)), ((), ())), preferred_element_type=F32)


def dot_t(a, b):
    return lax.dot_general(a, b, (((1,), (1,)), ((), ())), preferred_element_type=F32)


def normalize(values):
    center = values - jnp.mean(values, axis=-1, keepdims=True)
    inverse = lax.rsqrt(jnp.mean(center * center, axis=-1, keepdims=True) + 1e-05)
    return center * inverse, inverse


def silu(values):
    half = 0.5 * values
    return half * jnp.tanh(half) + half


def silu_slope(values):
    half = 0.5 * values
    two_sigma = 1.0 + jnp.tanh(half)
    return 0.5 * two_sigma * (1.0 + values - half * two_sigma)


def project_kernel(
    events_hbm, grad_hbm, w_hbm, w_outer_hbm, send, events, grad_out, weights, w_outer, parts, sems
):
    copies = [pltpu.make_async_copy(events_hbm, events, sems.at[4])]
    for part in (1, 3, 2, 0):
        cols = slice(part * D, (part + 1) * D)
        copies.append(pltpu.make_async_copy(w_hbm.at[:, cols], weights.at[part], sems.at[part]))
    copies.append(pltpu.make_async_copy(w_outer_hbm, w_outer, sems.at[5]))
    copies.append(pltpu.make_async_copy(grad_hbm, grad_out, sems.at[6]))
    for copy in copies:
        copy.start()
    leaving = []
    copies[0].wait()
    normed = normalize(events[...].astype(F32))[0].astype(BF16)
    for slot, part in enumerate((1, 3, 2, 0)):
        copies[slot + 1].wait()
        act = silu(dot(normed, weights[part])).astype(BF16)
        if part == 0:
            copies[5].wait()
            copies[6].wait()
            act = (dot_t(grad_out[...], w_outer[...]) * act.astype(F32)).astype(BF16)
        for g in range(2):
            for h in range(HEADS):
                piece = act[g * BLK : (g + 1) * BLK, h * HD : (h + 1) * HD]
                at = (g * HEADS + h) * BLK
                parts[slot, at : at + BLK, :] = piece
        cols = slice(slot * HD, (slot + 1) * HD)
        leaving.append(pltpu.make_async_copy(parts.at[slot], send.at[:, cols], sems.at[7 + slot]))
        leaving[-1].start()
    for copy in leaving:
        copy.wait()


def gate_kernel(events, grad_out, w_inner, w_outer, ids, slope, normed_out, inv_out, hot, ext):
    normed, inverse = normalize(events[...].astype(F32))
    normed_out[...] = normed
    inv_out[...] = jnp.broadcast_to(inverse, inv_out.shape)
    normed = normed.astype(BF16)
    for part in range(4):
        cols = slice(part * D, (part + 1) * D)
        values = silu_slope(dot(normed, w_inner[:, cols]))
        if part == 0:
            values = values * dot_t(grad_out[...], w_outer[...])
        slope[:, cols] = values
    count = 2 * BLK
    id_row = ids[...]
    id_cols = jnp.transpose(jnp.broadcast_to(id_row.astype(F32), (BLK, count))).astype(jnp.int32)
    owner_row = id_row // ROWS_DEV
    owner_col = id_cols[:, :1] // ROWS_DEV
    earlier = lax.broadcasted_iota(jnp.int32, (count, count), 0) < lax.broadcasted_iota(
        jnp.int32, (count, count), 1
    )
    same = jnp.where((owner_col == owner_row) & earlier, 1, 0)
    rank = jnp.sum(same, axis=0, keepdims=True)
    dest = (owner_row // 4 % 2) * 64 + owner_row // 8 * 4 + owner_row % 4
    slot = dest * CAP + rank
    slots = hot.shape[0]
    hot[...] = jnp.where(
        lax.broadcasted_iota(jnp.int32, (slots, count), 0) == slot, 1.0, 0.0
    ).astype(BF16)
    within = id_cols - (id_cols // ROWS_DEV) * ROWS_DEV
    high = within // 32
    lane = lax.broadcasted_iota(jnp.int32, (count, EXT), 1)
    ext[...] = (
        jnp.where(lane == 0, high + 1, jnp.where(lane == 1, within - high * 32, 0))
        .astype(F32)
        .astype(BF16)
    )


V_COLS, K_COLS, Q_COLS, G_COLS = (slice(i * HD, (i + 1) * HD) for i in range(4))
GRP = 2 * BLK


def my_place():
    return lax.axis_index("p"), lax.axis_index("c")


def my_length(lengths):
    return lengths[lax.axis_index("y") // 2]


def inverse_of(length):
    return 1.0 / jnp.full((1, HD), length, jnp.int32).astype(F32)


def diagonal(row_place, col_place, rows_are_keys):
    def start(place):
        return (4 * place[0] + place[1]) * BLK

    row = lax.broadcasted_iota(jnp.int32, (GRP, GRP), 0)
    col = lax.broadcasted_iota(jnp.int32, (GRP, GRP), 1)
    row = jnp.where(row >= BLK, row + BLK, row) + start(row_place)
    col = jnp.where(col >= BLK, col + BLK, col) + start(col_place)
    return row <= col if rows_are_keys else col <= row


def mask_first(mask, values):
    first = jnp.where(mask, values[:GRP, :], 0.0)
    return jnp.concatenate([first, values[GRP:, :]], axis=0) if values.shape[0] > GRP else first


def mask_last(mask, values):
    last = jnp.where(mask, values[-GRP:, :], 0.0)
    return jnp.concatenate([values[:-GRP, :], last], axis=0) if values.shape[0] > GRP else last


def part_place(part):
    p, c = my_place()
    return (1 - p if part & 2 else p), (1 - c if part & 1 else c)


def query_rows(y):
    start = y * (9 - y) // 2 * GRP
    return slice(start, start + (4 - y) * GRP)


def forward_kernel(part_ids, lengths, own, *refs):
    count = len(part_ids)
    first, last = part_ids[0] == 0, part_ids[-1] == 3
    keys_of, refs = refs[:count], refs[count:]
    if not first:
        before, *refs = refs
    out, *refs = refs
    slopes_out, refs = refs[:count], refs[count:]
    out[...] = jnp.zeros_like(out) if first else before[...]
    for y in range(4):
        rows = slice(y * GRP, 1024)
        queries = own[rows, Q_COLS]
        keys = slice(y * GRP, (y + 1) * GRP)
        for part, src, slope_out in zip(part_ids, keys_of, slopes_out):
            slope, attn = slopes(dot_t(queries, src[keys, K_COLS]))
            mask = diagonal(my_place(), part_place(part), False)
            slope_out[query_rows(y), :] = mask_first(mask, slope)
            attn = mask_first(mask, attn)
            out[rows, :] += dot(attn.astype(BF16), src[keys, V_COLS])
    if not last:
        return
    (stats,) = refs
    inv_len = inverse_of(my_length(lengths))
    for m in range(8):
        rows = slice(m * BLK, (m + 1) * BLK)
        total = out[rows, :] * inv_len
        out[rows, :] = total
        g = own[rows, G_COLS].astype(F32)
        mean = jnp.mean(total, axis=-1, keepdims=True)
        center = total - mean
        square = jnp.sum(center * center, axis=-1, keepdims=True)
        sum_g = jnp.sum(g, axis=-1, keepdims=True)
        sum_ga = jnp.sum(g * center, axis=-1, keepdims=True)
        lane = lax.broadcasted_iota(jnp.int32, (BLK, BLK), 1)
        packed = jnp.where(
            lane == 0, mean, jnp.where(lane == 1, square, jnp.where(lane == 2, sum_g, sum_ga))
        )
        stats[:, rows] = jnp.transpose(packed)[:8, :]


def grad_attn_kernel(lengths, attn_out, own, s0, s1, s2, s3, grad_attn, normed_out):
    p, c = my_place()
    length = my_length(lengths)
    parts = [s0[...], s1[...], s2[...], s3[...]]
    means = [part[0:1, :] for part in parts]
    mean = 0.25 * (means[0] + means[1] + means[2] + means[3])
    square = 0.0
    sum_g = 0.0
    sum_ga = 0.0
    for part, local_mean in zip(parts, means):
        shift = local_mean - mean
        square = square + part[1:2, :] + HD * (shift * shift)
        sum_g = sum_g + part[2:3, :]
        sum_ga = sum_ga + part[3:4, :] + part[2:3, :] * shift
    inverse = lax.rsqrt(square * (1.0 / D) + 1e-05)
    mean_g = sum_g * (1.0 / D)
    mean_gn = inverse * sum_ga * (1.0 / D)
    row = lax.broadcasted_iota(jnp.int32, (BLK, 1024), 0)
    packed = jnp.where(
        row == 0, mean, jnp.where(row == 1, inverse, jnp.where(row == 2, mean_g, mean_gn))
    )
    for m in range(8):
        rows = slice(m * BLK, (m + 1) * BLK)
        cols = jnp.transpose(packed[:, rows])
        inv = cols[:, 1:2]
        n = (attn_out[rows, :] - cols[:, 0:1]) * inv
        back = (own[rows, G_COLS].astype(F32) - cols[:, 2:3] - n * cols[:, 3:4]) * inv
        pos = lax.broadcasted_iota(jnp.int32, (BLK, 1), 0)
        pos = pos + (m // 2 * 8 + 4 * p + m % 2 * 2 + c) * BLK
        grad_attn[rows, :] = jnp.where(pos < length, back, 0.0).astype(BF16)
        normed_out[rows, :] = n.astype(BF16)


def slopes(raw):
    half = raw * (0.5 * SCALE)
    t = jnp.tanh(half)
    two_sigma = 1.0 + t
    return two_sigma + half * (1.0 - t * t), half * two_sigma


def grad_query_kernel(lengths, grad_attn, *refs):
    keys_of, slopes_of, (ret, total) = refs[:4], refs[4:8], refs[8:]
    total[...] = jnp.zeros_like(total)
    for y in range(4):
        rows = slice(y * GRP, 1024)
        keys = slice(y * GRP, (y + 1) * GRP)
        for src, slope in zip(keys_of, slopes_of):
            score = slope[query_rows(y), :] * dot_t(grad_attn[rows, :], src[keys, V_COLS])
            total[rows, :] += dot(score.astype(BF16), src[keys, K_COLS])
    inv_len = inverse_of(my_length(lengths))
    ret[...] = (total[...] * (0.5 * SCALE * inv_len)).astype(BF16)


PACKED = 10 * GRP


def packed_rows(y):
    start = y * (y + 1) // 2 * GRP
    return slice(start, start + (y + 1) * GRP)


def key_scores_kernel(part_ids, own, *refs):
    queries_of, outs = refs[:2], (refs[2:4], refs[4:6])
    for y in range(4):
        keys = own[: (y + 1) * GRP, K_COLS]
        events = slice(y * GRP, (y + 1) * GRP)
        for part, src, (slope_out, attn_out) in zip(part_ids, queries_of, outs):
            slope, attn = slopes(dot_t(keys, src[events, :]))
            mask = diagonal(my_place(), part_place(part), True)
            slope_out[packed_rows(y), :] = mask_last(mask, slope)
            attn_out[packed_rows(y), :] = mask_last(mask, attn).astype(BF16)


def grad_key_kernel(last, lengths, own, *refs):
    queries_of, scores, grads_of, refs = refs[:2], (refs[2:4], refs[4:6]), refs[6:8], refs[8:]
    if last:
        k_before, v_before, normed_out, grad_q, ret, grad_k, grad_v = refs
        grad_k[...] = k_before[...]
        grad_v[...] = v_before[...]
    else:
        grad_k, grad_v = refs
        grad_k[...] = jnp.zeros_like(grad_k)
        grad_v[...] = jnp.zeros_like(grad_v)
    for y in range(4):
        rows = slice(0, (y + 1) * GRP)
        events = slice(y * GRP, (y + 1) * GRP)
        values = own[rows, V_COLS]
        for q, (slope, attn), grad_attn in zip(queries_of, scores, grads_of):
            ga = grad_attn[events, :]
            score = slope[packed_rows(y), :] * dot_t(values, ga)
            grad_k[rows, :] += dot(score.astype(BF16), q[events, :])
            grad_v[rows, :] += dot(attn[packed_rows(y), :], ga)
    if last:
        inv_len = inverse_of(my_length(lengths))
        ret[:, :HD] = normed_out[...]
        ret[:, HD : 2 * HD] = (grad_v[...] * inv_len).astype(BF16)
        ret[:, 2 * HD : 3 * HD] = grad_q[...]
        ret[:, 3 * HD :] = (grad_k[...] * (0.5 * SCALE * inv_len)).astype(BF16)


def finish_kernel(
    lengths, ret, slope, normed, inverse, grad_out, w_inner, hot, ext, send, grads
):
    for g in range(2):
        rows = slice(g * BLK, (g + 1) * BLK)
        for h in range(HEADS):
            at = slice((g * HEADS + h) * BLK, (g * HEADS + h + 1) * BLK)
            for part in range(4):
                cols = slice(part * D + h * HD, part * D + (h + 1) * HD)
                grad = ret[at, part * HD : (part + 1) * HD].astype(F32)
                grads[rows, cols] = (grad * slope[rows, cols]).astype(BF16)
    grad_normed = dot_t(grads[...], w_inner[...])
    back = inverse[:, :1] * (
        grad_normed
        - jnp.mean(grad_normed, axis=-1, keepdims=True)
        - normed[...] * jnp.mean(grad_normed * normed[...], axis=-1, keepdims=True)
    )
    total = grad_out[...].astype(F32) + back
    chip = (lax.axis_index("y") * 2 + lax.axis_index("p")) * 2 + lax.axis_index("w")
    first = (chip * 2 + lax.axis_index("c")) * BLK
    row = lax.broadcasted_iota(jnp.int32, (2 * BLK, 1), 0)
    second = row >= BLK
    pos = first + jnp.where(second, row - BLK, row)
    total = jnp.where(pos < jnp.where(second, lengths[1], lengths[0]), total, 0.0)
    send[:, :D] = dot(hot[...], total.astype(BF16)).astype(BF16)
    send[:, D:] = dot(hot[...], ext[...]).astype(BF16)


def table_kernel(got, table, stage, sems):
    packed = jnp.transpose(got[:, D:].astype(F32))
    dest = ((packed[0:1, :] - 1.0) * 32.0 + packed[1:2, :]).astype(jnp.int32)
    leaving = []
    for i in range(ROWS_DEV // BLK):
        rows = slice(i * BLK, (i + 1) * BLK)
        row = lax.broadcasted_iota(jnp.int32, (BLK, got.shape[0]), 0) + i * BLK
        hot = jnp.where(row == dest, 1.0, 0.0).astype(BF16)
        stage[rows, :] = dot(hot, got[:, :D])
        leaving.append(pltpu.make_async_copy(stage.at[rows], table.at[rows], sems.at[i]))
        leaving[-1].start()
    for copy in leaving:
        copy.wait()


def call(kernel, outs, args, scalars=1, scratch=(), flops=0):
    vmem = pl.BlockSpec(memory_space=pltpu.VMEM)
    smem = pl.BlockSpec(memory_space=pltpu.SMEM)
    return pl.pallas_call(
        kernel,
        out_shape=[jax.ShapeDtypeStruct(shape, dtype) for shape, dtype in outs],
        in_specs=[smem] * scalars + [vmem] * (len(args) - scalars),
        out_specs=[vmem] * len(outs),
        scratch_shapes=[pltpu.VMEM(shape, dtype) for shape, dtype in scratch],
        compiler_params=pltpu.CompilerParams(vmem_limit_bytes=VMEM_LIMIT),
        cost_estimate=pl.CostEstimate(flops=flops, bytes_accessed=2**20, transcendentals=0),
    )(*args)


def project(*args):
    hbm = pl.BlockSpec(memory_space=pltpu.HBM)
    return pl.pallas_call(
        project_kernel,
        out_shape=jax.ShapeDtypeStruct((8 * BLK, 4 * HD), BF16),
        in_specs=[hbm] * len(args),
        out_specs=hbm,
        scratch_shapes=[
            pltpu.VMEM((2 * BLK, D), BF16),
            pltpu.VMEM((2 * BLK, D), BF16),
            pltpu.VMEM((4, D, D), BF16),
            pltpu.VMEM((D, D), BF16),
            pltpu.VMEM((4, 8 * BLK, HD), BF16),
            pltpu.SemaphoreType.DMA((11,)),
        ],
        compiler_params=pltpu.CompilerParams(vmem_limit_bytes=PROJECT_LIMIT),
    )(*args)


def local(events, grad_out, w_inner, w_outer, valid_lengths, item_ids):
    events = events.reshape(2 * BLK, D)
    grad_out = grad_out.reshape(2 * BLK, D)
    rows_bf16, rows_f32 = ((1024, HD), BF16), ((1024, HD), F32)
    swap = [(0, 1), (1, 0)]
    send = project(events, grad_out, w_inner, w_outer)
    own = lax.all_to_all(send, ("y", "w"), 0, 0, tiled=True)
    slope, normed, inverse, hot, ext = call(
        gate_kernel,
        [
            ((2 * BLK, 4 * D), F32),
            ((2 * BLK, D), F32),
            ((2 * BLK, HD), F32),
            ((CAP * 128, 2 * BLK), BF16),
            ((2 * BLK, EXT), BF16),
        ],
        (events, grad_out, w_inner, w_outer, item_ids.reshape(1, 2 * BLK)),
        scalars=0,
        flops=2 * 10**9,
    )
    own, slope = lax.optimization_barrier((own, slope))
    slope_shape, score_shapes = ((PACKED, GRP), F32), [((PACKED, GRP), F32), ((PACKED, GRP), BF16)]
    vk, q = own[:, : 2 * HD], own[:, Q_COLS]
    vk_p = lax.ppermute(vk, "p", swap)
    vk_c = lax.ppermute(vk, "c", swap)
    q_c = lax.ppermute(q, "c", swap)

    def forward(part_ids, keys, before, extra=()):
        return call(
            functools.partial(forward_kernel, part_ids),
            [rows_f32] + [slope_shape] * len(keys) + list(extra),
            (valid_lengths, own, *keys, *before),
            flops=10**9 * len(keys) // 2,
        )

    def key_scores(part_ids, src, queries):
        return call(
            functools.partial(key_scores_kernel, part_ids),
            score_shapes * 2,
            (src, *queries),
            scalars=0,
            flops=10**9,
        )

    attn_out, slope_o, slope_c = forward((0, 1), (own, vk_c), ())
    scores_one = key_scores((0, 1), own, (q, q_c))
    vk_p, attn_out, scores_one, q_late = lax.optimization_barrier((vk_p, attn_out, scores_one, q))
    vk_pc = lax.ppermute(vk_p, "c", swap)
    q_p = lax.ppermute(q_late, "p", swap)
    attn_out, slope_p = forward((2,), (vk_p,), (attn_out,))
    attn_out, slope_pc, stats = forward((3,), (vk_pc,), (attn_out,), [((8, 1024), F32)])
    others = [
        lax.ppermute(stats, ("y", "w"), [(i, i ^ m) for i in range(8)]) for m in (1, 2, 3)
    ]
    q_p, others = lax.optimization_barrier((q_p, others))
    q_pc = lax.ppermute(q_p, "c", swap)
    grad_attn, normed_out = call(
        grad_attn_kernel,
        [rows_bf16, rows_bf16],
        (valid_lengths, attn_out, own, stats, *others),
        flops=10**7,
    )
    grad_p = lax.ppermute(grad_attn, "p", swap)
    own_late, grad_attn = lax.optimization_barrier((own, grad_attn))
    scores_two = key_scores((2, 3), own_late, (q_p, q_pc))
    (grad_q,) = call(
        grad_query_kernel,
        [rows_bf16],
        (valid_lengths, grad_attn, own, vk_c, vk_p, vk_pc, slope_o, slope_c, slope_p, slope_pc),
        scratch=[rows_f32],
        flops=4 * 10**9,
    )
    grad_late, grad_q = lax.optimization_barrier((grad_attn, grad_q))
    grad_c = lax.ppermute(grad_late, "c", swap)
    grad_p, grad_q, scores_two = lax.optimization_barrier((grad_p, grad_q, scores_two))
    grad_pc = lax.ppermute(grad_p, "c", swap)
    grad_k, grad_v = call(
        functools.partial(grad_key_kernel, False),
        [rows_f32, rows_f32],
        (valid_lengths, own, q, q_c, *scores_one, grad_attn, grad_c),
        flops=3 * 10**9,
    )
    (ret,) = call(
        functools.partial(grad_key_kernel, True),
        [((1024, 4 * HD), BF16)],
        (
            valid_lengths,
            own,
            q_p,
            q_pc,
            *scores_two,
            grad_p,
            grad_pc,
            grad_k,
            grad_v,
            normed_out,
            grad_q,
        ),
        scratch=[rows_f32, rows_f32],
        flops=3 * 10**9,
    )
    got = lax.all_to_all(ret, ("y", "w"), 0, 0, tiled=True)
    (rows,) = call(
        finish_kernel,
        [((CAP * 128, D + EXT), BF16)],
        (valid_lengths, got, slope, normed, inverse, grad_out, w_inner, hot, ext),
        scratch=[((2 * BLK, 4 * D), BF16)],
        flops=10**9,
    )
    got = lax.all_to_all(
        rows.reshape(128, CAP, D + EXT), ("c", "y", "p", "w", "row"), 0, 0, tiled=True
    ).reshape(128 * CAP, D + EXT)
    return pl.pallas_call(
        table_kernel,
        out_shape=jax.ShapeDtypeStruct((ROWS_DEV, D), F32),
        in_specs=[pl.BlockSpec(memory_space=pltpu.VMEM)],
        out_specs=pl.BlockSpec(memory_space=pltpu.HBM),
        scratch_shapes=[pltpu.VMEM((ROWS_DEV, D), F32), pltpu.SemaphoreType.DMA((8,))],
        compiler_params=pltpu.CompilerParams(vmem_limit_bytes=VMEM_LIMIT),
    )(got)


def solution(mesh):
    fine = Mesh(mesh.devices.reshape(4, 2, 2, 2, 4), ("y", "p", "w", "c", "row"))
    seq = ("y", "p", "w", "c")
    return jax.shard_map(
        local,
        mesh=fine,
        in_specs=(
            P("row", seq, None),
            P("row", seq, None),
            P(),
            P(),
            P("row"),
            P("row", seq),
        ),
        out_specs=P(seq + ("row",), None),
        check_vma=False,
    )
```

```python
import functools

import jax
import jax.numpy as jnp
from jax import lax
from jax.experimental import pallas as pl
from jax.experimental.pallas import tpu as pltpu
from jax.sharding import Mesh
from jax.sharding import PartitionSpec as P

HEADS = 4
ROWS_DEV = 1024
D = 512
HD = 128
BLK = 128
CAP = 4
EXT = 128
F32 = jnp.float32
BF16 = jnp.bfloat16
SCALE = HD**-0.5
VMEM_LIMIT = 12 * 2**20
PROJECT_LIMIT = 60 * 2**20


def dot(a, b):
    return lax.dot_general(a, b, (((1,), (0,)), ((), ())), preferred_element_type=F32)


def dot_t(a, b):
    return lax.dot_general(a, b, (((1,), (1,)), ((), ())), preferred_element_type=F32)


def normalize(values):
    center = values - jnp.mean(values, axis=-1, keepdims=True)
    inverse = lax.rsqrt(jnp.mean(center * center, axis=-1, keepdims=True) + 1e-05)
    return center * inverse, inverse


def silu(values):
    half = 0.5 * values
    return half * jnp.tanh(half) + half


def silu_slope(values):
    half = 0.5 * values
    two_sigma = 1.0 + jnp.tanh(half)
    return 0.5 * two_sigma * (1.0 + values - half * two_sigma)


def project_kernel(
    events_hbm, grad_hbm, w_hbm, w_outer_hbm, send, events, grad_out, weights, w_outer, parts, sems
):
    copies = [pltpu.make_async_copy(events_hbm, events, sems.at[4])]
    for part in (1, 3, 2, 0):
        cols = slice(part * D, (part + 1) * D)
        copies.append(pltpu.make_async_copy(w_hbm.at[:, cols], weights.at[part], sems.at[part]))
    copies.append(pltpu.make_async_copy(w_outer_hbm, w_outer, sems.at[5]))
    copies.append(pltpu.make_async_copy(grad_hbm, grad_out, sems.at[6]))
    for copy in copies:
        copy.start()
    leaving = []
    copies[0].wait()
    normed = normalize(events[...].astype(F32))[0].astype(BF16)
    for slot, part in enumerate((1, 3, 2, 0)):
        copies[slot + 1].wait()
        act = silu(dot(normed, weights[part])).astype(BF16)
        if part == 0:
            copies[5].wait()
            copies[6].wait()
            act = (dot_t(grad_out[...], w_outer[...]) * act.astype(F32)).astype(BF16)
        for g in range(2):
            for h in range(HEADS):
                piece = act[g * BLK : (g + 1) * BLK, h * HD : (h + 1) * HD]
                at = (g * HEADS + h) * BLK
                parts[slot, at : at + BLK, :] = piece
        cols = slice(slot * HD, (slot + 1) * HD)
        leaving.append(pltpu.make_async_copy(parts.at[slot], send.at[:, cols], sems.at[7 + slot]))
        leaving[-1].start()
    for copy in leaving:
        copy.wait()


def gate_kernel(events, grad_out, w_inner, w_outer, ids, slope, normed_out, inv_out, hot, ext):
    normed, inverse = normalize(events[...].astype(F32))
    normed_out[...] = normed
    inv_out[...] = jnp.broadcast_to(inverse, inv_out.shape)
    normed = normed.astype(BF16)
    for part in range(4):
        cols = slice(part * D, (part + 1) * D)
        values = silu_slope(dot(normed, w_inner[:, cols]))
        if part == 0:
            values = values * dot_t(grad_out[...], w_outer[...])
        slope[:, cols] = values
    count = 2 * BLK
    id_row = ids[...]
    id_cols = jnp.transpose(jnp.broadcast_to(id_row.astype(F32), (BLK, count))).astype(jnp.int32)
    owner_row = id_row // ROWS_DEV
    owner_col = id_cols[:, :1] // ROWS_DEV
    earlier = lax.broadcasted_iota(jnp.int32, (count, count), 0) < lax.broadcasted_iota(
        jnp.int32, (count, count), 1
    )
    same = jnp.where((owner_col == owner_row) & earlier, 1, 0)
    rank = jnp.sum(same, axis=0, keepdims=True)
    slot = owner_row * CAP + rank
    slots = hot.shape[0]
    hot[...] = jnp.where(
        lax.broadcasted_iota(jnp.int32, (slots, count), 0) == slot, 1.0, 0.0
    ).astype(BF16)
    within = id_cols - (id_cols // ROWS_DEV) * ROWS_DEV
    high = within // 32
    lane = lax.broadcasted_iota(jnp.int32, (count, EXT), 1)
    ext[...] = (
        jnp.where(lane == 0, high + 1, jnp.where(lane == 1, within - high * 32, 0))
        .astype(F32)
        .astype(BF16)
    )


V_COLS, K_COLS, Q_COLS, G_COLS = (slice(i * HD, (i + 1) * HD) for i in range(4))
GRP = 2 * BLK


def my_place():
    return lax.axis_index("p"), lax.axis_index("c")


def my_length(lengths):
    return lengths[lax.axis_index("y") // 2]


def inverse_of(length):
    return 1.0 / jnp.full((1, HD), length, jnp.int32).astype(F32)


def diagonal(row_place, col_place, rows_are_keys):
    def start(place):
        return (4 * place[0] + place[1]) * BLK

    row = lax.broadcasted_iota(jnp.int32, (GRP, GRP), 0)
    col = lax.broadcasted_iota(jnp.int32, (GRP, GRP), 1)
    row = jnp.where(row >= BLK, row + BLK, row) + start(row_place)
    col = jnp.where(col >= BLK, col + BLK, col) + start(col_place)
    return row <= col if rows_are_keys else col <= row


def mask_first(mask, values):
    first = jnp.where(mask, values[:GRP, :], 0.0)
    return jnp.concatenate([first, values[GRP:, :]], axis=0) if values.shape[0] > GRP else first


def mask_last(mask, values):
    last = jnp.where(mask, values[-GRP:, :], 0.0)
    return jnp.concatenate([values[:-GRP, :], last], axis=0) if values.shape[0] > GRP else last


def part_place(part):
    p, c = my_place()
    return (1 - p if part & 2 else p), (1 - c if part & 1 else c)


def query_rows(y):
    start = y * (9 - y) // 2 * GRP
    return slice(start, start + (4 - y) * GRP)


def forward_kernel(part_ids, lengths, own, *refs):
    count = len(part_ids)
    first, last = part_ids[0] == 0, part_ids[-1] == 3
    keys_of, refs = refs[:count], refs[count:]
    if not first:
        before, *refs = refs
    out, *refs = refs
    slopes_out, refs = refs[:count], refs[count:]
    out[...] = jnp.zeros_like(out) if first else before[...]
    for y in range(4):
        rows = slice(y * GRP, 1024)
        queries = own[rows, Q_COLS]
        keys = slice(y * GRP, (y + 1) * GRP)
        for part, src, slope_out in zip(part_ids, keys_of, slopes_out):
            slope, attn = slopes(dot_t(queries, src[keys, K_COLS]))
            mask = diagonal(my_place(), part_place(part), False)
            slope_out[query_rows(y), :] = mask_first(mask, slope)
            attn = mask_first(mask, attn)
            out[rows, :] += dot(attn.astype(BF16), src[keys, V_COLS])
    if not last:
        return
    (stats,) = refs
    inv_len = inverse_of(my_length(lengths))
    for m in range(8):
        rows = slice(m * BLK, (m + 1) * BLK)
        total = out[rows, :] * inv_len
        out[rows, :] = total
        g = own[rows, G_COLS].astype(F32)
        mean = jnp.mean(total, axis=-1, keepdims=True)
        center = total - mean
        square = jnp.sum(center * center, axis=-1, keepdims=True)
        sum_g = jnp.sum(g, axis=-1, keepdims=True)
        sum_ga = jnp.sum(g * center, axis=-1, keepdims=True)
        lane = lax.broadcasted_iota(jnp.int32, (BLK, BLK), 1)
        packed = jnp.where(
            lane == 0, mean, jnp.where(lane == 1, square, jnp.where(lane == 2, sum_g, sum_ga))
        )
        stats[:, rows] = jnp.transpose(packed)[:8, :]


def grad_attn_kernel(lengths, attn_out, own, s0, s1, s2, s3, grad_attn, normed_out):
    p, c = my_place()
    length = my_length(lengths)
    parts = [s0[...], s1[...], s2[...], s3[...]]
    means = [part[0:1, :] for part in parts]
    mean = 0.25 * (means[0] + means[1] + means[2] + means[3])
    square = 0.0
    sum_g = 0.0
    sum_ga = 0.0
    for part, local_mean in zip(parts, means):
        shift = local_mean - mean
        square = square + part[1:2, :] + HD * (shift * shift)
        sum_g = sum_g + part[2:3, :]
        sum_ga = sum_ga + part[3:4, :] + part[2:3, :] * shift
    inverse = lax.rsqrt(square * (1.0 / D) + 1e-05)
    mean_g = sum_g * (1.0 / D)
    mean_gn = inverse * sum_ga * (1.0 / D)
    row = lax.broadcasted_iota(jnp.int32, (BLK, 1024), 0)
    packed = jnp.where(
        row == 0, mean, jnp.where(row == 1, inverse, jnp.where(row == 2, mean_g, mean_gn))
    )
    for m in range(8):
        rows = slice(m * BLK, (m + 1) * BLK)
        cols = jnp.transpose(packed[:, rows])
        inv = cols[:, 1:2]
        n = (attn_out[rows, :] - cols[:, 0:1]) * inv
        back = (own[rows, G_COLS].astype(F32) - cols[:, 2:3] - n * cols[:, 3:4]) * inv
        pos = lax.broadcasted_iota(jnp.int32, (BLK, 1), 0)
        pos = pos + (m // 2 * 8 + 4 * p + m % 2 * 2 + c) * BLK
        grad_attn[rows, :] = jnp.where(pos < length, back, 0.0).astype(BF16)
        normed_out[rows, :] = n.astype(BF16)


def slopes(raw):
    half = raw * (0.5 * SCALE)
    t = jnp.tanh(half)
    two_sigma = 1.0 + t
    return two_sigma + half * (1.0 - t * t), half * two_sigma


def grad_query_kernel(lengths, grad_attn, *refs):
    keys_of, slopes_of, (ret, total) = refs[:4], refs[4:8], refs[8:]
    total[...] = jnp.zeros_like(total)
    for y in range(4):
        rows = slice(y * GRP, 1024)
        keys = slice(y * GRP, (y + 1) * GRP)
        for src, slope in zip(keys_of, slopes_of):
            score = slope[query_rows(y), :] * dot_t(grad_attn[rows, :], src[keys, V_COLS])
            total[rows, :] += dot(score.astype(BF16), src[keys, K_COLS])
    inv_len = inverse_of(my_length(lengths))
    ret[...] = (total[...] * (0.5 * SCALE * inv_len)).astype(BF16)


PACKED = 10 * GRP


def packed_rows(y):
    start = y * (y + 1) // 2 * GRP
    return slice(start, start + (y + 1) * GRP)


def key_scores_kernel(part_ids, own, *refs):
    queries_of, outs = refs[:2], (refs[2:4], refs[4:6])
    for y in range(4):
        keys = own[: (y + 1) * GRP, K_COLS]
        events = slice(y * GRP, (y + 1) * GRP)
        for part, src, (slope_out, attn_out) in zip(part_ids, queries_of, outs):
            slope, attn = slopes(dot_t(keys, src[events, :]))
            mask = diagonal(my_place(), part_place(part), True)
            slope_out[packed_rows(y), :] = mask_last(mask, slope)
            attn_out[packed_rows(y), :] = mask_last(mask, attn).astype(BF16)


def grad_key_kernel(last, lengths, own, *refs):
    queries_of, scores, grads_of, refs = refs[:2], (refs[2:4], refs[4:6]), refs[6:8], refs[8:]
    if last:
        k_before, v_before, normed_out, grad_q, ret, grad_k, grad_v = refs
        grad_k[...] = k_before[...]
        grad_v[...] = v_before[...]
    else:
        grad_k, grad_v = refs
        grad_k[...] = jnp.zeros_like(grad_k)
        grad_v[...] = jnp.zeros_like(grad_v)
    for y in range(4):
        rows = slice(0, (y + 1) * GRP)
        events = slice(y * GRP, (y + 1) * GRP)
        values = own[rows, V_COLS]
        for q, (slope, attn), grad_attn in zip(queries_of, scores, grads_of):
            ga = grad_attn[events, :]
            score = slope[packed_rows(y), :] * dot_t(values, ga)
            grad_k[rows, :] += dot(score.astype(BF16), q[events, :])
            grad_v[rows, :] += dot(attn[packed_rows(y), :], ga)
    if last:
        inv_len = inverse_of(my_length(lengths))
        ret[:, :HD] = normed_out[...]
        ret[:, HD : 2 * HD] = (grad_v[...] * inv_len).astype(BF16)
        ret[:, 2 * HD : 3 * HD] = grad_q[...]
        ret[:, 3 * HD :] = (grad_k[...] * (0.5 * SCALE * inv_len)).astype(BF16)


def finish_kernel(
    lengths, ret, slope, normed, inverse, grad_out, w_inner, hot, ext, send, grads
):
    for g in range(2):
        rows = slice(g * BLK, (g + 1) * BLK)
        for h in range(HEADS):
            at = slice((g * HEADS + h) * BLK, (g * HEADS + h + 1) * BLK)
            for part in range(4):
                cols = slice(part * D + h * HD, part * D + (h + 1) * HD)
                grad = ret[at, part * HD : (part + 1) * HD].astype(F32)
                grads[rows, cols] = (grad * slope[rows, cols]).astype(BF16)
    grad_normed = dot_t(grads[...], w_inner[...])
    back = inverse[:, :1] * (
        grad_normed
        - jnp.mean(grad_normed, axis=-1, keepdims=True)
        - normed[...] * jnp.mean(grad_normed * normed[...], axis=-1, keepdims=True)
    )
    total = grad_out[...].astype(F32) + back
    chip = (lax.axis_index("y") * 2 + lax.axis_index("p")) * 2 + lax.axis_index("w")
    first = (chip * 2 + lax.axis_index("c")) * BLK
    row = lax.broadcasted_iota(jnp.int32, (2 * BLK, 1), 0)
    second = row >= BLK
    pos = first + jnp.where(second, row - BLK, row)
    total = jnp.where(pos < jnp.where(second, lengths[1], lengths[0]), total, 0.0)
    send[:, :D] = dot(hot[...], total.astype(BF16)).astype(BF16)
    send[:, D:] = dot(hot[...], ext[...]).astype(BF16)


def table_kernel(got, table, stage, sems):
    packed = jnp.transpose(got[:, D:].astype(F32))
    dest = ((packed[0:1, :] - 1.0) * 32.0 + packed[1:2, :]).astype(jnp.int32)
    leaving = []
    for i in range(ROWS_DEV // BLK):
        rows = slice(i * BLK, (i + 1) * BLK)
        row = lax.broadcasted_iota(jnp.int32, (BLK, got.shape[0]), 0) + i * BLK
        hot = jnp.where(row == dest, 1.0, 0.0).astype(BF16)
        stage[rows, :] = dot(hot, got[:, :D])
        leaving.append(pltpu.make_async_copy(stage.at[rows], table.at[rows], sems.at[i]))
        leaving[-1].start()
    for copy in leaving:
        copy.wait()


def call(kernel, outs, args, scalars=1, scratch=(), flops=0):
    vmem = pl.BlockSpec(memory_space=pltpu.VMEM)
    smem = pl.BlockSpec(memory_space=pltpu.SMEM)
    return pl.pallas_call(
        kernel,
        out_shape=[jax.ShapeDtypeStruct(shape, dtype) for shape, dtype in outs],
        in_specs=[smem] * scalars + [vmem] * (len(args) - scalars),
        out_specs=[vmem] * len(outs),
        scratch_shapes=[pltpu.VMEM(shape, dtype) for shape, dtype in scratch],
        compiler_params=pltpu.CompilerParams(vmem_limit_bytes=VMEM_LIMIT),
        cost_estimate=pl.CostEstimate(flops=flops, bytes_accessed=2**20, transcendentals=0),
    )(*args)


def project(*args):
    hbm = pl.BlockSpec(memory_space=pltpu.HBM)
    return pl.pallas_call(
        project_kernel,
        out_shape=jax.ShapeDtypeStruct((8 * BLK, 4 * HD), BF16),
        in_specs=[hbm] * len(args),
        out_specs=hbm,
        scratch_shapes=[
            pltpu.VMEM((2 * BLK, D), BF16),
            pltpu.VMEM((2 * BLK, D), BF16),
            pltpu.VMEM((4, D, D), BF16),
            pltpu.VMEM((D, D), BF16),
            pltpu.VMEM((4, 8 * BLK, HD), BF16),
            pltpu.SemaphoreType.DMA((11,)),
        ],
        compiler_params=pltpu.CompilerParams(vmem_limit_bytes=PROJECT_LIMIT),
    )(*args)


def local(events, grad_out, w_inner, w_outer, valid_lengths, item_ids):
    events = events.reshape(2 * BLK, D)
    grad_out = grad_out.reshape(2 * BLK, D)
    rows_bf16, rows_f32 = ((1024, HD), BF16), ((1024, HD), F32)
    swap = [(0, 1), (1, 0)]
    send = project(events, grad_out, w_inner, w_outer)
    own = lax.all_to_all(send, ("y", "w"), 0, 0, tiled=True)
    slope, normed, inverse, hot, ext = call(
        gate_kernel,
        [
            ((2 * BLK, 4 * D), F32),
            ((2 * BLK, D), F32),
            ((2 * BLK, HD), F32),
            ((CAP * 128, 2 * BLK), BF16),
            ((2 * BLK, EXT), BF16),
        ],
        (events, grad_out, w_inner, w_outer, item_ids.reshape(1, 2 * BLK)),
        scalars=0,
        flops=2 * 10**9,
    )
    own, slope = lax.optimization_barrier((own, slope))
    slope_shape, score_shapes = ((PACKED, GRP), F32), [((PACKED, GRP), F32), ((PACKED, GRP), BF16)]
    vk, q = own[:, : 2 * HD], own[:, Q_COLS]
    vk_p = lax.ppermute(vk, "p", swap)
    vk_c = lax.ppermute(vk, "c", swap)
    q_c = lax.ppermute(q, "c", swap)

    def forward(part_ids, keys, before, extra=()):
        return call(
            functools.partial(forward_kernel, part_ids),
            [rows_f32] + [slope_shape] * len(keys) + list(extra),
            (valid_lengths, own, *keys, *before),
            flops=10**9 * len(keys) // 2,
        )

    def key_scores(part_ids, src, queries):
        return call(
            functools.partial(key_scores_kernel, part_ids),
            score_shapes * 2,
            (src, *queries),
            scalars=0,
            flops=10**9,
        )

    attn_out, slope_o, slope_c = forward((0, 1), (own, vk_c), ())
    scores_one = key_scores((0, 1), own, (q, q_c))
    vk_p, attn_out, scores_one, q_late = lax.optimization_barrier((vk_p, attn_out, scores_one, q))
    vk_pc = lax.ppermute(vk_p, "c", swap)
    q_p = lax.ppermute(q_late, "p", swap)
    attn_out, slope_p = forward((2,), (vk_p,), (attn_out,))
    attn_out, slope_pc, stats = forward((3,), (vk_pc,), (attn_out,), [((8, 1024), F32)])
    others = [
        lax.ppermute(stats, ("y", "w"), [(i, i ^ m) for i in range(8)]) for m in (1, 2, 3)
    ]
    q_p, others = lax.optimization_barrier((q_p, others))
    q_pc = lax.ppermute(q_p, "c", swap)
    grad_attn, normed_out = call(
        grad_attn_kernel,
        [rows_bf16, rows_bf16],
        (valid_lengths, attn_out, own, stats, *others),
        flops=10**7,
    )
    grad_p = lax.ppermute(grad_attn, "p", swap)
    own_late, grad_attn = lax.optimization_barrier((own, grad_attn))
    scores_two = key_scores((2, 3), own_late, (q_p, q_pc))
    (grad_q,) = call(
        grad_query_kernel,
        [rows_bf16],
        (valid_lengths, grad_attn, own, vk_c, vk_p, vk_pc, slope_o, slope_c, slope_p, slope_pc),
        scratch=[rows_f32],
        flops=4 * 10**9,
    )
    grad_late, grad_q = lax.optimization_barrier((grad_attn, grad_q))
    grad_c = lax.ppermute(grad_late, "c", swap)
    grad_p, grad_q, scores_two = lax.optimization_barrier((grad_p, grad_q, scores_two))
    grad_pc = lax.ppermute(grad_p, "c", swap)
    grad_k, grad_v = call(
        functools.partial(grad_key_kernel, False),
        [rows_f32, rows_f32],
        (valid_lengths, own, q, q_c, *scores_one, grad_attn, grad_c),
        flops=3 * 10**9,
    )
    (ret,) = call(
        functools.partial(grad_key_kernel, True),
        [((1024, 4 * HD), BF16)],
        (
            valid_lengths,
            own,
            q_p,
            q_pc,
            *scores_two,
            grad_p,
            grad_pc,
            grad_k,
            grad_v,
            normed_out,
            grad_q,
        ),
        scratch=[rows_f32, rows_f32],
        flops=3 * 10**9,
    )
    got = lax.all_to_all(ret, ("y", "w"), 0, 0, tiled=True)
    (rows,) = call(
        finish_kernel,
        [((CAP * 128, D + EXT), BF16)],
        (valid_lengths, got, slope, normed, inverse, grad_out, w_inner, hot, ext),
        scratch=[((2 * BLK, 4 * D), BF16)],
        flops=10**9,
    )
    got = lax.all_to_all(
        rows.reshape(128, CAP, D + EXT), ("y", "p", "w", "c", "row"), 0, 0, tiled=True
    ).reshape(128 * CAP, D + EXT)
    return pl.pallas_call(
        table_kernel,
        out_shape=jax.ShapeDtypeStruct((ROWS_DEV, D), F32),
        in_specs=[pl.BlockSpec(memory_space=pltpu.VMEM)],
        out_specs=pl.BlockSpec(memory_space=pltpu.HBM),
        scratch_shapes=[pltpu.VMEM((ROWS_DEV, D), F32), pltpu.SemaphoreType.DMA((8,))],
        compiler_params=pltpu.CompilerParams(vmem_limit_bytes=VMEM_LIMIT),
    )(got)


def solution(mesh):
    fine = Mesh(mesh.devices.reshape(4, 2, 2, 2, 4), ("y", "p", "w", "c", "row"))
    seq = ("y", "p", "w", "c")
    return jax.shard_map(
        local,
        mesh=fine,
        in_specs=(
            P("row", seq, None),
            P("row", seq, None),
            P(),
            P(),
            P("row"),
            P("row", seq),
        ),
        out_specs=P(seq + ("row",), None),
        check_vma=False,
    )
```

```python
import functools

import jax
import jax.numpy as jnp
from jax import lax
from jax.experimental import pallas as pl
from jax.experimental.pallas import tpu as pltpu
from jax.sharding import Mesh
from jax.sharding import PartitionSpec as P

HEADS = 4
ROWS_DEV = 1024
D = 512
HD = 128
BLK = 128
CAP = 4
EXT = 128
F32 = jnp.float32
BF16 = jnp.bfloat16
SCALE = HD**-0.5
VMEM_LIMIT = 12 * 2**20
PROJECT_LIMIT = 60 * 2**20


def dot(a, b):
    return lax.dot_general(a, b, (((1,), (0,)), ((), ())), preferred_element_type=F32)


def dot_t(a, b):
    return lax.dot_general(a, b, (((1,), (1,)), ((), ())), preferred_element_type=F32)


def normalize(values):
    center = values - jnp.mean(values, axis=-1, keepdims=True)
    inverse = lax.rsqrt(jnp.mean(center * center, axis=-1, keepdims=True) + 1e-05)
    return center * inverse, inverse


def silu(values):
    half = 0.5 * values
    return half * jnp.tanh(half) + half


def silu_slope(values):
    half = 0.5 * values
    two_sigma = 1.0 + jnp.tanh(half)
    return 0.5 * two_sigma * (1.0 + values - half * two_sigma)


def project_kernel(
    events_hbm, grad_hbm, w_hbm, w_outer_hbm, send, events, grad_out, weights, w_outer, parts, sems
):
    copies = [pltpu.make_async_copy(events_hbm, events, sems.at[4])]
    for part in (1, 3, 2, 0):
        cols = slice(part * D, (part + 1) * D)
        copies.append(pltpu.make_async_copy(w_hbm.at[:, cols], weights.at[part], sems.at[part]))
    copies.append(pltpu.make_async_copy(w_outer_hbm, w_outer, sems.at[5]))
    copies.append(pltpu.make_async_copy(grad_hbm, grad_out, sems.at[6]))
    for copy in copies:
        copy.start()
    leaving = []
    copies[0].wait()
    normed = normalize(events[...].astype(F32))[0].astype(BF16)
    for slot, part in enumerate((1, 3, 2, 0)):
        copies[slot + 1].wait()
        act = silu(dot(normed, weights[part])).astype(BF16)
        if part == 0:
            copies[5].wait()
            copies[6].wait()
            act = (dot_t(grad_out[...], w_outer[...]) * act.astype(F32)).astype(BF16)
        for g in range(2):
            for h in range(HEADS):
                piece = act[g * BLK : (g + 1) * BLK, h * HD : (h + 1) * HD]
                at = (g * HEADS + h) * BLK
                parts[slot, at : at + BLK, :] = piece
        cols = slice(slot * HD, (slot + 1) * HD)
        leaving.append(pltpu.make_async_copy(parts.at[slot], send.at[:, cols], sems.at[7 + slot]))
        leaving[-1].start()
    for copy in leaving:
        copy.wait()


def gate_kernel(events, grad_out, w_inner, w_outer, ids, slope, normed_out, inv_out, hot, ext):
    normed, inverse = normalize(events[...].astype(F32))
    normed_out[...] = normed
    inv_out[...] = jnp.broadcast_to(inverse, inv_out.shape)
    normed = normed.astype(BF16)
    for part in range(4):
        cols = slice(part * D, (part + 1) * D)
        values = silu_slope(dot(normed, w_inner[:, cols]))
        if part == 0:
            values = values * dot_t(grad_out[...], w_outer[...])
        slope[:, cols] = values
    count = 2 * BLK
    id_row = ids[...]
    id_cols = jnp.transpose(jnp.broadcast_to(id_row.astype(F32), (BLK, count))).astype(jnp.int32)
    owner_row = id_row // ROWS_DEV
    owner_col = id_cols[:, :1] // ROWS_DEV
    earlier = lax.broadcasted_iota(jnp.int32, (count, count), 0) < lax.broadcasted_iota(
        jnp.int32, (count, count), 1
    )
    same = jnp.where((owner_col == owner_row) & earlier, 1, 0)
    rank = jnp.sum(same, axis=0, keepdims=True)
    dest = (owner_row // 4 % 2) * 64 + owner_row // 8 * 4 + owner_row % 4
    slot = dest * CAP + rank
    slots = hot.shape[0]
    hot[...] = jnp.where(
        lax.broadcasted_iota(jnp.int32, (slots, count), 0) == slot, 1.0, 0.0
    ).astype(BF16)
    within = id_cols - (id_cols // ROWS_DEV) * ROWS_DEV
    high = within // 32
    lane = lax.broadcasted_iota(jnp.int32, (count, EXT), 1)
    ext[...] = (
        jnp.where(lane == 0, high + 1, jnp.where(lane == 1, within - high * 32, 0))
        .astype(F32)
        .astype(BF16)
    )


V_COLS, K_COLS, Q_COLS, G_COLS = (slice(i * HD, (i + 1) * HD) for i in range(4))
GRP = 2 * BLK


def my_place():
    return lax.axis_index("p"), lax.axis_index("c")


def my_length(lengths):
    return lengths[lax.axis_index("y") // 2]


def inverse_of(length):
    return 1.0 / jnp.full((1, HD), length, jnp.int32).astype(F32)


def diagonal(row_place, col_place, rows_are_keys):
    def start(place):
        return (4 * place[0] + place[1]) * BLK

    row = lax.broadcasted_iota(jnp.int32, (GRP, GRP), 0)
    col = lax.broadcasted_iota(jnp.int32, (GRP, GRP), 1)
    row = jnp.where(row >= BLK, row + BLK, row) + start(row_place)
    col = jnp.where(col >= BLK, col + BLK, col) + start(col_place)
    return row <= col if rows_are_keys else col <= row


def mask_first(mask, values):
    first = jnp.where(mask, values[:GRP, :], 0.0)
    return jnp.concatenate([first, values[GRP:, :]], axis=0) if values.shape[0] > GRP else first


def mask_last(mask, values):
    last = jnp.where(mask, values[-GRP:, :], 0.0)
    return jnp.concatenate([values[:-GRP, :], last], axis=0) if values.shape[0] > GRP else last


def part_place(part):
    p, c = my_place()
    return (1 - p if part & 2 else p), (1 - c if part & 1 else c)


def query_rows(y):
    start = y * (9 - y) // 2 * GRP
    return slice(start, start + (4 - y) * GRP)


def forward_kernel(part_ids, lengths, own, *refs):
    count = len(part_ids)
    first, last = part_ids[0] == 0, part_ids[-1] == 3
    keys_of, refs = refs[:count], refs[count:]
    if not first:
        before, *refs = refs
    out, *refs = refs
    slopes_out, refs = refs[:count], refs[count:]
    out[...] = jnp.zeros_like(out) if first else before[...]
    for y in range(4):
        rows = slice(y * GRP, 1024)
        queries = own[rows, Q_COLS]
        keys = slice(y * GRP, (y + 1) * GRP)
        for part, src, slope_out in zip(part_ids, keys_of, slopes_out):
            slope, attn = slopes(dot_t(queries, src[keys, K_COLS]))
            mask = diagonal(my_place(), part_place(part), False)
            slope_out[query_rows(y), :] = mask_first(mask, slope)
            attn = mask_first(mask, attn)
            out[rows, :] += dot(attn.astype(BF16), src[keys, V_COLS])
    if not last:
        return
    (stats,) = refs
    inv_len = inverse_of(my_length(lengths))
    for m in range(8):
        rows = slice(m * BLK, (m + 1) * BLK)
        total = out[rows, :] * inv_len
        out[rows, :] = total
        g = own[rows, G_COLS].astype(F32)
        mean = jnp.mean(total, axis=-1, keepdims=True)
        center = total - mean
        square = jnp.sum(center * center, axis=-1, keepdims=True)
        sum_g = jnp.sum(g, axis=-1, keepdims=True)
        sum_ga = jnp.sum(g * center, axis=-1, keepdims=True)
        lane = lax.broadcasted_iota(jnp.int32, (BLK, BLK), 1)
        packed = jnp.where(
            lane == 0, mean, jnp.where(lane == 1, square, jnp.where(lane == 2, sum_g, sum_ga))
        )
        stats[:, rows] = jnp.transpose(packed)[:8, :]


def grad_attn_kernel(lengths, attn_out, own, s0, s1, s2, s3, grad_attn, normed_out):
    p, c = my_place()
    length = my_length(lengths)
    parts = [s0[...], s1[...], s2[...], s3[...]]
    means = [part[0:1, :] for part in parts]
    mean = 0.25 * (means[0] + means[1] + means[2] + means[3])
    square = 0.0
    sum_g = 0.0
    sum_ga = 0.0
    for part, local_mean in zip(parts, means):
        shift = local_mean - mean
        square = square + part[1:2, :] + HD * (shift * shift)
        sum_g = sum_g + part[2:3, :]
        sum_ga = sum_ga + part[3:4, :] + part[2:3, :] * shift
    inverse = lax.rsqrt(square * (1.0 / D) + 1e-05)
    mean_g = sum_g * (1.0 / D)
    mean_gn = inverse * sum_ga * (1.0 / D)
    row = lax.broadcasted_iota(jnp.int32, (BLK, 1024), 0)
    packed = jnp.where(
        row == 0, mean, jnp.where(row == 1, inverse, jnp.where(row == 2, mean_g, mean_gn))
    )
    for m in range(8):
        rows = slice(m * BLK, (m + 1) * BLK)
        cols = jnp.transpose(packed[:, rows])
        inv = cols[:, 1:2]
        n = (attn_out[rows, :] - cols[:, 0:1]) * inv
        back = (own[rows, G_COLS].astype(F32) - cols[:, 2:3] - n * cols[:, 3:4]) * inv
        pos = lax.broadcasted_iota(jnp.int32, (BLK, 1), 0)
        pos = pos + (m // 2 * 8 + 4 * p + m % 2 * 2 + c) * BLK
        grad_attn[rows, :] = jnp.where(pos < length, back, 0.0).astype(BF16)
        normed_out[rows, :] = n.astype(BF16)


def slopes(raw):
    half = raw * (0.5 * SCALE)
    t = jnp.tanh(half)
    two_sigma = 1.0 + t
    return two_sigma + half * (1.0 - t * t), half * two_sigma


def grad_query_kernel(lengths, grad_attn, *refs):
    keys_of, slopes_of, (ret, total) = refs[:4], refs[4:8], refs[8:]
    total[...] = jnp.zeros_like(total)
    for y in range(4):
        rows = slice(y * GRP, 1024)
        keys = slice(y * GRP, (y + 1) * GRP)
        for src, slope in zip(keys_of, slopes_of):
            score = slope[query_rows(y), :] * dot_t(grad_attn[rows, :], src[keys, V_COLS])
            total[rows, :] += dot(score.astype(BF16), src[keys, K_COLS])
    inv_len = inverse_of(my_length(lengths))
    ret[...] = (total[...] * (0.5 * SCALE * inv_len)).astype(BF16)


PACKED = 10 * GRP


def packed_rows(y):
    start = y * (y + 1) // 2 * GRP
    return slice(start, start + (y + 1) * GRP)


def key_scores_kernel(part_ids, own, *refs):
    queries_of, outs = refs[:2], (refs[2:4], refs[4:6])
    for y in range(4):
        keys = own[: (y + 1) * GRP, K_COLS]
        events = slice(y * GRP, (y + 1) * GRP)
        for part, src, (slope_out, attn_out) in zip(part_ids, queries_of, outs):
            slope, attn = slopes(dot_t(keys, src[events, :]))
            mask = diagonal(my_place(), part_place(part), True)
            slope_out[packed_rows(y), :] = mask_last(mask, slope)
            attn_out[packed_rows(y), :] = mask_last(mask, attn).astype(BF16)


def grad_key_kernel(last, lengths, own, *refs):
    queries_of, scores, grads_of, refs = refs[:2], (refs[2:4], refs[4:6]), refs[6:8], refs[8:]
    if last:
        k_before, v_before, normed_out, grad_q, ret, grad_k, grad_v = refs
        grad_k[...] = k_before[...]
        grad_v[...] = v_before[...]
    else:
        grad_k, grad_v = refs
        grad_k[...] = jnp.zeros_like(grad_k)
        grad_v[...] = jnp.zeros_like(grad_v)
    for y in range(4):
        rows = slice(0, (y + 1) * GRP)
        events = slice(y * GRP, (y + 1) * GRP)
        values = own[rows, V_COLS]
        for q, (slope, attn), grad_attn in zip(queries_of, scores, grads_of):
            ga = grad_attn[events, :]
            score = slope[packed_rows(y), :] * dot_t(values, ga)
            grad_k[rows, :] += dot(score.astype(BF16), q[events, :])
            grad_v[rows, :] += dot(attn[packed_rows(y), :], ga)
    if last:
        inv_len = inverse_of(my_length(lengths))
        ret[:, :HD] = normed_out[...]
        ret[:, HD : 2 * HD] = (grad_v[...] * inv_len).astype(BF16)
        ret[:, 2 * HD : 3 * HD] = grad_q[...]
        ret[:, 3 * HD :] = (grad_k[...] * (0.5 * SCALE * inv_len)).astype(BF16)


def finish_kernel(
    lengths, ret, slope, normed, inverse, grad_out, w_inner, hot, ext, send, grads
):
    for g in range(2):
        rows = slice(g * BLK, (g + 1) * BLK)
        for h in range(HEADS):
            at = slice((g * HEADS + h) * BLK, (g * HEADS + h + 1) * BLK)
            for part in range(4):
                cols = slice(part * D + h * HD, part * D + (h + 1) * HD)
                grad = ret[at, part * HD : (part + 1) * HD].astype(F32)
                grads[rows, cols] = (grad * slope[rows, cols]).astype(BF16)
    grad_normed = dot_t(grads[...], w_inner[...])
    back = inverse[:, :1] * (
        grad_normed
        - jnp.mean(grad_normed, axis=-1, keepdims=True)
        - normed[...] * jnp.mean(grad_normed * normed[...], axis=-1, keepdims=True)
    )
    total = grad_out[...].astype(F32) + back
    chip = (lax.axis_index("y") * 2 + lax.axis_index("p")) * 2 + lax.axis_index("w")
    first = (chip * 2 + lax.axis_index("c")) * BLK
    row = lax.broadcasted_iota(jnp.int32, (2 * BLK, 1), 0)
    second = row >= BLK
    pos = first + jnp.where(second, row - BLK, row)
    total = jnp.where(pos < jnp.where(second, lengths[1], lengths[0]), total, 0.0)
    send[:, :D] = dot(hot[...], total.astype(BF16)).astype(BF16)
    send[:, D:] = dot(hot[...], ext[...]).astype(BF16)


def table_kernel(got, table, stage, sems):
    packed = jnp.transpose(got[:, D:].astype(F32))
    dest = ((packed[0:1, :] - 1.0) * 32.0 + packed[1:2, :]).astype(jnp.int32)
    leaving = []
    for i in range(ROWS_DEV // BLK):
        rows = slice(i * BLK, (i + 1) * BLK)
        row = lax.broadcasted_iota(jnp.int32, (BLK, got.shape[0]), 0) + i * BLK
        hot = jnp.where(row == dest, 1.0, 0.0).astype(BF16)
        stage[rows, :] = dot(hot, got[:, :D])
        leaving.append(pltpu.make_async_copy(stage.at[rows], table.at[rows], sems.at[i]))
        leaving[-1].start()
    for copy in leaving:
        copy.wait()


def call(kernel, outs, args, scalars=1, scratch=(), flops=0):
    vmem = pl.BlockSpec(memory_space=pltpu.VMEM)
    smem = pl.BlockSpec(memory_space=pltpu.SMEM)
    return pl.pallas_call(
        kernel,
        out_shape=[jax.ShapeDtypeStruct(shape, dtype) for shape, dtype in outs],
        in_specs=[smem] * scalars + [vmem] * (len(args) - scalars),
        out_specs=[vmem] * len(outs),
        scratch_shapes=[pltpu.VMEM(shape, dtype) for shape, dtype in scratch],
        compiler_params=pltpu.CompilerParams(vmem_limit_bytes=VMEM_LIMIT),
        cost_estimate=pl.CostEstimate(flops=flops, bytes_accessed=2**20, transcendentals=0),
    )(*args)


def project(*args):
    hbm = pl.BlockSpec(memory_space=pltpu.HBM)
    return pl.pallas_call(
        project_kernel,
        out_shape=jax.ShapeDtypeStruct((8 * BLK, 4 * HD), BF16),
        in_specs=[hbm] * len(args),
        out_specs=hbm,
        scratch_shapes=[
            pltpu.VMEM((2 * BLK, D), BF16),
            pltpu.VMEM((2 * BLK, D), BF16),
            pltpu.VMEM((4, D, D), BF16),
            pltpu.VMEM((D, D), BF16),
            pltpu.VMEM((4, 8 * BLK, HD), BF16),
            pltpu.SemaphoreType.DMA((11,)),
        ],
        compiler_params=pltpu.CompilerParams(vmem_limit_bytes=PROJECT_LIMIT),
    )(*args)


def local(events, grad_out, w_inner, w_outer, valid_lengths, item_ids):
    events = events.reshape(2 * BLK, D)
    grad_out = grad_out.reshape(2 * BLK, D)
    rows_bf16, rows_f32 = ((1024, HD), BF16), ((1024, HD), F32)
    swap = [(0, 1), (1, 0)]
    send = project(events, grad_out, w_inner, w_outer)
    own = lax.all_to_all(send, ("y", "w"), 0, 0, tiled=True)
    slope, normed, inverse, hot, ext = call(
        gate_kernel,
        [
            ((2 * BLK, 4 * D), F32),
            ((2 * BLK, D), F32),
            ((2 * BLK, HD), F32),
            ((CAP * 128, 2 * BLK), BF16),
            ((2 * BLK, EXT), BF16),
        ],
        (events, grad_out, w_inner, w_outer, item_ids.reshape(1, 2 * BLK)),
        scalars=0,
        flops=2 * 10**9,
    )
    own, slope = lax.optimization_barrier((own, slope))
    slope_shape, score_shapes = ((PACKED, GRP), F32), [((PACKED, GRP), F32), ((PACKED, GRP), BF16)]
    vk, q = own[:, : 2 * HD], own[:, Q_COLS]
    vk_p = lax.ppermute(vk, "p", swap)
    vk_c = lax.ppermute(vk, "c", swap)
    q_c = lax.ppermute(q, "c", swap)

    def forward(part_ids, keys, before, extra=()):
        return call(
            functools.partial(forward_kernel, part_ids),
            [rows_f32] + [slope_shape] * len(keys) + list(extra),
            (valid_lengths, own, *keys, *before),
            flops=10**9 * len(keys) // 2,
        )

    def key_scores(part_ids, src, queries):
        return call(
            functools.partial(key_scores_kernel, part_ids),
            score_shapes * 2,
            (src, *queries),
            scalars=0,
            flops=10**9,
        )

    attn_out, slope_o, slope_c = forward((0, 1), (own, vk_c), ())
    scores_one = key_scores((0, 1), own, (q, q_c))
    vk_p, attn_out, scores_one = lax.optimization_barrier((vk_p, attn_out, scores_one))
    vk_pc = lax.ppermute(vk_p, "c", swap)
    attn_out, slope_p = forward((2,), (vk_p,), (attn_out,))
    attn_out, q_late = lax.optimization_barrier((attn_out, q))
    q_p = lax.ppermute(q_late, "p", swap)
    attn_out, slope_pc, stats = forward((3,), (vk_pc,), (attn_out,), [((8, 1024), F32)])
    others = [
        lax.ppermute(stats, ("y", "w"), [(i, i ^ m) for i in range(8)]) for m in (1, 2, 3)
    ]
    q_p, others = lax.optimization_barrier((q_p, others))
    q_pc = lax.ppermute(q_p, "c", swap)
    grad_attn, normed_out = call(
        grad_attn_kernel,
        [rows_bf16, rows_bf16],
        (valid_lengths, attn_out, own, stats, *others),
        flops=10**7,
    )
    grad_p = lax.ppermute(grad_attn, "p", swap)
    own_late, grad_attn = lax.optimization_barrier((own, grad_attn))
    scores_two = key_scores((2, 3), own_late, (q_p, q_pc))
    (grad_q,) = call(
        grad_query_kernel,
        [rows_bf16],
        (valid_lengths, grad_attn, own, vk_c, vk_p, vk_pc, slope_o, slope_c, slope_p, slope_pc),
        scratch=[rows_f32],
        flops=4 * 10**9,
    )
    grad_late, grad_q = lax.optimization_barrier((grad_attn, grad_q))
    grad_c = lax.ppermute(grad_late, "c", swap)
    grad_p, grad_q, scores_two = lax.optimization_barrier((grad_p, grad_q, scores_two))
    grad_pc = lax.ppermute(grad_p, "c", swap)
    grad_k, grad_v = call(
        functools.partial(grad_key_kernel, False),
        [rows_f32, rows_f32],
        (valid_lengths, own, q, q_c, *scores_one, grad_attn, grad_c),
        flops=3 * 10**9,
    )
    (ret,) = call(
        functools.partial(grad_key_kernel, True),
        [((1024, 4 * HD), BF16)],
        (
            valid_lengths,
            own,
            q_p,
            q_pc,
            *scores_two,
            grad_p,
            grad_pc,
            grad_k,
            grad_v,
            normed_out,
            grad_q,
        ),
        scratch=[rows_f32, rows_f32],
        flops=3 * 10**9,
    )
    got = lax.all_to_all(ret, ("y", "w"), 0, 0, tiled=True)
    (rows,) = call(
        finish_kernel,
        [((CAP * 128, D + EXT), BF16)],
        (valid_lengths, got, slope, normed, inverse, grad_out, w_inner, hot, ext),
        scratch=[((2 * BLK, 4 * D), BF16)],
        flops=10**9,
    )
    got = lax.all_to_all(
        rows.reshape(128, CAP, D + EXT), ("c", "y", "p", "w", "row"), 0, 0, tiled=True
    ).reshape(128 * CAP, D + EXT)
    return pl.pallas_call(
        table_kernel,
        out_shape=jax.ShapeDtypeStruct((ROWS_DEV, D), F32),
        in_specs=[pl.BlockSpec(memory_space=pltpu.VMEM)],
        out_specs=pl.BlockSpec(memory_space=pltpu.HBM),
        scratch_shapes=[pltpu.VMEM((ROWS_DEV, D), F32), pltpu.SemaphoreType.DMA((8,))],
        compiler_params=pltpu.CompilerParams(vmem_limit_bytes=VMEM_LIMIT),
    )(got)


def solution(mesh):
    fine = Mesh(mesh.devices.reshape(4, 2, 2, 2, 4), ("y", "p", "w", "c", "row"))
    seq = ("y", "p", "w", "c")
    return jax.shard_map(
        local,
        mesh=fine,
        in_specs=(
            P("row", seq, None),
            P("row", seq, None),
            P(),
            P(),
            P("row"),
            P("row", seq),
        ),
        out_specs=P(seq + ("row",), None),
        check_vma=False,
    )
```
